512 devices in a mesh: seq: 64 (over z, x, core), head: 8 (over y).
Axes of the slice: x: 4, y: 8, z: 8, core: 2. Of those that a mesh axis runs over, the one named last changes fastest.
Arguments:
- input_x: bfloat16 [16384, 4096], P('seq', 'head'), may hold values from -6 to 6
- input_z: bfloat16 [16384, 4096], P('seq', 'head'), may hold values from -6 to 6
- input_b: bfloat16 [16384, 128], P('seq'), may hold values from -6 to 6
- input_c: bfloat16 [16384, 128], P('seq'), may hold values from -6 to 6
- step_raw: float32 [16384, 64], P('seq', 'head'), may hold values from -8 to 2
- doc_starts: int32 [16384], P('seq'), may hold values from 0 to 1, as said below
- log_rate: float32 [64], P('head'), may hold values from -9.5 to 2.5
- step_bias: float32 [64], P('head'), may hold values from -0.5 to 0.5
- skip_gain: float32 [64], P('head'), may hold values from 0.5 to 1.5
- norm_gain: float32 [4096], P('head'), may hold values from 0.1 to 1.9
- out_weight: bfloat16 [4096, 4096], P('head'), may hold values from -0.125 to 0.125
Outputs:
- mixed: bfloat16 [16384, 4096], P('seq', 'head')
The draws below stay inside these ranges and needn't reach their ends.
Inputs may be any that keep to these rules, and one draw needn't show every extreme that they name: `doc_starts`: the first token of the context always carries a document start. Some document start lies within the first 4096 tokens such that the 12288 tokens after it carry no document start.
All inputs are finite; a program needn't handle non-finite values.
Results may differ from the reference program's by a relative error of at most 0.019.
Values may be sent and summed in bfloat16 or wider, within the bound.
No kernel may reach another device: no remote copies, remote signals or barrier semaphores. Data moves between devices by JAX's collectives and lax.ppermute only.
A program may use at most 128 MiB of HBM per device.

```python
import math
import jax
import jax.numpy as jnp
from jax import lax

D = 4096
HEAD_SIZE = 64
STATE = 128
SPAN = 256
SLICE_LENGTH = 256
WINDOW_LENGTH = 16384
HEADS = 64
INNER = 4096
N_HEAD = 8


def draw_doc_starts(key, part):
    key = jax.random.fold_in(key, 11)
    key_one, key_two = jax.random.split(key)
    draws_int = jax.random.randint(key_one, (WINDOW_LENGTH,), 0, 4 * SLICE_LENGTH)
    quiet_from = jax.random.randint(key_two, (), 0, WINDOW_LENGTH // 4)
    positions = jnp.arange(WINDOW_LENGTH)
    quiet = (positions > quiet_from) & (positions <= quiet_from + 3 * WINDOW_LENGTH // 4)
    starts = jnp.where(quiet, 0, (draws_int == 0).astype(jnp.int32)).astype(jnp.int32)
    starts = jnp.where(positions == quiet_from, 1, starts).astype(jnp.int32)
    return starts.at[0].set(1)


def draw_step_raw(key, part):
    key = jax.random.fold_in(key, 12)
    key_one, key_two, tertiary_seed, key_four = jax.random.split(key, 4)
    blocks = WINDOW_LENGTH // SPAN
    opening_indices = jax.random.uniform(key_one, (blocks, 1, HEADS), jnp.float32, -0.7, 0.7)
    opening_indices = jnp.broadcast_to(opening_indices, (blocks, SPAN, HEADS)).reshape(WINDOW_LENGTH, HEADS)
    noise_perturbation = jnp.clip(0.4 * jax.random.normal(key_two, (WINDOW_LENGTH, HEADS), jnp.float32), -1.0, 1.0)
    floor_amplitude = -6.0
    sudden_peaks = jax.random.randint(tertiary_seed, (WINDOW_LENGTH, 1), 0, 4 * SLICE_LENGTH) == 0
    amplitude_series = jax.random.uniform(key_four, (WINDOW_LENGTH, HEADS), jnp.float32, 0.5, 2.0)
    return jnp.where(sudden_peaks, amplitude_series, floor_amplitude + opening_indices + noise_perturbation)


def rate_mixture(key, share_slow, slow_low, slow_high, fast_low, fast_high):
    key_one, key_two, tertiary_seed = jax.random.split(key, 3)
    slow_ones = jax.random.uniform(key_one, (HEADS,), jnp.float32, math.log(slow_low), math.log(slow_high))
    fast_ones = jax.random.uniform(key_two, (HEADS,), jnp.float32, math.log(fast_low), math.log(fast_high))
    picks = jax.random.uniform(tertiary_seed, (HEADS,), jnp.float32) < share_slow
    return jnp.where(picks, slow_ones, fast_ones)


def draw_log_rate(key, part):
    key = jax.random.fold_in(key, 13)
    chain = WINDOW_LENGTH * 0.003
    return rate_mixture(key, 0.5, 0.2 / chain, 1.5 / chain, 1.5 / chain, 12.0)


def strengthened(drawn, stream_key, source, target, parts, factor):
    owner, partner = [(jnp.arange(drawn.shape[position]) // (drawn.shape[position] // parts)).reshape([-1 if axis == position else 1 for axis in range(drawn.ndim)]) for position in (source, target)]
    chosen = jax.random.permutation(stream_key, parts)[partner]
    strong = (owner == chosen) | (owner == (partner + parts // 2) % parts)
    return jnp.where(strong, factor * drawn, drawn)


def block_scale(key, shape, cuts, smallest, high):
    def one(dim, parts):
        draws = jax.random.uniform(jax.random.fold_in(jax.random.fold_in(key, 6), dim), (parts,), jnp.float32, smallest / len(cuts), high / len(cuts))
        return jnp.repeat(jnp.exp(draws), shape[dim] // parts).reshape((-1,) + (1,) * (len(shape) - dim - 1))

    factor_of = one(*cuts[0])
    for cut in cuts[1:]:
        factor_of = factor_of * one(*cut)
    return factor_of


def bell_draw(key, shape, deviation, most, cuts=(), dtype=jnp.bfloat16):
    values = jax.random.normal(key, shape, jnp.float32) * deviation
    if len(cuts) > 0:
        values = block_scale(key, shape, cuts, -0.22, 0.18) * values
    return jnp.clip(values, min=-most, max=most).astype(dtype)


def bell_draw_with(own_key, dims, deviation, bound, shards, heavy, dtype=jnp.bfloat16):
    values = deviation * jax.random.normal(own_key, dims, jnp.float32)
    if shards:
        values = values * block_scale(own_key, dims, shards, -0.22, 0.18)
    return jnp.clip(strengthened(values, jax.random.fold_in(own_key, 3), *heavy), -bound, bound).astype(dtype)


def setup_inputs(seed: int = 0) -> dict:
    key_of = jax.random.split(jax.random.key(seed), 12)
    return {
        "input_x": bell_draw(key_of[0], (WINDOW_LENGTH, INNER), 1.0, 6.0, ((0, 64), (1, 8))),
        "input_z": bell_draw(key_of[1], (WINDOW_LENGTH, INNER), 1.0, 6.0, ((0, 64), (1, 8))),
        "input_b": bell_draw(key_of[2], (WINDOW_LENGTH, STATE), 1.0, 6.0, ((0, 64),)),
        "input_c": bell_draw(key_of[3], (WINDOW_LENGTH, STATE), 1.0, 6.0, ((0, 64),)),
        "step_raw": draw_step_raw(jax.random.fold_in(key_of[11], 71), 0),
        "doc_starts": draw_doc_starts(jax.random.fold_in(key_of[11], 71), 0),
        "log_rate": draw_log_rate(jax.random.fold_in(key_of[11], 71), 0),
        "step_bias": jnp.clip(jax.random.uniform(key_of[7], (HEADS,), jnp.float32, -0.5, 0.5) * block_scale(key_of[7], (HEADS,), ((0, 8),), -0.4, 0.0), -0.5, 0.5),
        "skip_gain": jnp.clip(0.5 + 1.0 * jax.random.uniform(key_of[8], (HEADS,), jnp.float32) ** block_scale(key_of[8], (HEADS,), ((0, 8),), -0.2, 0.2), 0.5, 1.5),
        "norm_gain": jnp.clip(1.0 + 0.18 * jax.random.normal(key_of[9], (INNER,), jnp.float32), 0.1, 1.9),
        "out_weight": bell_draw_with(key_of[10], (INNER, D), INNER ** -0.5, 0.125, ((0, 8),), (0, 1, 8, 2.0)),
    }


def span_parts(pieces, rate_values):
    x_block, b_block, c_block, dt_block, flag_block = pieces
    log_steps = dt_block * rate_values[None, :]
    running = jnp.cumsum(log_steps, axis=0)
    resets = jnp.cumsum(flag_block, axis=0)
    positions = jnp.arange(flag_block.shape[0])
    allowed = (positions[:, None] >= positions[None, :]) & (resets[:, None] == resets[None, :])
    running_t = running.T
    spread = running_t[:, :, None] - running_t[:, None, :]
    decays = jnp.where(allowed[None], jnp.exp(jnp.where(allowed[None], spread, 0.0)), 0.0)
    scores = jnp.dot(c_block, b_block.T, preferred_element_type=jnp.float32)
    mixing = (scores[None] * decays * dt_block.T[:, None, :]).astype(jnp.bfloat16)
    intra_out = jnp.einsum('hts,shp->thp', mixing.astype(jnp.float32), x_block.astype(jnp.float32))
    living = resets == resets[-1]
    weights = jnp.where(living[:, None], jnp.exp(running[-1][None, :] - running), 0.0) * dt_block
    scaled = (weights[:, :, None] * x_block.astype(jnp.float32)).astype(jnp.bfloat16)
    states = jnp.einsum('shp,sn->hpn', scaled.astype(jnp.float32), b_block.astype(jnp.float32))
    through = jnp.where(resets[-1] == 0, jnp.exp(running[-1]), 0.0)
    opening = jnp.where((resets == 0)[:, None], jnp.exp(running), 0.0)
    return (intra_out, states, through, opening)

def reference(input_x, input_z, input_b, input_c, step_raw, doc_starts, log_rate, step_bias, skip_gain, norm_gain, out_weight):
    blocks = WINDOW_LENGTH // SPAN
    step_dt = jax.nn.softplus(step_raw + step_bias[None, :])
    rate_values = -jnp.exp(log_rate)
    x_blocks = input_x.reshape(blocks, SPAN, HEADS, HEAD_SIZE)
    b_blocks = input_b.reshape(blocks, SPAN, STATE)
    c_blocks = input_c.reshape(blocks, SPAN, STATE)
    dt_blocks = step_dt.reshape(blocks, SPAN, HEADS)
    flag_blocks = doc_starts.reshape(blocks, SPAN)
    intra_out, states, through, opening = lax.map(lambda pieces: span_parts(pieces, rate_values), (x_blocks, b_blocks, c_blocks, dt_blocks, flag_blocks))

    def advance(carried, element):
        through_one, state_one = element
        return (through_one[:, None, None] * carried + state_one, carried)
    finals, entries = lax.scan(advance, jnp.zeros((HEADS, HEAD_SIZE, STATE), jnp.float32), (through, states))
    entry_bf = entries.astype(jnp.bfloat16)
    carried_out = jnp.einsum('ctn,chpn->cthp', c_blocks.astype(jnp.float32), entry_bf.astype(jnp.float32)) * opening[:, :, :, None]
    ys = intra_out + carried_out + skip_gain[None, None, :, None] * x_blocks.astype(jnp.float32)
    ys = ys.reshape(WINDOW_LENGTH, INNER)
    gated_out = ys * jax.nn.silu(input_z.astype(jnp.float32))
    mean_square = lax.optimization_barrier(jnp.mean(gated_out * gated_out, axis=1, keepdims=True))
    normed = (gated_out * lax.rsqrt(mean_square + 1e-05) * norm_gain[None, :]).astype(jnp.bfloat16)
    group_width = INNER // N_HEAD

    def add_group(group, total):
        offset = (group * group_width).astype(jnp.int32)
        channels = lax.dynamic_slice_in_dim(normed, offset, group_width, 1)
        weight_rows = lax.dynamic_slice_in_dim(out_weight, offset, group_width, 0)
        partial_out = lax.optimization_barrier(jnp.dot(channels, weight_rows, preferred_element_type=jnp.float32).astype(jnp.bfloat16))
        return total + partial_out.astype(jnp.float32)
    summed = lax.fori_loop(jnp.int32(0), jnp.int32(N_HEAD), add_group, jnp.zeros((WINDOW_LENGTH, D), jnp.float32))
    return summed.astype(jnp.bfloat16)
```

```python
import jax
import jax.numpy as jnp
from jax import lax
from jax.experimental import pallas as pl
from jax.experimental.pallas import tpu as pltpu
from jax.sharding import PartitionSpec as P

SPAN = 256
N_ROW = 8
PAD = 16
F32, BF16 = (jnp.float32, jnp.bfloat16)
VMEM = pl.BlockSpec(memory_space=pltpu.VMEM)
SMEM = pl.BlockSpec(memory_space=pltpu.SMEM)


def column_of(ref, shape):
    rows = lax.broadcasted_iota(jnp.int32, shape, 0)
    out = jnp.zeros(shape, F32)
    for h in range(shape[0]):
        out = jnp.where(rows == h, ref[h], out)
    return out


def running_sum(rows):
    lanes = lax.broadcasted_iota(jnp.int32, rows.shape, 1)
    step = 1
    while step < rows.shape[1]:
        rows = rows + jnp.where(lanes >= step, pltpu.roll(rows, step, 1), 0.0)
        step *= 2
    return rows


def keep_rows(keep):
    high = keep.astype(BF16).astype(F32)
    middle = (keep - high).astype(BF16).astype(F32)
    low = keep - high - middle
    rows = lax.broadcasted_iota(jnp.int32, (PAD, keep.shape[1]), 0)
    out = jnp.where(rows == 0, high, jnp.where(rows == 1, middle, jnp.where(rows == 2, low, 0.0)))
    return out.astype(BF16)


def piece(ref, index, state_rows):
    state = ref[index, :state_rows, :].astype(F32)
    keep = jnp.sum(ref[index, state_rows:, :].astype(F32), axis=0, keepdims=True)
    return state, keep


def state_kernel(log_rate, bias, raw_ref, flag_ref, x_ref, b_ref, out_ref, rows_ref, cols_ref):
    heads, tokens = raw_ref.shape
    width = x_ref.shape[1] // heads
    raw = raw_ref[...]
    dt = jax.nn.softplus(raw + column_of(bias, raw.shape))
    rate = -jnp.exp(column_of(log_rate, raw.shape))
    flags = jnp.broadcast_to(flag_ref[...].astype(F32), raw.shape)
    sums = running_sum(jnp.concatenate([rate * dt, flags], axis=0))
    running, resets = (sums[:heads], sums[heads:])
    run_last = jnp.broadcast_to(running[:, tokens - 1 :], raw.shape)
    reset_last = jnp.broadcast_to(resets[:, tokens - 1 :], raw.shape)
    weights = jnp.where(resets == reset_last, jnp.exp(run_last - running), 0.0) * dt
    opening = jnp.where(resets == 0.0, jnp.exp(running), 0.0)
    rows = jnp.concatenate([running, dt, resets, opening, weights], axis=0)
    rows_ref[...] = rows
    cols = jnp.concatenate([rows, jnp.zeros((128 - rows.shape[0], tokens), F32)], axis=0).T
    cols_ref[...] = cols
    through = jnp.where(reset_last == 0.0, jnp.exp(run_last), 0.0)
    spread = jnp.concatenate(
        [
            jnp.broadcast_to(cols[:, 4 * heads + h : 4 * heads + h + 1], (tokens, width))
            for h in range(heads)
        ],
        axis=1,
    )
    scaled = (spread * x_ref[...].astype(F32)).astype(BF16)
    states = lax.dot_general(scaled, b_ref[...], (((0,), (0,)), ((), ())), preferred_element_type=F32)
    for h in range(heads):
        out_ref[h, :width, :] = states[h * width : (h + 1) * width].astype(BF16)
        out_ref[h, width:, :] = keep_rows(through[h : h + 1, :128])


def intra_kernel(skip, rows_ref, cols_ref, x_ref, z_ref, b_ref, c_ref, own_ref, open_ref):
    tokens = x_ref.shape[0]
    heads = skip.shape[0]
    width = x_ref.shape[1] // heads
    scores = lax.dot_general(c_ref[...], b_ref[...], (((1,), (1,)), ((), ())), preferred_element_type=F32)
    reset_row = rows_ref[2 * heads : 2 * heads + 1, :]
    reset_col = cols_ref[:, 2 * heads : 2 * heads + 1]
    later = lax.broadcasted_iota(jnp.int32, scores.shape, 0)
    earlier = lax.broadcasted_iota(jnp.int32, scores.shape, 1)
    allowed = (later >= earlier) & (reset_col == reset_row)
    scores = jnp.where(allowed, scores, 0.0)
    for h in range(heads):
        span = slice(h * width, (h + 1) * width)
        spread = cols_ref[:, h : h + 1] - rows_ref[h : h + 1, :]
        decays = jnp.exp(jnp.where(allowed, spread, 0.0))
        mixing = (scores * decays * rows_ref[heads + h : heads + h + 1, :]).astype(BF16)
        x_h = x_ref[:, span]
        out = jnp.dot(mixing, x_h, preferred_element_type=F32) + skip[h] * x_h.astype(F32)
        v = z_ref[:, span].astype(F32)
        gate = v / (1.0 + jnp.exp(-v))
        own_ref[:, span] = out * gate
        open_ref[:, span] = gate * cols_ref[:, 3 * heads + h : 3 * heads + h + 1]


def plane_kernel(got_ref, out_ref):
    count, rows, lanes = got_ref.shape
    state_rows = rows - PAD
    total, keep = piece(got_ref, 0, state_rows)
    for i in range(1, count):
        state, factor = piece(got_ref, i, state_rows)
        total = factor * total + state
        keep = keep * factor
    total, keep = (total.astype(BF16), keep_rows(keep))
    for i in range(out_ref.shape[0]):
        out_ref[i, :state_rows, :] = total
        out_ref[i, state_rows:, :] = keep


def entry_kernel(plane, got_ref, planes_ref, out_ref):
    count, rows, lanes = got_ref.shape
    state_rows = rows - PAD
    mine = plane[0]
    entry = jnp.zeros((state_rows, lanes), F32)
    for i in range(planes_ref.shape[0] - 1):
        state, factor = piece(planes_ref, i, state_rows)
        entry = jnp.where(i < mine, factor * entry + state, entry)
    out_ref[0] = entry.astype(BF16)
    for i in range(count - 1):
        state, factor = piece(got_ref, i, state_rows)
        entry = factor * entry + state
        out_ref[i + 1] = entry.astype(BF16)


def project_kernel(entry_ref, c_ref, own_ref, open_ref, gain_ref, w_ref, out_ref, square_ref):
    heads, width, lanes = entry_ref.shape
    entries = entry_ref[...].reshape(heads * width, lanes)
    carried = lax.dot_general(c_ref[...], entries, (((1,), (1,)), ((), ())), preferred_element_type=F32)
    gated = own_ref[...] + open_ref[...] * carried
    tokens = gated.shape[0]
    squares = jnp.sum(gated * gated, axis=1, keepdims=True)
    square_ref[...] = jnp.broadcast_to(squares, (tokens, 128)).T[:1]
    gated = (gated * gain_ref[...]).astype(BF16)
    groups, _, features = out_ref.shape
    for g in range(groups):
        out_ref[g] = jnp.dot(
            gated, w_ref[:, g * features : (g + 1) * features], preferred_element_type=F32
        ).astype(BF16)


def scale_kernel(inner, summed_ref, square_ref, out_ref):
    tokens, features = out_ref.shape
    factor = lax.rsqrt(square_ref[...] * (1.0 / inner) + 1e-05)
    factor = jnp.broadcast_to(factor, (128, tokens)).T
    for i in range(features // 128):
        span = slice(i * 128, (i + 1) * 128)
        out_ref[:, span] = (summed_ref[:, span].astype(F32) * factor).astype(BF16)


def call(kernel, ins, outs, args, flops=0, moved=0, limit=None):
    return pl.pallas_call(
        kernel,
        in_specs=ins,
        out_specs=[VMEM] * len(outs),
        out_shape=[jax.ShapeDtypeStruct(*o) for o in outs],
        cost_estimate=pl.CostEstimate(flops=flops, bytes_accessed=moved, transcendentals=0),
        compiler_params=pltpu.CompilerParams(vmem_limit_bytes=limit or 16 * 2**20),
    )(*args)


def body(
    input_x, input_z, input_b, input_c, step_raw, doc_starts, log_rate, step_bias, skip_gain, norm_gain, out_weight
):
    tokens, channels = input_x.shape
    heads = log_rate.shape[0]
    width = channels // heads
    state_width = input_b.shape[1]
    devices = lax.axis_size("seq")
    parts = lax.axis_size("head")
    planes = devices // N_ROW
    in_plane = [[p * N_ROW + i for i in range(N_ROW)] for p in range(planes)]
    across = [[p * N_ROW + i for p in range(planes)] for i in range(N_ROW)]
    sent = (width + PAD, state_width)

    pieces, rows, cols = call(
        state_kernel,
        [SMEM, SMEM] + [VMEM] * 4,
        [((heads, *sent), BF16), ((5 * heads, tokens), F32), ((tokens, 128), F32)],
        (log_rate, step_bias, step_raw.T, doc_starts.reshape(1, tokens), input_x, input_b),
        flops=2 * tokens * channels * state_width,
        moved=2 * tokens * channels,
    )
    got = lax.all_to_all(pieces, "seq", 0, 0, axis_index_groups=in_plane)
    own, opened = call(
        intra_kernel,
        [SMEM] + [VMEM] * 6,
        [((tokens, channels), F32)] * 2,
        (skip_gain, rows, cols, input_x, input_z, input_b, input_c),
        flops=2 * tokens * tokens * channels,
        moved=12 * tokens * channels,
    )
    (totals,) = call(plane_kernel, [VMEM], [((planes, *sent), BF16)], (got,), moved=2**19)
    got_planes = lax.all_to_all(totals, "seq", 0, 0, axis_index_groups=across)
    plane = lax.div(lax.axis_index("seq"), N_ROW).reshape(1)
    (entries,) = call(
        entry_kernel, [SMEM, VMEM, VMEM], [((N_ROW, width, state_width), BF16)], (plane, got, got_planes), moved=2**19
    )
    entries = lax.all_to_all(entries, "seq", 0, 0, axis_index_groups=in_plane)
    partial, squares = call(
        project_kernel,
        [VMEM] * 6,
        [((parts, tokens, out_weight.shape[1] // parts), BF16), ((1, tokens), F32)],
        (entries, input_c, own, opened, norm_gain.reshape(1, channels), out_weight),
        flops=2 * tokens * channels * out_weight.shape[1],
        moved=8 * 2**20,
        limit=32 * 2**20,
    )
    summed = lax.psum_scatter(partial, "head", scatter_dimension=0, tiled=False)
    squares = lax.psum(squares, "head")
    (out,) = call(
        lambda *refs: scale_kernel(channels * parts, *refs),
        [VMEM] * 2,
        [(summed.shape, BF16)],
        (summed, squares),
        moved=2**19,
    )
    return out


def solution(mesh):
    in_specs = (
        P("seq", "head"),
        P("seq", "head"),
        P("seq", None),
        P("seq", None),
        P("seq", "head"),
        P("seq"),
        P("head"),
        P("head"),
        P("head"),
        P("head"),
        P("head", None),
    )
    out_specs = P("seq", "head")
    return jax.shard_map(body, mesh=mesh, in_specs=in_specs, out_specs=out_specs, check_vma=False)
```

```python
import jax
import jax.numpy as jnp
from jax import lax
from jax.experimental import pallas as pl
from jax.experimental.pallas import tpu as pltpu
from jax.sharding import PartitionSpec as P

SPAN = 256
N_ROW = 8
PAD = 16
F32, BF16 = (jnp.float32, jnp.bfloat16)
VMEM = pl.BlockSpec(memory_space=pltpu.VMEM)
SMEM = pl.BlockSpec(memory_space=pltpu.SMEM)
HBM = pl.BlockSpec(memory_space=pltpu.HBM)
ANY = pl.BlockSpec(memory_space=pl.ANY)


def column_of(row, shape):
    count = shape[0]
    spread = jnp.broadcast_to(row, (count, count))
    same = lax.broadcasted_iota(jnp.int32, spread.shape, 0) == lax.broadcasted_iota(jnp.int32, spread.shape, 1)
    return jnp.broadcast_to(jnp.sum(jnp.where(same, spread, 0.0), axis=1, keepdims=True), shape)


def fetch(sources, targets, sems):
    copies = [pltpu.make_async_copy(s, t, sems.at[i]) for i, (s, t) in enumerate(zip(sources, targets))]
    for copy in copies:
        copy.start()
    return copies


def running_sum(rows):
    lanes = lax.broadcasted_iota(jnp.int32, rows.shape, 1)
    step = 1
    while step < rows.shape[1]:
        rows = rows + jnp.where(lanes >= step, pltpu.roll(rows, step, 1), 0.0)
        step *= 2
    return rows


def keep_rows(keep):
    high = keep.astype(BF16).astype(F32)
    middle = (keep - high).astype(BF16).astype(F32)
    low = keep - high - middle
    rows = lax.broadcasted_iota(jnp.int32, (PAD, keep.shape[1]), 0)
    out = jnp.where(rows == 0, high, jnp.where(rows == 1, middle, jnp.where(rows == 2, low, 0.0)))
    return out.astype(BF16)


def piece(ref, index, state_rows):
    state = ref[index, :state_rows, :].astype(F32)
    keep = jnp.sum(ref[index, state_rows:, :].astype(F32), axis=0, keepdims=True)
    return state, keep


def state_kernel(*refs):
    (log_rate, bias, raw_ref, flag_ref, b_ref, x_ref) = refs[9:15]
    out_ref, rows_ref, cols_ref = refs[6:9]
    copies = fetch(refs[:6], refs[9:15], refs[15])
    for copy in copies[:4]:
        copy.wait()
    heads, tokens = raw_ref.shape
    width = x_ref.shape[1] // heads
    raw = raw_ref[...]
    dt = jax.nn.softplus(raw + column_of(bias[...], raw.shape))
    rate = -jnp.exp(column_of(log_rate[...], raw.shape))
    flags = jnp.broadcast_to(flag_ref[...].astype(F32), raw.shape)
    sums = running_sum(jnp.concatenate([rate * dt, flags], axis=0))
    running, resets = (sums[:heads], sums[heads:])
    run_last = jnp.broadcast_to(running[:, tokens - 1 :], raw.shape)
    reset_last = jnp.broadcast_to(resets[:, tokens - 1 :], raw.shape)
    weights = jnp.where(resets == reset_last, jnp.exp(run_last - running), 0.0) * dt
    opening = jnp.where(resets == 0.0, jnp.exp(running), 0.0)
    rows = jnp.concatenate([running, dt, resets, opening, weights], axis=0)
    rows_ref[...] = rows
    cols = jnp.concatenate([rows, jnp.zeros((128 - rows.shape[0], tokens), F32)], axis=0).T
    cols_ref[...] = cols
    through = jnp.where(reset_last == 0.0, jnp.exp(run_last), 0.0)
    spread = jnp.concatenate(
        [
            jnp.broadcast_to(cols[:, 4 * heads + h : 4 * heads + h + 1], (tokens, width))
            for h in range(heads)
        ],
        axis=1,
    )
    for copy in copies[4:]:
        copy.wait()
    scaled = (spread * x_ref[...].astype(F32)).astype(BF16)
    states = lax.dot_general(scaled, b_ref[...], (((0,), (0,)), ((), ())), preferred_element_type=F32)
    for h in range(heads):
        out_ref[h, :width, :] = states[h * width : (h + 1) * width].astype(BF16)
        out_ref[h, width:, :] = keep_rows(through[h : h + 1, :128])


def intra_kernel(*refs):
    own_ref, open_ref, done_ref = refs[7:10]
    c_ref, b_ref, rows_ref, cols_ref, skip_ref, x_ref, z_ref = refs[10:17]
    for copy in fetch(refs[:7], refs[10:17], refs[17]):
        copy.wait()
    done_ref[...] = jnp.zeros_like(done_ref)
    tokens = x_ref.shape[0]
    heads = skip_ref.shape[1]
    width = x_ref.shape[1] // heads
    skip = skip_ref[...]
    scores = lax.dot_general(c_ref[...], b_ref[...], (((1,), (1,)), ((), ())), preferred_element_type=F32)
    reset_row = rows_ref[2 * heads : 2 * heads + 1, :]
    reset_col = cols_ref[:, 2 * heads : 2 * heads + 1]
    later = lax.broadcasted_iota(jnp.int32, scores.shape, 0)
    earlier = lax.broadcasted_iota(jnp.int32, scores.shape, 1)
    allowed = (later >= earlier) & (reset_col == reset_row)
    scores = jnp.where(allowed, scores, 0.0)
    for h in range(heads):
        span = slice(h * width, (h + 1) * width)
        spread = cols_ref[:, h : h + 1] - rows_ref[h : h + 1, :]
        decays = jnp.exp(jnp.where(allowed, spread, 0.0))
        mixing = (scores * decays * rows_ref[heads + h : heads + h + 1, :]).astype(BF16)
        x_h = x_ref[:, span]
        out = jnp.dot(mixing, x_h, preferred_element_type=F32) + skip[:, h : h + 1] * x_h.astype(F32)
        v = z_ref[:, span].astype(F32)
        gate = v / (1.0 + jnp.exp(-v))
        own_ref[:, span] = out * gate
        open_ref[:, span] = gate * cols_ref[:, 3 * heads + h : 3 * heads + h + 1]


def plane_kernel(after_ref, got_ref, out_ref):
    count, rows, lanes = got_ref.shape
    state_rows = rows - PAD
    total, keep = piece(got_ref, 0, state_rows)
    for i in range(1, count):
        state, factor = piece(got_ref, i, state_rows)
        total = factor * total + state
        keep = keep * factor
    total, keep = (total.astype(BF16), keep_rows(keep))
    for i in range(out_ref.shape[0]):
        out_ref[i, :state_rows, :] = total
        out_ref[i, state_rows:, :] = keep


def entry_kernel(plane, got_ref, planes_ref, out_ref):
    count, rows, lanes = got_ref.shape
    state_rows = rows - PAD
    mine = plane[0]
    entry = jnp.zeros((state_rows, lanes), F32)
    for i in range(planes_ref.shape[0] - 1):
        state, factor = piece(planes_ref, i, state_rows)
        entry = jnp.where(i < mine, factor * entry + state, entry)
    out_ref[0] = entry.astype(BF16)
    for i in range(count - 1):
        state, factor = piece(got_ref, i, state_rows)
        entry = factor * entry + state
        out_ref[i + 1] = entry.astype(BF16)


def project_kernel(*refs):
    out_ref, square_ref = refs[6:8]
    entry_ref, c_ref, own_ref, open_ref, gain_ref, w_ref = refs[8:14]
    groups, tokens, features = out_ref.shape
    copies = fetch(refs[:5], refs[8:13], refs[14])
    spans = [slice(g * features, (g + 1) * features) for g in range(groups)]
    weights = fetch([refs[5].at[:, s] for s in spans], [w_ref.at[:, s] for s in spans], refs[15])
    for copy in copies:
        copy.wait()
    heads, width, lanes = entry_ref.shape
    entries = entry_ref[...].reshape(heads * width, lanes)
    carried = lax.dot_general(c_ref[...], entries, (((1,), (1,)), ((), ())), preferred_element_type=F32)
    gated = own_ref[...] + open_ref[...] * carried
    squares = jnp.sum(gated * gated, axis=1, keepdims=True)
    square_ref[...] = jnp.broadcast_to(squares, (tokens, 128)).T[:1]
    gated = (gated * gain_ref[...]).astype(BF16)
    for g in range(groups):
        weights[g].wait()
        out_ref[g] = jnp.dot(gated, w_ref[:, spans[g]], preferred_element_type=F32).astype(BF16)


def scale_kernel(inner, summed_hbm, square_ref, out_ref, summed_ref, sems, _):
    (copy,) = fetch([summed_hbm], [summed_ref], sems)
    tokens, features = out_ref.shape
    factor = lax.rsqrt(square_ref[...] * (1.0 / inner) + 1e-05)
    factor = jnp.broadcast_to(factor, (128, tokens)).T
    copy.wait()
    for i in range(features // 128):
        span = slice(i * 128, (i + 1) * 128)
        out_ref[:, span] = (summed_ref[:, span].astype(F32) * factor).astype(BF16)


def call(kernel, ins, outs, args, fetched=(), flops=0, moved=0, limit=None):
    scratch = [pltpu.VMEM(a.shape, a.dtype) for a in fetched]
    return pl.pallas_call(
        kernel,
        in_specs=ins,
        out_specs=[VMEM] * len(outs),
        out_shape=[jax.ShapeDtypeStruct(*o) for o in outs],
        scratch_shapes=scratch + [pltpu.SemaphoreType.DMA((8,))] * 2 * (HBM in ins),
        cost_estimate=pl.CostEstimate(flops=flops, bytes_accessed=moved, transcendentals=0),
        compiler_params=pltpu.CompilerParams(vmem_limit_bytes=limit or 16 * 2**20),
    )(*args)


def body(
    input_x, input_z, input_b, input_c, step_raw, doc_starts, log_rate, step_bias, skip_gain, norm_gain, out_weight
):
    tokens, channels = input_x.shape
    heads = log_rate.shape[0]
    width = channels // heads
    state_width = input_b.shape[1]
    parts = lax.axis_size("head")
    planes = lax.axis_size("seq") // N_ROW
    in_plane = [[p * N_ROW + i for i in range(N_ROW)] for p in range(planes)]
    across = [[p * N_ROW + i for p in range(planes)] for i in range(N_ROW)]
    sent = (width + PAD, state_width)

    local = (
        log_rate.reshape(1, heads),
        step_bias.reshape(1, heads),
        step_raw.T,
        doc_starts.reshape(1, tokens),
        input_b,
        input_x,
    )
    pieces, rows, cols = call(
        state_kernel,
        [HBM] * 6,
        [((heads, *sent), BF16), ((5 * heads, tokens), F32), ((tokens, 128), F32)],
        local,
        fetched=local,
        limit=60 * 2**20,
        flops=2 * tokens * channels * state_width,
        moved=2 * tokens * channels,
    )
    got = lax.all_to_all(pieces, "seq", 0, 0, axis_index_groups=in_plane)
    skip = skip_gain.reshape(1, heads)
    gain = norm_gain.reshape(1, channels)
    near = (input_c, input_b, rows, cols, skip, input_x, input_z)
    own, opened, done = call(
        intra_kernel,
        [HBM] * 7,
        [((tokens, channels), F32)] * 2 + [((8, 128), F32)],
        near,
        fetched=near,
        flops=2 * tokens * tokens * channels,
        moved=8 * 2**20,
        limit=60 * 2**20,
    )
    (totals,) = call(plane_kernel, [ANY, VMEM], [((planes, *sent), BF16)], (done, got), moved=2**19)
    got_planes = lax.all_to_all(totals, "seq", 0, 0, axis_index_groups=across)
    plane = lax.div(lax.axis_index("seq"), N_ROW).reshape(1)
    (entries,) = call(
        entry_kernel, [SMEM, VMEM, VMEM], [((N_ROW, width, state_width), BF16)], (plane, got, got_planes), moved=2**19
    )
    entries = lax.all_to_all(entries, "seq", 0, 0, axis_index_groups=in_plane)
    last = (entries, input_c, own, opened, gain, out_weight)
    partial, squares = call(
        project_kernel,
        [HBM] * 6,
        [((parts, tokens, out_weight.shape[1] // parts), BF16), ((1, tokens), F32)],
        last,
        fetched=last,
        flops=2 * tokens * channels * out_weight.shape[1],
        moved=8 * 2**20,
        limit=60 * 2**20,
    )
    summed = lax.psum_scatter(partial, "head", scatter_dimension=0, tiled=False)
    squares = lax.psum(squares, "head")
    (out,) = call(
        lambda *refs: scale_kernel(channels * parts, *refs),
        [HBM, VMEM],
        [(summed.shape, BF16)],
        (summed, squares),
        fetched=(summed,),
        limit=60 * 2**20,
        moved=2**19,
    )
    return out


def solution(mesh):
    in_specs = (
        P("seq", "head"),
        P("seq", "head"),
        P("seq", None),
        P("seq", None),
        P("seq", "head"),
        P("seq"),
        P("head"),
        P("head"),
        P("head"),
        P("head"),
        P("head", None),
    )
    out_specs = P("seq", "head")
    return jax.shard_map(body, mesh=mesh, in_specs=in_specs, out_specs=out_specs, check_vma=False)
```

```python
import jax
import jax.numpy as jnp
from jax import lax
from jax.experimental import pallas as pl
from jax.experimental.pallas import tpu as pltpu
from jax.sharding import PartitionSpec as P

SPAN = 256
N_ROW = 8
PAD = 16
F32, BF16 = (jnp.float32, jnp.bfloat16)
VMEM = pl.BlockSpec(memory_space=pltpu.VMEM)
SMEM = pl.BlockSpec(memory_space=pltpu.SMEM)
HBM = pl.BlockSpec(memory_space=pltpu.HBM)
ANY = pl.BlockSpec(memory_space=pl.ANY)


def column_of(row, shape):
    count = shape[0]
    spread = jnp.broadcast_to(row, (count, count))
    same = lax.broadcasted_iota(jnp.int32, spread.shape, 0) == lax.broadcasted_iota(jnp.int32, spread.shape, 1)
    return jnp.broadcast_to(jnp.sum(jnp.where(same, spread, 0.0), axis=1, keepdims=True), shape)


def fetch(sources, targets, sems):
    copies = [pltpu.make_async_copy(s, t, sems.at[i]) for i, (s, t) in enumerate(zip(sources, targets))]
    for copy in copies:
        copy.start()
    return copies


def running_sum(rows):
    lanes = lax.broadcasted_iota(jnp.int32, rows.shape, 1)
    step = 1
    while step < rows.shape[1]:
        rows = rows + jnp.where(lanes >= step, pltpu.roll(rows, step, 1), 0.0)
        step *= 2
    return rows


def keep_rows(keep):
    high = keep.astype(BF16).astype(F32)
    middle = (keep - high).astype(BF16).astype(F32)
    low = keep - high - middle
    rows = lax.broadcasted_iota(jnp.int32, (PAD, keep.shape[1]), 0)
    out = jnp.where(rows == 0, high, jnp.where(rows == 1, middle, jnp.where(rows == 2, low, 0.0)))
    return out.astype(BF16)


def piece(ref, index, state_rows):
    state = ref[index, :state_rows, :].astype(F32)
    keep = jnp.sum(ref[index, state_rows:, :].astype(F32), axis=0, keepdims=True)
    return state, keep


def state_kernel(*refs):
    (log_rate, bias, raw_ref, flag_ref, b_ref, x_ref) = refs[9:15]
    out_ref, rows_ref, cols_ref = refs[6:9]
    copies = fetch(refs[:6], refs[9:15], refs[15])
    for copy in copies[:4]:
        copy.wait()
    heads, tokens = raw_ref.shape
    width = x_ref.shape[1] // heads
    raw = raw_ref[...]
    dt = jax.nn.softplus(raw + column_of(bias[...], raw.shape))
    rate = -jnp.exp(column_of(log_rate[...], raw.shape))
    flags = jnp.broadcast_to(flag_ref[...].astype(F32), raw.shape)
    sums = running_sum(jnp.concatenate([rate * dt, flags], axis=0))
    running, resets = (sums[:heads], sums[heads:])
    run_last = jnp.broadcast_to(running[:, tokens - 1 :], raw.shape)
    reset_last = jnp.broadcast_to(resets[:, tokens - 1 :], raw.shape)
    weights = jnp.where(resets == reset_last, jnp.exp(run_last - running), 0.0) * dt
    opening = jnp.where(resets == 0.0, jnp.exp(running), 0.0)
    rows = jnp.concatenate([running, dt, resets, opening, weights], axis=0)
    rows_ref[...] = rows
    cols = jnp.concatenate([rows, jnp.zeros((128 - rows.shape[0], tokens), F32)], axis=0).T
    cols_ref[...] = cols
    through = jnp.where(reset_last == 0.0, jnp.exp(run_last), 0.0)
    spread = jnp.concatenate(
        [
            jnp.broadcast_to(cols[:, 4 * heads + h : 4 * heads + h + 1], (tokens, width))
            for h in range(heads)
        ],
        axis=1,
    )
    for copy in copies[4:]:
        copy.wait()
    scaled = (spread * x_ref[...].astype(F32)).astype(BF16)
    states = lax.dot_general(scaled, b_ref[...], (((0,), (0,)), ((), ())), preferred_element_type=F32)
    for h in range(heads):
        out_ref[h, :width, :] = states[h * width : (h + 1) * width].astype(BF16)
        out_ref[h, width:, :] = keep_rows(through[h : h + 1, :128])


def intra_kernel(*refs):
    own_ref, open_ref, done_ref = refs[7:10]
    c_ref, b_ref, rows_ref, cols_ref, skip_ref, x_ref, z_ref = refs[10:17]
    for copy in fetch(refs[:7], refs[10:17], refs[17]):
        copy.wait()
    done_ref[...] = jnp.zeros_like(done_ref)
    tokens = x_ref.shape[0]
    heads = skip_ref.shape[1]
    width = x_ref.shape[1] // heads
    skip = skip_ref[...]
    scores = lax.dot_general(c_ref[...], b_ref[...], (((1,), (1,)), ((), ())), preferred_element_type=F32)
    reset_row = rows_ref[2 * heads : 2 * heads + 1, :]
    reset_col = cols_ref[:, 2 * heads : 2 * heads + 1]
    later = lax.broadcasted_iota(jnp.int32, scores.shape, 0)
    earlier = lax.broadcasted_iota(jnp.int32, scores.shape, 1)
    allowed = (later >= earlier) & (reset_col == reset_row)
    scores = jnp.where(allowed, scores, 0.0)
    for h in range(heads):
        span = slice(h * width, (h + 1) * width)
        spread = cols_ref[:, h : h + 1] - rows_ref[h : h + 1, :]
        decays = jnp.exp(jnp.where(allowed, spread, 0.0))
        mixing = (scores * decays * rows_ref[heads + h : heads + h + 1, :]).astype(BF16)
        x_h = x_ref[:, span]
        out = jnp.dot(mixing, x_h, preferred_element_type=F32) + skip[:, h : h + 1] * x_h.astype(F32)
        v = z_ref[:, span].astype(F32)
        gate = v / (1.0 + jnp.exp(-v))
        own_ref[:, span] = out * gate
        open_ref[:, span] = gate * cols_ref[:, 3 * heads + h : 3 * heads + h + 1]


def plane_kernel(after_ref, got_ref, out_ref):
    count, rows, lanes = got_ref.shape
    state_rows = rows - PAD
    total, keep = piece(got_ref, 0, state_rows)
    for i in range(1, count):
        state, factor = piece(got_ref, i, state_rows)
        total = factor * total + state
        keep = keep * factor
    total, keep = (total.astype(BF16), keep_rows(keep))
    for i in range(out_ref.shape[0]):
        out_ref[i, :state_rows, :] = total
        out_ref[i, state_rows:, :] = keep


def entry_kernel(plane, got_ref, planes_ref, out_ref):
    count, rows, lanes = got_ref.shape
    state_rows = rows - PAD
    mine = plane[0]
    entry = jnp.zeros((state_rows, lanes), F32)
    for i in range(planes_ref.shape[0] - 1):
        state, factor = piece(planes_ref, i, state_rows)
        entry = jnp.where(i < mine, factor * entry + state, entry)
    out_ref[0] = entry.astype(BF16)
    for i in range(count - 1):
        state, factor = piece(got_ref, i, state_rows)
        entry = factor * entry + state
        out_ref[i + 1] = entry.astype(BF16)


def project_kernel(*refs):
    out_hbm, square_ref = refs[6:8]
    entry_ref, c_ref, own_ref, open_ref, gain_ref, w_ref = refs[8:14]
    out_ref, in_sems, w_sems, out_sems = refs[14:]
    groups, tokens, features = out_ref.shape
    copies = fetch(refs[:5], refs[8:13], in_sems)
    for copy in copies:
        copy.wait()
    spans = [slice(g * features, (g + 1) * features) for g in range(groups)]
    weights = fetch([refs[5].at[:, s] for s in spans], [w_ref.at[:, s] for s in spans], w_sems)
    heads, width, lanes = entry_ref.shape
    entries = entry_ref[...].reshape(heads * width, lanes)
    carried = lax.dot_general(c_ref[...], entries, (((1,), (1,)), ((), ())), preferred_element_type=F32)
    gated = own_ref[...] + open_ref[...] * carried
    scaled = (gated * gain_ref[...]).astype(BF16)
    sent = []
    for g in range(groups):
        weights[g].wait()
        out_ref[g] = jnp.dot(scaled, w_ref[:, spans[g]], preferred_element_type=F32).astype(BF16)
        sent.append(pltpu.make_async_copy(out_ref.at[g], out_hbm.at[g], out_sems.at[g]))
        sent[g].start()
    squares = jnp.sum(gated * gated, axis=1, keepdims=True)
    square_ref[...] = jnp.broadcast_to(squares, (tokens, 128)).T[:1]
    for copy in sent:
        copy.wait()


def scale_kernel(inner, summed_hbm, square_ref, out_ref, summed_ref, sems, *_):
    (copy,) = fetch([summed_hbm], [summed_ref], sems)
    tokens, features = out_ref.shape
    factor = lax.rsqrt(square_ref[...] * (1.0 / inner) + 1e-05)
    factor = jnp.broadcast_to(factor, (128, tokens)).T
    copy.wait()
    for i in range(features // 128):
        span = slice(i * 128, (i + 1) * 128)
        out_ref[:, span] = (summed_ref[:, span].astype(F32) * factor).astype(BF16)


def call(kernel, ins, outs, args, fetched=(), staged=(), flops=0, moved=0):
    scratch = [pltpu.VMEM(a.shape, a.dtype) for a in fetched]
    scratch += [pltpu.VMEM(*a) for a in staged]
    scratch += [pltpu.SemaphoreType.DMA((8,))] * 3 * (len(fetched) > 0)
    return pl.pallas_call(
        kernel,
        in_specs=ins,
        out_specs=[HBM] * len(staged) + [VMEM] * (len(outs) - len(staged)),
        out_shape=[jax.ShapeDtypeStruct(*o) for o in outs],
        scratch_shapes=scratch,
        cost_estimate=pl.CostEstimate(flops=flops, bytes_accessed=moved, transcendentals=0),
        compiler_params=pltpu.CompilerParams(vmem_limit_bytes=(60 if fetched else 16) * 2**20),
    )(*args)


def body(
    input_x, input_z, input_b, input_c, step_raw, doc_starts, log_rate, step_bias, skip_gain, norm_gain, out_weight
):
    tokens, channels = input_x.shape
    heads = log_rate.shape[0]
    width = channels // heads
    state_width = input_b.shape[1]
    parts = lax.axis_size("head")
    planes = lax.axis_size("seq") // N_ROW
    in_plane = [[p * N_ROW + i for i in range(N_ROW)] for p in range(planes)]
    across = [[p * N_ROW + i for p in range(planes)] for i in range(N_ROW)]
    sent = (width + PAD, state_width)

    local = (
        log_rate.reshape(1, heads),
        step_bias.reshape(1, heads),
        step_raw.T,
        doc_starts.reshape(1, tokens),
        input_b,
        input_x,
    )
    pieces, rows, cols = call(
        state_kernel,
        [HBM] * 6,
        [((heads, *sent), BF16), ((5 * heads, tokens), F32), ((tokens, 128), F32)],
        local,
        fetched=local,
        flops=2 * tokens * channels * state_width,
        moved=2 * tokens * channels,
    )
    got = lax.all_to_all(pieces, "seq", 0, 0, axis_index_groups=in_plane)
    skip = skip_gain.reshape(1, heads)
    gain = norm_gain.reshape(1, channels)
    near = (input_c, input_b, rows, cols, skip, input_x, input_z)
    own, opened, done = call(
        intra_kernel,
        [HBM] * 7,
        [((tokens, channels), F32)] * 2 + [((8, 128), F32)],
        near,
        fetched=near,
        flops=2 * tokens * tokens * channels,
        moved=8 * 2**20,
    )
    (totals,) = call(plane_kernel, [ANY, VMEM], [((planes, *sent), BF16)], (done, got), moved=2**19)
    got_planes = lax.all_to_all(totals, "seq", 0, 0, axis_index_groups=across)
    plane = lax.div(lax.axis_index("seq"), N_ROW).reshape(1)
    (entries,) = call(
        entry_kernel, [SMEM, VMEM, VMEM], [((N_ROW, width, state_width), BF16)], (plane, got, got_planes), moved=2**19
    )
    entries = lax.all_to_all(entries, "seq", 0, 0, axis_index_groups=in_plane)
    last = (entries, input_c, own, opened, gain, out_weight)
    partials = ((parts, tokens, out_weight.shape[1] // parts), BF16)
    partial, squares = call(
        project_kernel,
        [HBM] * 6,
        [partials, ((1, tokens), F32)],
        last,
        fetched=last,
        staged=[partials],
        flops=2 * tokens * channels * out_weight.shape[1],
        moved=8 * 2**20,
    )
    summed = lax.psum_scatter(partial, "head", scatter_dimension=0, tiled=False)
    squares = lax.psum(squares, "head")
    (out,) = call(
        lambda *refs: scale_kernel(channels * parts, *refs),
        [HBM, VMEM],
        [(summed.shape, BF16)],
        (summed, squares),
        fetched=(summed,),
        moved=2**19,
    )
    return out


def solution(mesh):
    in_specs = (
        P("seq", "head"),
        P("seq", "head"),
        P("seq", None),
        P("seq", None),
        P("seq", "head"),
        P("seq"),
        P("head"),
        P("head"),
        P("head"),
        P("head"),
        P("head", None),
    )
    out_specs = P("seq", "head")
    return jax.shard_map(body, mesh=mesh, in_specs=in_specs, out_specs=out_specs, check_vma=False)
```

```python
import functools

import jax
import jax.numpy as jnp
from jax import lax
from jax.experimental import pallas as pl
from jax.experimental.pallas import tpu as pltpu
from jax.sharding import PartitionSpec as P

SPAN = 256
N_ROW = 8
N_PART = 8
NEAR = (3, -3, 2, -2, 1, -1, 0)
PAD = 16
F32, BF16 = (jnp.float32, jnp.bfloat16)
VMEM = pl.BlockSpec(memory_space=pltpu.VMEM)
SMEM = pl.BlockSpec(memory_space=pltpu.SMEM)
HBM = pl.BlockSpec(memory_space=pltpu.HBM)
ANY = pl.BlockSpec(memory_space=pl.ANY)


def column_of(row, shape):
    count = shape[0]
    spread = jnp.broadcast_to(row, (count, count))
    same = lax.broadcasted_iota(jnp.int32, spread.shape, 0) == lax.broadcasted_iota(jnp.int32, spread.shape, 1)
    return jnp.broadcast_to(jnp.sum(jnp.where(same, spread, 0.0), axis=1, keepdims=True), shape)


def fetch(sources, targets, sems):
    copies = [pltpu.make_async_copy(s, t, sems.at[i]) for i, (s, t) in enumerate(zip(sources, targets))]
    for copy in copies:
        copy.start()
    return copies


def running_sum(rows):
    lanes = lax.broadcasted_iota(jnp.int32, rows.shape, 1)
    step = 1
    while step < rows.shape[1]:
        rows = rows + jnp.where(lanes >= step, pltpu.roll(rows, step, 1), 0.0)
        step *= 2
    return rows


def keep_rows(keep):
    high = keep.astype(BF16).astype(F32)
    middle = (keep - high).astype(BF16).astype(F32)
    low = keep - high - middle
    rows = lax.broadcasted_iota(jnp.int32, (PAD, keep.shape[1]), 0)
    out = jnp.where(rows == 0, high, jnp.where(rows == 1, middle, jnp.where(rows == 2, low, 0.0)))
    return out.astype(BF16)


def piece(ref, index, state_rows):
    state = ref[index, :state_rows, :].astype(F32)
    keep = jnp.sum(ref[index, state_rows:, :].astype(F32), axis=0, keepdims=True)
    return state, keep


def state_kernel(*refs):
    (log_rate, bias, raw_ref, flag_ref, b_ref, x_ref) = refs[9:15]
    out_ref, rows_ref, cols_ref = refs[6:9]
    copies = fetch(refs[:6], refs[9:15], refs[15])
    for copy in copies[:4]:
        copy.wait()
    heads, tokens = raw_ref.shape
    width = x_ref.shape[1] // heads
    raw = raw_ref[...]
    dt = jax.nn.softplus(raw + column_of(bias[...], raw.shape))
    rate = -jnp.exp(column_of(log_rate[...], raw.shape))
    flags = jnp.broadcast_to(flag_ref[...].astype(F32), raw.shape)
    sums = running_sum(jnp.concatenate([rate * dt, flags], axis=0))
    running, resets = (sums[:heads], sums[heads:])
    run_last = jnp.broadcast_to(running[:, tokens - 1 :], raw.shape)
    reset_last = jnp.broadcast_to(resets[:, tokens - 1 :], raw.shape)
    weights = jnp.where(resets == reset_last, jnp.exp(run_last - running), 0.0) * dt
    opening = jnp.where(resets == 0.0, jnp.exp(running), 0.0)
    rows = jnp.concatenate([running, dt, resets, opening, weights], axis=0)
    rows_ref[...] = rows
    cols = jnp.concatenate([rows, jnp.zeros((128 - rows.shape[0], tokens), F32)], axis=0).T
    cols_ref[...] = cols
    through = jnp.where(reset_last == 0.0, jnp.exp(run_last), 0.0)
    spread = jnp.concatenate(
        [
            jnp.broadcast_to(cols[:, 4 * heads + h : 4 * heads + h + 1], (tokens, width))
            for h in range(heads)
        ],
        axis=1,
    )
    for copy in copies[4:]:
        copy.wait()
    scaled = (spread * x_ref[...].astype(F32)).astype(BF16)
    states = lax.dot_general(scaled, b_ref[...], (((0,), (0,)), ((), ())), preferred_element_type=F32)
    for h in range(heads):
        out_ref[h, :width, :] = states[h * width : (h + 1) * width].astype(BF16)
        out_ref[h, width:, :] = keep_rows(through[h : h + 1, :128])


def intra_kernel(*refs):
    own_ref, open_ref, done_ref = refs[7:10]
    c_ref, b_ref, rows_ref, cols_ref, skip_ref, x_ref, z_ref = refs[10:17]
    for copy in fetch(refs[:7], refs[10:17], refs[17]):
        copy.wait()
    done_ref[...] = jnp.zeros_like(done_ref)
    tokens = x_ref.shape[0]
    heads = skip_ref.shape[1]
    width = x_ref.shape[1] // heads
    skip = skip_ref[...]
    scores = lax.dot_general(c_ref[...], b_ref[...], (((1,), (1,)), ((), ())), preferred_element_type=F32)
    reset_row = rows_ref[2 * heads : 2 * heads + 1, :]
    reset_col = cols_ref[:, 2 * heads : 2 * heads + 1]
    later = lax.broadcasted_iota(jnp.int32, scores.shape, 0)
    earlier = lax.broadcasted_iota(jnp.int32, scores.shape, 1)
    allowed = (later >= earlier) & (reset_col == reset_row)
    scores = jnp.where(allowed, scores, 0.0)
    for h in range(heads):
        span = slice(h * width, (h + 1) * width)
        spread = cols_ref[:, h : h + 1] - rows_ref[h : h + 1, :]
        decays = jnp.exp(jnp.where(allowed, spread, 0.0))
        mixing = (scores * decays * rows_ref[heads + h : heads + h + 1, :]).astype(BF16)
        x_h = x_ref[:, span]
        out = jnp.dot(mixing, x_h, preferred_element_type=F32) + skip[:, h : h + 1] * x_h.astype(F32)
        v = z_ref[:, span].astype(F32)
        gate = v / (1.0 + jnp.exp(-v))
        own_ref[:, span] = out * gate
        open_ref[:, span] = gate * cols_ref[:, 3 * heads + h : 3 * heads + h + 1]


def plane_kernel(after_ref, got_ref, out_ref):
    count, rows, lanes = got_ref.shape
    state_rows = rows - PAD
    total, keep = piece(got_ref, 0, state_rows)
    for i in range(1, count):
        state, factor = piece(got_ref, i, state_rows)
        total = factor * total + state
        keep = keep * factor
    total, keep = (total.astype(BF16), keep_rows(keep))
    for i in range(out_ref.shape[0]):
        out_ref[i, :state_rows, :] = total
        out_ref[i, state_rows:, :] = keep


def entry_kernel(plane, got_ref, planes_ref, out_ref):
    count, rows, lanes = got_ref.shape
    state_rows = rows - PAD
    mine = plane[0]
    entry = jnp.zeros((state_rows, lanes), F32)
    for i in range(planes_ref.shape[0] - 1):
        state, factor = piece(planes_ref, i, state_rows)
        entry = jnp.where(i < mine, factor * entry + state, entry)
    out_ref[0] = entry.astype(BF16)
    for i in range(count - 1):
        state, factor = piece(got_ref, i, state_rows)
        entry = factor * entry + state
        out_ref[i + 1] = entry.astype(BF16)


def bring_kernel(*refs):
    count = len(refs) // 2 - 1
    for copy in fetch(refs[1 : count + 1], refs[count + 1 : -1], refs[-1]):
        copy.wait()


def put_squares(ref, squares):
    high = squares.astype(BF16).astype(F32)
    middle = (squares - high).astype(BF16).astype(F32)
    low = squares - high - middle
    first = jnp.concatenate([high, middle], axis=1)
    second = jnp.concatenate([low, jnp.zeros_like(low)], axis=1)
    row = lax.broadcasted_iota(jnp.int32, (PAD, ref.shape[1]), 0)
    rows = jnp.where(row == 0, first, jnp.where(row == 1, second, 0.0))
    ref[ref.shape[0] - PAD :, :] = rows.astype(BF16)


def get_squares(ref):
    rows = jnp.sum(ref[ref.shape[0] - PAD :, :].astype(F32), axis=0, keepdims=True)
    half = ref.shape[1] // 2
    return rows[:, :half] + rows[:, half:]


def columns(w_hbm, me, away, features):
    place = (me[0] + away + N_PART) % N_PART
    return w_hbm.at[:, pl.ds(pl.multiple_of(place * features, features), features)]


def gate_kernel(me, entry_ref, c_ref, own_ref, open_ref, gain_ref, w_hbm, *refs):
    scaled_ref, square_ref, right_ref, left_ref, w_ref, sems = refs
    heads, width, lanes = entry_ref.shape
    tokens = own_ref.shape[0]
    half = tokens // 2
    (copy,) = fetch([columns(w_hbm, me, N_PART // 2, w_ref.shape[1])], [w_ref], sems)
    entries = entry_ref[...].reshape(heads * width, lanes)
    carried = lax.dot_general(c_ref[...], entries, (((1,), (1,)), ((), ())), preferred_element_type=F32)
    gated = own_ref[...] + open_ref[...] * carried
    scaled = (gated * gain_ref[...]).astype(BF16)
    scaled_ref[...] = scaled
    squares = jnp.sum(gated * gated, axis=1, keepdims=True)
    squares = jnp.broadcast_to(squares, (tokens, 128)).T[:1]
    square_ref[...] = squares
    first = lax.broadcasted_iota(jnp.int32, squares.shape, 1) < half
    put_squares(right_ref, jnp.where(first, squares, 0.0))
    put_squares(left_ref, jnp.where(first, 0.0, squares))
    copy.wait()
    far = jnp.dot(scaled, w_ref[...], preferred_element_type=F32).astype(BF16)
    right_ref[:half] = far[:half]
    left_ref[:half] = far[half:]


def chunks_kernel(me, scaled_ref, w_hbm, out_ref, w_ref, sems):
    features = out_ref.shape[2]
    copies = fetch([columns(w_hbm, me, away, features) for away in NEAR], [w_ref.at[i] for i in range(len(NEAR))], sems)
    for i, copy in enumerate(copies):
        copy.wait()
        out_ref[i] = jnp.dot(scaled_ref[...], w_ref[i], preferred_element_type=F32).astype(BF16)


def join_kernel(index, from_row, got_ref, chunks_ref, square_ref, out_ref):
    tokens = chunks_ref.shape[1]
    count = got_ref.shape[0] - PAD
    if count < tokens:
        out_ref[:tokens] = chunks_ref[index]
    rows = slice(from_row, from_row + count)
    out_ref[rows] = (chunks_ref[index, rows].astype(F32) + got_ref[:count].astype(F32)).astype(BF16)
    put_squares(out_ref, square_ref[...] + get_squares(got_ref))


def end_kernel(inner, right_ref, left_ref, chunks_ref, square_ref, out_ref):
    tokens, features = out_ref.shape
    squares = square_ref[...] + get_squares(right_ref) + get_squares(left_ref)
    factor = lax.rsqrt(squares * (1.0 / inner) + 1e-05)
    factor = jnp.broadcast_to(factor, (128, tokens)).T
    for i in range(features // 128):
        span = slice(i * 128, (i + 1) * 128)
        total = chunks_ref[len(NEAR) - 1, :, span].astype(F32)
        total = total + right_ref[:tokens, span].astype(F32) + left_ref[:tokens, span].astype(F32)
        out_ref[:, span] = (total * factor).astype(BF16)


def call(kernel, ins, outs, args, scratch=(), flops=0, moved=0, limit=24):
    return pl.pallas_call(
        kernel,
        in_specs=ins,
        out_specs=[VMEM] * len(outs),
        out_shape=[jax.ShapeDtypeStruct(*o) for o in outs],
        scratch_shapes=[pltpu.VMEM(a.shape, a.dtype) for a in scratch] + [pltpu.SemaphoreType.DMA((8,))] * (HBM in ins),
        cost_estimate=pl.CostEstimate(flops=flops, bytes_accessed=moved, transcendentals=0),
        compiler_params=pltpu.CompilerParams(vmem_limit_bytes=limit * 2**20),
    )(*args)


def body(
    input_x, input_z, input_b, input_c, step_raw, doc_starts, log_rate, step_bias, skip_gain, norm_gain, out_weight
):
    tokens, channels = input_x.shape
    heads = log_rate.shape[0]
    width = channels // heads
    state_width = input_b.shape[1]
    planes = lax.axis_size("seq") // N_ROW
    in_plane = [[p * N_ROW + i for i in range(N_ROW)] for p in range(planes)]
    across = [[p * N_ROW + i for p in range(planes)] for i in range(N_ROW)]
    sent = (width + PAD, state_width)

    local = (
        log_rate.reshape(1, heads),
        step_bias.reshape(1, heads),
        step_raw.T,
        doc_starts.reshape(1, tokens),
        input_b,
        input_x,
    )
    pieces, rows, cols = call(
        state_kernel,
        [HBM] * 6,
        [((heads, *sent), BF16), ((5 * heads, tokens), F32), ((tokens, 128), F32)],
        local,
        scratch=local,
        limit=60,
        flops=2 * tokens * channels * state_width,
        moved=2 * tokens * channels,
    )
    got = lax.all_to_all(pieces, "seq", 0, 0, axis_index_groups=in_plane)
    skip = skip_gain.reshape(1, heads)
    gain = norm_gain.reshape(1, channels)
    near = (input_c, input_b, rows, cols, skip, input_x, input_z)
    own, opened, done = call(
        intra_kernel,
        [HBM] * 7,
        [((tokens, channels), F32)] * 2 + [((8, 128), F32)],
        near,
        scratch=near,
        limit=60,
        flops=2 * tokens * tokens * channels,
        moved=8 * 2**20,
    )
    (totals,) = call(plane_kernel, [ANY, VMEM], [((planes, *sent), BF16)], (done, got), moved=2**19)
    got_planes = lax.all_to_all(totals, "seq", 0, 0, axis_index_groups=across)
    plane = lax.div(lax.axis_index("seq"), N_ROW).reshape(1)
    (entries,) = call(
        entry_kernel, [SMEM, VMEM, VMEM], [((N_ROW, width, state_width), BF16)], (plane, got, got_planes), moved=2**19
    )
    needed = (input_c, own, opened, gain)
    needed = call(
        bring_kernel,
        [ANY] + [HBM] * len(needed),
        [(a.shape, a.dtype) for a in needed],
        (entries, *needed),
        moved=2**21,
        limit=48,
    )
    entries = lax.all_to_all(entries, "seq", 0, 0, axis_index_groups=in_plane)
    me = lax.axis_index("head").reshape(1)
    features = out_weight.shape[1] // N_PART
    half_sent = ((tokens // 2 + PAD, features), BF16)
    full_sent = ((tokens + PAD, features), BF16)
    scaled, squares, right, left = call(
        gate_kernel,
        [SMEM] + [VMEM] * 5 + [HBM],
        [((tokens, channels), BF16), ((1, tokens), F32), half_sent, half_sent],
        (me, entries, *needed, out_weight),
        scratch=[jax.ShapeDtypeStruct((channels, features), BF16)],
        limit=50,
        flops=2 * tokens * channels * features,
        moved=2**21,
    )
    turn = [[(i, (i + step) % N_PART) for i in range(N_PART)] for step in (1, -1)]
    right = lax.ppermute(right, "head", turn[0])
    left = lax.ppermute(left, "head", turn[1])
    (chunks,) = call(
        chunks_kernel,
        [SMEM, VMEM, HBM],
        [((len(NEAR), tokens, features), BF16)],
        (me, scaled, out_weight),
        scratch=[jax.ShapeDtypeStruct((len(NEAR), channels, features), BF16)],
        limit=50,
        flops=2 * tokens * channels * features * len(NEAR),
        moved=2**22,
    )
    for step in range(N_PART // 2 - 1):
        begin = tokens // 2 if step == 0 else 0
        (right,) = call(
            functools.partial(join_kernel, 2 * step, 0), [VMEM] * 3, [full_sent], (right, chunks, squares), moved=2**19
        )
        right = lax.ppermute(right, "head", turn[0])
        (left,) = call(
            functools.partial(join_kernel, 2 * step + 1, begin), [VMEM] * 3, [full_sent], (left, chunks, squares), moved=2**19
        )
        left = lax.ppermute(left, "head", turn[1])
    (out,) = call(
        functools.partial(end_kernel, channels * N_PART),
        [VMEM] * 4,
        [((tokens, features), BF16)],
        (right, left, chunks, squares),
        moved=2**19,
    )
    return out


def solution(mesh):
    in_specs = (
        P("seq", "head"),
        P("seq", "head"),
        P("seq", None),
        P("seq", None),
        P("seq", "head"),
        P("seq"),
        P("head"),
        P("head"),
        P("head"),
        P("head"),
        P("head", None),
    )
    out_specs = P("seq", "head")
    return jax.shard_map(body, mesh=mesh, in_specs=in_specs, out_specs=out_specs, check_vma=False)
```

```python
import functools

import jax
import jax.numpy as jnp
from jax import lax
from jax.experimental import pallas as pl
from jax.experimental.pallas import tpu as pltpu
from jax.sharding import PartitionSpec as P

SPAN = 256
N_ROW = 8
N_PART = 8
PAD = 16
F32, BF16 = (jnp.float32, jnp.bfloat16)
VMEM = pl.BlockSpec(memory_space=pltpu.VMEM)
SMEM = pl.BlockSpec(memory_space=pltpu.SMEM)
HBM = pl.BlockSpec(memory_space=pltpu.HBM)
ANY = pl.BlockSpec(memory_space=pl.ANY)


def column_of(row, shape):
    count = shape[0]
    spread = jnp.broadcast_to(row, (count, count))
    same = lax.broadcasted_iota(jnp.int32, spread.shape, 0) == lax.broadcasted_iota(jnp.int32, spread.shape, 1)
    return jnp.broadcast_to(jnp.sum(jnp.where(same, spread, 0.0), axis=1, keepdims=True), shape)


def fetch(sources, targets, sems):
    copies = [pltpu.make_async_copy(s, t, sems.at[i]) for i, (s, t) in enumerate(zip(sources, targets))]
    for copy in copies:
        copy.start()
    return copies


def running_sum(rows):
    lanes = lax.broadcasted_iota(jnp.int32, rows.shape, 1)
    step = 1
    while step < rows.shape[1]:
        rows = rows + jnp.where(lanes >= step, pltpu.roll(rows, step, 1), 0.0)
        step *= 2
    return rows


def keep_rows(keep):
    high = keep.astype(BF16).astype(F32)
    middle = (keep - high).astype(BF16).astype(F32)
    low = keep - high - middle
    rows = lax.broadcasted_iota(jnp.int32, (PAD, keep.shape[1]), 0)
    out = jnp.where(rows == 0, high, jnp.where(rows == 1, middle, jnp.where(rows == 2, low, 0.0)))
    return out.astype(BF16)


def piece(ref, index, state_rows):
    state = ref[index, :state_rows, :].astype(F32)
    keep = jnp.sum(ref[index, state_rows:, :].astype(F32), axis=0, keepdims=True)
    return state, keep


def state_kernel(*refs):
    (log_rate, bias, raw_ref, flag_ref, b_ref, x_ref) = refs[9:15]
    out_ref, rows_ref, cols_ref = refs[6:9]
    copies = fetch(refs[:6], refs[9:15], refs[15])
    for copy in copies[:4]:
        copy.wait()
    heads, tokens = raw_ref.shape
    width = x_ref.shape[1] // heads
    raw = raw_ref[...]
    dt = jax.nn.softplus(raw + column_of(bias[...], raw.shape))
    rate = -jnp.exp(column_of(log_rate[...], raw.shape))
    flags = jnp.broadcast_to(flag_ref[...].astype(F32), raw.shape)
    sums = running_sum(jnp.concatenate([rate * dt, flags], axis=0))
    running, resets = (sums[:heads], sums[heads:])
    run_last = jnp.broadcast_to(running[:, tokens - 1 :], raw.shape)
    reset_last = jnp.broadcast_to(resets[:, tokens - 1 :], raw.shape)
    weights = jnp.where(resets == reset_last, jnp.exp(run_last - running), 0.0) * dt
    opening = jnp.where(resets == 0.0, jnp.exp(running), 0.0)
    rows = jnp.concatenate([running, dt, resets, opening, weights], axis=0)
    rows_ref[...] = rows
    cols = jnp.concatenate([rows, jnp.zeros((128 - rows.shape[0], tokens), F32)], axis=0).T
    cols_ref[...] = cols
    through = jnp.where(reset_last == 0.0, jnp.exp(run_last), 0.0)
    spread = jnp.concatenate(
        [
            jnp.broadcast_to(cols[:, 4 * heads + h : 4 * heads + h + 1], (tokens, width))
            for h in range(heads)
        ],
        axis=1,
    )
    for copy in copies[4:]:
        copy.wait()
    scaled = (spread * x_ref[...].astype(F32)).astype(BF16)
    states = lax.dot_general(scaled, b_ref[...], (((0,), (0,)), ((), ())), preferred_element_type=F32)
    for h in range(heads):
        out_ref[h, :width, :] = states[h * width : (h + 1) * width].astype(BF16)
        out_ref[h, width:, :] = keep_rows(through[h : h + 1, :128])


def intra_kernel(*refs):
    own_ref, open_ref, done_ref = refs[7:10]
    c_ref, b_ref, rows_ref, cols_ref, skip_ref, x_ref, z_ref = refs[10:17]
    for copy in fetch(refs[:7], refs[10:17], refs[17]):
        copy.wait()
    done_ref[...] = jnp.zeros_like(done_ref)
    tokens = x_ref.shape[0]
    heads = skip_ref.shape[1]
    width = x_ref.shape[1] // heads
    skip = skip_ref[...]
    scores = lax.dot_general(c_ref[...], b_ref[...], (((1,), (1,)), ((), ())), preferred_element_type=F32)
    reset_row = rows_ref[2 * heads : 2 * heads + 1, :]
    reset_col = cols_ref[:, 2 * heads : 2 * heads + 1]
    later = lax.broadcasted_iota(jnp.int32, scores.shape, 0)
    earlier = lax.broadcasted_iota(jnp.int32, scores.shape, 1)
    allowed = (later >= earlier) & (reset_col == reset_row)
    scores = jnp.where(allowed, scores, 0.0)
    for h in range(heads):
        span = slice(h * width, (h + 1) * width)
        spread = cols_ref[:, h : h + 1] - rows_ref[h : h + 1, :]
        decays = jnp.exp(jnp.where(allowed, spread, 0.0))
        mixing = (scores * decays * rows_ref[heads + h : heads + h + 1, :]).astype(BF16)
        x_h = x_ref[:, span]
        out = jnp.dot(mixing, x_h, preferred_element_type=F32) + skip[:, h : h + 1] * x_h.astype(F32)
        v = z_ref[:, span].astype(F32)
        gate = v / (1.0 + jnp.exp(-v))
        own_ref[:, span] = out * gate
        open_ref[:, span] = gate * cols_ref[:, 3 * heads + h : 3 * heads + h + 1]


def plane_kernel(after_ref, got_ref, out_ref):
    count, rows, lanes = got_ref.shape
    state_rows = rows - PAD
    total, keep = piece(got_ref, 0, state_rows)
    for i in range(1, count):
        state, factor = piece(got_ref, i, state_rows)
        total = factor * total + state
        keep = keep * factor
    total, keep = (total.astype(BF16), keep_rows(keep))
    for i in range(out_ref.shape[0]):
        out_ref[i, :state_rows, :] = total
        out_ref[i, state_rows:, :] = keep


def entry_kernel(plane, got_ref, planes_ref, out_ref):
    count, rows, lanes = got_ref.shape
    state_rows = rows - PAD
    mine = plane[0]
    entry = jnp.zeros((state_rows, lanes), F32)
    for i in range(planes_ref.shape[0] - 1):
        state, factor = piece(planes_ref, i, state_rows)
        entry = jnp.where(i < mine, factor * entry + state, entry)
    out_ref[0] = entry.astype(BF16)
    for i in range(count - 1):
        state, factor = piece(got_ref, i, state_rows)
        entry = factor * entry + state
        out_ref[i + 1] = entry.astype(BF16)


def bring_kernel(*refs):
    count = len(refs) // 2 - 1
    for copy in fetch(refs[1 : count + 1], refs[count + 1 : -1], refs[-1]):
        copy.wait()


def put_squares(ref, squares):
    high = squares.astype(BF16).astype(F32)
    middle = (squares - high).astype(BF16).astype(F32)
    low = squares - high - middle
    first = jnp.concatenate([high, middle], axis=1)
    second = jnp.concatenate([low, jnp.zeros_like(low)], axis=1)
    row = lax.broadcasted_iota(jnp.int32, (PAD, ref.shape[1]), 0)
    rows = jnp.where(row == 0, first, jnp.where(row == 1, second, 0.0))
    ref[ref.shape[0] - PAD :, :] = rows.astype(BF16)


def get_squares(ref):
    rows = jnp.sum(ref[ref.shape[0] - PAD :, :].astype(F32), axis=0, keepdims=True)
    half = ref.shape[1] // 2
    return rows[:, :half] + rows[:, half:]


def columns(w_hbm, me, away, features):
    place = (me[0] + away + N_PART) % N_PART
    return w_hbm.at[:, pl.ds(pl.multiple_of(place * features, features), features)]


def project(scaled_ref, w_ref, copy):
    copy.wait()
    return jnp.dot(scaled_ref[...], w_ref[...], preferred_element_type=F32).astype(BF16)


def gate_kernel(me, entry_ref, c_ref, own_ref, open_ref, gain_ref, w_hbm, *refs):
    scaled_ref, square_ref, far_right_ref, far_left_ref, right_ref, left_ref, w_ref, sems = refs
    heads, width, lanes = entry_ref.shape
    tokens = own_ref.shape[0]
    half = tokens // 2
    away = (N_PART // 2, 3, -3)
    copies = fetch([columns(w_hbm, me, a, w_ref.shape[2]) for a in away], [w_ref.at[i] for i in range(3)], sems)
    entries = entry_ref[...].reshape(heads * width, lanes)
    carried = lax.dot_general(c_ref[...], entries, (((1,), (1,)), ((), ())), preferred_element_type=F32)
    gated = own_ref[...] + open_ref[...] * carried
    scaled_ref[...] = (gated * gain_ref[...]).astype(BF16)
    squares = jnp.sum(gated * gated, axis=1, keepdims=True)
    squares = jnp.broadcast_to(squares, (tokens, 128)).T[:1]
    square_ref[...] = squares
    first = lax.broadcasted_iota(jnp.int32, squares.shape, 1) < half
    far = project(scaled_ref, w_ref.at[0], copies[0])
    far_right_ref[:half] = far[:half]
    far_left_ref[:half] = far[half:]
    put_squares(far_right_ref, jnp.where(first, squares, 0.0))
    put_squares(far_left_ref, jnp.where(first, 0.0, squares))
    for i, ref in ((1, right_ref), (2, left_ref)):
        ref[:tokens] = project(scaled_ref, w_ref.at[i], copies[i])
        put_squares(ref, squares)


def near_kernel(me, scaled_ref, square_ref, w_hbm, right_ref, left_ref, near_ref, w_ref, sems):
    tokens, features = near_ref.shape[1:]
    copies = fetch([columns(w_hbm, me, a, features) for a in (1, -1, 2, -2, 0)], [w_ref.at[i] for i in range(5)], sems)
    for i, ref in enumerate((right_ref, left_ref)):
        ref[:tokens] = project(scaled_ref, w_ref.at[i], copies[i])
        put_squares(ref, square_ref[...])
    for i in range(2, 5):
        near_ref[i - 2] = project(scaled_ref, w_ref.at[i], copies[i])


def join_kernel(index, far_row, near_ref, square_ref, far_ref, got_ref, out_ref):
    tokens = near_ref.shape[1]
    half = tokens // 2
    for row in (0, half):
        rows = slice(row, row + half)
        total = near_ref[index, rows].astype(F32) + got_ref[rows].astype(F32)
        if row == far_row:
            total = total + far_ref[:half].astype(F32)
        out_ref[rows] = total.astype(BF16)
    put_squares(out_ref, square_ref[...] + get_squares(got_ref) + get_squares(far_ref))


def end_kernel(inner, near_ref, square_ref, *refs):
    got_refs, out_ref = refs[:-1], refs[-1]
    tokens, features = out_ref.shape
    squares = square_ref[...]
    for ref in got_refs:
        squares = squares + get_squares(ref)
    factor = lax.rsqrt(squares * (1.0 / inner) + 1e-05)
    factor = jnp.broadcast_to(factor, (128, tokens)).T
    for i in range(features // 128):
        span = slice(i * 128, (i + 1) * 128)
        total = near_ref[2, :, span].astype(F32)
        for ref in got_refs:
            total = total + ref[:tokens, span].astype(F32)
        out_ref[:, span] = (total * factor).astype(BF16)


def call(kernel, ins, outs, args, scratch=(), flops=0, moved=0, limit=24):
    return pl.pallas_call(
        kernel,
        in_specs=ins,
        out_specs=[VMEM] * len(outs),
        out_shape=[jax.ShapeDtypeStruct(*o) for o in outs],
        scratch_shapes=[pltpu.VMEM(a.shape, a.dtype) for a in scratch] + [pltpu.SemaphoreType.DMA((8,))] * (HBM in ins),
        cost_estimate=pl.CostEstimate(flops=flops, bytes_accessed=moved, transcendentals=0),
        compiler_params=pltpu.CompilerParams(vmem_limit_bytes=limit * 2**20),
    )(*args)


def body(
    input_x, input_z, input_b, input_c, step_raw, doc_starts, log_rate, step_bias, skip_gain, norm_gain, out_weight
):
    tokens, channels = input_x.shape
    heads = log_rate.shape[0]
    width = channels // heads
    state_width = input_b.shape[1]
    planes = lax.axis_size("seq") // N_ROW
    in_plane = [[p * N_ROW + i for i in range(N_ROW)] for p in range(planes)]
    across = [[p * N_ROW + i for p in range(planes)] for i in range(N_ROW)]
    sent = (width + PAD, state_width)

    local = (
        log_rate.reshape(1, heads),
        step_bias.reshape(1, heads),
        step_raw.T,
        doc_starts.reshape(1, tokens),
        input_b,
        input_x,
    )
    pieces, rows, cols = call(
        state_kernel,
        [HBM] * 6,
        [((heads, *sent), BF16), ((5 * heads, tokens), F32), ((tokens, 128), F32)],
        local,
        scratch=local,
        limit=60,
        flops=2 * tokens * channels * state_width,
        moved=2 * tokens * channels,
    )
    got = lax.all_to_all(pieces, "seq", 0, 0, axis_index_groups=in_plane)
    skip = skip_gain.reshape(1, heads)
    gain = norm_gain.reshape(1, channels)
    near = (input_c, input_b, rows, cols, skip, input_x, input_z)
    own, opened, done = call(
        intra_kernel,
        [HBM] * 7,
        [((tokens, channels), F32)] * 2 + [((8, 128), F32)],
        near,
        scratch=near,
        limit=60,
        flops=2 * tokens * tokens * channels,
        moved=8 * 2**20,
    )
    (totals,) = call(plane_kernel, [ANY, VMEM], [((planes, *sent), BF16)], (done, got), moved=2**19)
    got_planes = lax.all_to_all(totals, "seq", 0, 0, axis_index_groups=across)
    plane = lax.div(lax.axis_index("seq"), N_ROW).reshape(1)
    (entries,) = call(
        entry_kernel, [SMEM, VMEM, VMEM], [((N_ROW, width, state_width), BF16)], (plane, got, got_planes), moved=2**19
    )
    needed = (input_c, own, opened, gain)
    needed = call(
        bring_kernel,
        [ANY] + [HBM] * len(needed),
        [(a.shape, a.dtype) for a in needed],
        (entries, *needed),
        moved=2**21,
        limit=48,
    )
    entries = lax.all_to_all(entries, "seq", 0, 0, axis_index_groups=in_plane)
    me = lax.axis_index("head").reshape(1)
    features = out_weight.shape[1] // N_PART
    half_sent = ((tokens // 2 + PAD, features), BF16)
    full_sent = ((tokens + PAD, features), BF16)
    def turn(array, step):
        return lax.ppermute(array, "head", [(i, (i + step) % N_PART) for i in range(N_PART)])

    scaled, squares, far_right, far_left, right, left = call(
        gate_kernel,
        [SMEM] + [VMEM] * 5 + [HBM],
        [((tokens, channels), BF16), ((1, tokens), F32), half_sent, half_sent, full_sent, full_sent],
        (me, entries, *needed, out_weight),
        scratch=[jax.ShapeDtypeStruct((3, channels, features), BF16)],
        flops=6 * tokens * channels * features,
        moved=2**21,
        limit=50,
    )
    far_right, far_left = turn(far_right, 2), turn(far_left, -2)
    right, left = turn(right, 1), turn(left, -1)
    next_right, next_left, near = call(
        near_kernel,
        [SMEM, VMEM, VMEM, HBM],
        [full_sent, full_sent, ((3, tokens, features), BF16)],
        (me, scaled, squares, out_weight),
        scratch=[jax.ShapeDtypeStruct((5, channels, features), BF16)],
        flops=10 * tokens * channels * features,
        moved=2**22,
        limit=50,
    )
    next_right, next_left = turn(next_right, 1), turn(next_left, -1)
    (right,) = call(
        functools.partial(join_kernel, 0, 0), [VMEM] * 4, [full_sent], (near, squares, far_right, right), moved=2**20
    )
    (left,) = call(
        functools.partial(join_kernel, 1, tokens // 2), [VMEM] * 4, [full_sent], (near, squares, far_left, left), moved=2**20
    )
    right, left = turn(right, 2), turn(left, -2)
    (out,) = call(
        functools.partial(end_kernel, channels * N_PART),
        [VMEM] * 6,
        [((tokens, features), BF16)],
        (near, squares, next_right, next_left, right, left),
        moved=2**20,
    )
    return out


def solution(mesh):
    in_specs = (
        P("seq", "head"),
        P("seq", "head"),
        P("seq", None),
        P("seq", None),
        P("seq", "head"),
        P("seq"),
        P("head"),
        P("head"),
        P("head"),
        P("head"),
        P("head", None),
    )
    out_specs = P("seq", "head")
    return jax.shard_map(body, mesh=mesh, in_specs=in_specs, out_specs=out_specs, check_vma=False)
```

```python
import functools

import jax
import jax.numpy as jnp
from jax import lax
from jax.experimental import pallas as pl
from jax.experimental.pallas import tpu as pltpu
from jax.sharding import PartitionSpec as P

SPAN = 256
N_ROW = 8
N_PART = 8
PAD = 16
F32, BF16 = (jnp.float32, jnp.bfloat16)
VMEM = pl.BlockSpec(memory_space=pltpu.VMEM)
SMEM = pl.BlockSpec(memory_space=pltpu.SMEM)
HBM = pl.BlockSpec(memory_space=pltpu.HBM)
ANY = pl.BlockSpec(memory_space=pl.ANY)


def column_of(row, shape):
    count = shape[0]
    spread = jnp.broadcast_to(row, (count, count))
    same = lax.broadcasted_iota(jnp.int32, spread.shape, 0) == lax.broadcasted_iota(jnp.int32, spread.shape, 1)
    return jnp.broadcast_to(jnp.sum(jnp.where(same, spread, 0.0), axis=1, keepdims=True), shape)


def fetch(sources, targets, sems):
    copies = [pltpu.make_async_copy(s, t, sems.at[i]) for i, (s, t) in enumerate(zip(sources, targets))]
    for copy in copies:
        copy.start()
    return copies


def running_sum(rows):
    lanes = lax.broadcasted_iota(jnp.int32, rows.shape, 1)
    step = 1
    while step < rows.shape[1]:
        rows = rows + jnp.where(lanes >= step, pltpu.roll(rows, step, 1), 0.0)
        step *= 2
    return rows


def keep_rows(keep):
    high = keep.astype(BF16).astype(F32)
    middle = (keep - high).astype(BF16).astype(F32)
    low = keep - high - middle
    rows = lax.broadcasted_iota(jnp.int32, (PAD, keep.shape[1]), 0)
    out = jnp.where(rows == 0, high, jnp.where(rows == 1, middle, jnp.where(rows == 2, low, 0.0)))
    return out.astype(BF16)


def piece(ref, index, state_rows):
    state = ref[index, :state_rows, :].astype(F32)
    keep = jnp.sum(ref[index, state_rows:, :].astype(F32), axis=0, keepdims=True)
    return state, keep


def state_kernel(*refs):
    (log_rate, bias, raw_ref, flag_ref, b_ref, x_ref) = refs[9:15]
    out_ref, rows_ref, cols_ref = refs[6:9]
    copies = fetch(refs[:6], refs[9:15], refs[15])
    for copy in copies[:4]:
        copy.wait()
    heads, tokens = raw_ref.shape
    width = x_ref.shape[1] // heads
    raw = raw_ref[...]
    dt = jax.nn.softplus(raw + column_of(bias[...], raw.shape))
    rate = -jnp.exp(column_of(log_rate[...], raw.shape))
    flags = jnp.broadcast_to(flag_ref[...].astype(F32), raw.shape)
    sums = running_sum(jnp.concatenate([rate * dt, flags], axis=0))
    running, resets = (sums[:heads], sums[heads:])
    run_last = jnp.broadcast_to(running[:, tokens - 1 :], raw.shape)
    reset_last = jnp.broadcast_to(resets[:, tokens - 1 :], raw.shape)
    weights = jnp.where(resets == reset_last, jnp.exp(run_last - running), 0.0) * dt
    opening = jnp.where(resets == 0.0, jnp.exp(running), 0.0)
    rows = jnp.concatenate([running, dt, resets, opening, weights], axis=0)
    rows_ref[...] = rows
    cols = jnp.concatenate([rows, jnp.zeros((128 - rows.shape[0], tokens), F32)], axis=0).T
    cols_ref[...] = cols
    through = jnp.where(reset_last == 0.0, jnp.exp(run_last), 0.0)
    spread = jnp.concatenate(
        [
            jnp.broadcast_to(cols[:, 4 * heads + h : 4 * heads + h + 1], (tokens, width))
            for h in range(heads)
        ],
        axis=1,
    )
    for copy in copies[4:]:
        copy.wait()
    scaled = (spread * x_ref[...].astype(F32)).astype(BF16)
    states = lax.dot_general(scaled, b_ref[...], (((0,), (0,)), ((), ())), preferred_element_type=F32)
    for h in range(heads):
        out_ref[h, :width, :] = states[h * width : (h + 1) * width].astype(BF16)
        out_ref[h, width:, :] = keep_rows(through[h : h + 1, :128])


def intra_kernel(*refs):
    own_ref, open_ref = refs[8:10]
    c_ref, b_ref, rows_ref, cols_ref, skip_ref, x_ref, z_ref = refs[10:17]
    for copy in fetch(refs[1:8], refs[10:17], refs[17]):
        copy.wait()
    tokens = x_ref.shape[0]
    heads = skip_ref.shape[1]
    width = x_ref.shape[1] // heads
    skip = skip_ref[...]
    scores = lax.dot_general(c_ref[...], b_ref[...], (((1,), (1,)), ((), ())), preferred_element_type=F32)
    reset_row = rows_ref[2 * heads : 2 * heads + 1, :]
    reset_col = cols_ref[:, 2 * heads : 2 * heads + 1]
    later = lax.broadcasted_iota(jnp.int32, scores.shape, 0)
    earlier = lax.broadcasted_iota(jnp.int32, scores.shape, 1)
    allowed = (later >= earlier) & (reset_col == reset_row)
    scores = jnp.where(allowed, scores, 0.0)
    for h in range(heads):
        span = slice(h * width, (h + 1) * width)
        spread = cols_ref[:, h : h + 1] - rows_ref[h : h + 1, :]
        decays = jnp.exp(jnp.where(allowed, spread, 0.0))
        mixing = (scores * decays * rows_ref[heads + h : heads + h + 1, :]).astype(BF16)
        x_h = x_ref[:, span]
        out = jnp.dot(mixing, x_h, preferred_element_type=F32) + skip[:, h : h + 1] * x_h.astype(F32)
        v = z_ref[:, span].astype(F32)
        gate = v / (1.0 + jnp.exp(-v))
        own_ref[:, span] = out * gate
        open_ref[:, span] = gate * cols_ref[:, 3 * heads + h : 3 * heads + h + 1]


def plane_kernel(got_ref, out_ref):
    count, rows, lanes = got_ref.shape
    state_rows = rows - PAD
    total, keep = piece(got_ref, 0, state_rows)
    for i in range(1, count):
        state, factor = piece(got_ref, i, state_rows)
        total = factor * total + state
        keep = keep * factor
    total, keep = (total.astype(BF16), keep_rows(keep))
    for i in range(out_ref.shape[0]):
        out_ref[i, :state_rows, :] = total
        out_ref[i, state_rows:, :] = keep


def entry_kernel(plane, got_ref, planes_ref, out_ref):
    count, rows, lanes = got_ref.shape
    state_rows = rows - PAD
    mine = plane[0]
    entry = jnp.zeros((state_rows, lanes), F32)
    for i in range(planes_ref.shape[0] - 1):
        state, factor = piece(planes_ref, i, state_rows)
        entry = jnp.where(i < mine, factor * entry + state, entry)
    out_ref[0] = entry.astype(BF16)
    for i in range(count - 1):
        state, factor = piece(got_ref, i, state_rows)
        entry = factor * entry + state
        out_ref[i + 1] = entry.astype(BF16)


def bring_kernel(*refs):
    count = len(refs) // 2 - 1
    for copy in fetch(refs[1 : count + 1], refs[count + 1 : -1], refs[-1]):
        copy.wait()


def put_squares(ref, squares):
    high = squares.astype(BF16).astype(F32)
    middle = (squares - high).astype(BF16).astype(F32)
    low = squares - high - middle
    first = jnp.concatenate([high, middle], axis=1)
    second = jnp.concatenate([low, jnp.zeros_like(low)], axis=1)
    row = lax.broadcasted_iota(jnp.int32, (PAD, ref.shape[1]), 0)
    rows = jnp.where(row == 0, first, jnp.where(row == 1, second, 0.0))
    ref[ref.shape[0] - PAD :, :] = rows.astype(BF16)


def get_squares(ref):
    rows = jnp.sum(ref[ref.shape[0] - PAD :, :].astype(F32), axis=0, keepdims=True)
    half = ref.shape[1] // 2
    return rows[:, :half] + rows[:, half:]


def columns(w_hbm, me, away, features):
    place = (me + away + N_PART) % N_PART
    return w_hbm.at[:, pl.ds(pl.multiple_of(place * features, features), features)]


def gate_kernel(me, entry_ref, c_ref, own_ref, open_ref, gain_ref, w_hbm, gated_ref, far_ref, w_ref, sems):
    heads, width, lanes = entry_ref.shape
    tokens = own_ref.shape[0]
    (copy,) = fetch([columns(w_hbm, me[0], N_PART // 2, w_ref.shape[1])], [w_ref], sems)
    entries = entry_ref[...].reshape(heads * width, lanes)
    carried = lax.dot_general(c_ref[...], entries, (((1,), (1,)), ((), ())), preferred_element_type=F32)
    gated = own_ref[...] + open_ref[...] * carried
    scaled = (gated * gain_ref[...]).astype(BF16)
    gated_ref[:tokens] = scaled
    squares = jnp.sum(gated * gated, axis=1, keepdims=True)
    squares = jnp.broadcast_to(squares, (tokens, 128)).T[:1]
    put_squares(gated_ref, squares)
    put_squares(far_ref, squares)
    copy.wait()
    far_ref[:tokens] = jnp.dot(scaled, w_ref[...], preferred_element_type=F32).astype(BF16)


def chunks_kernel(me, way, own_ref, other_ref, w_hbm, out_ref, base_ref, w_ref, sems):
    steps, _, tokens, features = out_ref.shape
    away = [(steps - i) * way[0] for i in range(steps + 1)]
    copies = fetch([columns(w_hbm, me[0], a, features) for a in away], [w_ref.at[i] for i in range(steps + 1)], sems)
    for i in range(steps + 1):
        copies[i].wait()
        for j, ref in enumerate((own_ref, other_ref)):
            if i < steps:
                out_ref[i, j] = jnp.dot(ref[:tokens], w_ref[i], preferred_element_type=F32).astype(BF16)
            elif j == 0:
                base_ref[...] = jnp.dot(ref[:tokens], w_ref[i], preferred_element_type=F32).astype(BF16)


def join_kernel(index, chunks_ref, own_ref, other_ref, got_ref, *out_refs):
    tokens = chunks_ref.shape[2]
    for j, ref in enumerate((own_ref, other_ref)):
        out = out_refs[0].at[j] if len(out_refs) == 1 else out_refs[j]
        squares = get_squares(ref)
        total = chunks_ref[index, j]
        if len(got_ref.shape) == 3 or j == 0:
            got = got_ref.at[j] if len(got_ref.shape) == 3 else got_ref
            squares = squares + get_squares(got)
            total = (total.astype(F32) + got[:tokens].astype(F32)).astype(BF16)
        out[:tokens] = total
        put_squares(out, squares)


def end_kernel(inner, base_ref, own_ref, right_ref, left_ref, out_ref):
    tokens, features = out_ref.shape
    squares = get_squares(own_ref) + get_squares(right_ref) + get_squares(left_ref)
    factor = lax.rsqrt(squares * (1.0 / inner) + 1e-05)
    factor = jnp.broadcast_to(factor, (128, tokens)).T
    for i in range(features // 128):
        span = slice(i * 128, (i + 1) * 128)
        total = base_ref[:, span].astype(F32)
        total = total + right_ref[:tokens, span].astype(F32) + left_ref[:tokens, span].astype(F32)
        out_ref[:, span] = (total * factor).astype(BF16)


def call(kernel, ins, outs, args, scratch=(), flops=0, moved=0, limit=24):
    return pl.pallas_call(
        kernel,
        in_specs=ins,
        out_specs=[VMEM] * len(outs),
        out_shape=[jax.ShapeDtypeStruct(*o) for o in outs],
        scratch_shapes=[pltpu.VMEM(a.shape, a.dtype) for a in scratch] + [pltpu.SemaphoreType.DMA((8,))] * (HBM in ins),
        cost_estimate=pl.CostEstimate(flops=flops, bytes_accessed=moved, transcendentals=0),
        compiler_params=pltpu.CompilerParams(vmem_limit_bytes=limit * 2**20),
    )(*args)


def body(
    input_x, input_z, input_b, input_c, step_raw, doc_starts, log_rate, step_bias, skip_gain, norm_gain, out_weight
):
    tokens, channels = input_x.shape
    heads = log_rate.shape[0]
    width = channels // heads
    state_width = input_b.shape[1]
    devices = lax.axis_size("seq")
    planes = devices // N_ROW
    in_plane = [[p * N_ROW + i for i in range(N_ROW)] for p in range(planes)]
    across = [[p * N_ROW + i for p in range(planes)] for i in range(N_ROW)]
    sent = (width + PAD, state_width)

    local = (
        log_rate.reshape(1, heads),
        step_bias.reshape(1, heads),
        step_raw.T,
        doc_starts.reshape(1, tokens),
        input_b,
        input_x,
    )
    pieces, rows, cols = call(
        state_kernel,
        [HBM] * 6,
        [((heads, *sent), BF16), ((5 * heads, tokens), F32), ((tokens, 128), F32)],
        local,
        scratch=local,
        limit=60,
        flops=2 * tokens * channels * state_width,
        moved=2 * tokens * channels,
    )
    got = lax.all_to_all(pieces, "seq", 0, 0, axis_index_groups=in_plane)
    skip = skip_gain.reshape(1, heads)
    gain = norm_gain.reshape(1, channels)
    (totals,) = call(plane_kernel, [VMEM], [((planes, *sent), BF16)], (got,), moved=2**19)
    near = (input_c, input_b, rows, cols, skip, input_x, input_z)
    own, opened = call(
        intra_kernel,
        [ANY] + [HBM] * 7,
        [((tokens, channels), F32)] * 2,
        (totals, *near),
        scratch=near,
        limit=60,
        flops=2 * tokens * tokens * channels,
        moved=8 * 2**20,
    )
    got_planes = lax.all_to_all(totals, "seq", 0, 0, axis_index_groups=across)
    got_planes, own = lax.optimization_barrier((got_planes, own))
    plane = lax.div(lax.axis_index("seq"), N_ROW).reshape(1)
    (entries,) = call(
        entry_kernel, [SMEM, VMEM, VMEM], [((N_ROW, width, state_width), BF16)], (plane, got, got_planes), moved=2**19
    )
    needed = (input_c, own, opened, gain)
    needed = call(
        bring_kernel,
        [ANY] + [HBM] * len(needed),
        [(a.shape, a.dtype) for a in needed],
        (entries, *needed),
        moved=2**21,
        limit=48,
    )
    entries = lax.all_to_all(entries, "seq", 0, 0, axis_index_groups=in_plane)
    me = lax.axis_index("head").reshape(1)
    features = out_weight.shape[1] // N_PART
    slab = ((tokens + PAD, features), BF16)
    slabs = ((2, tokens + PAD, features), BF16)
    way = (1 - 2 * lax.rem(lax.axis_index("seq"), 2)).reshape(1)

    def send(array, steps, swap):
        pairs = []
        for seq in range(devices):
            for head in range(N_PART):
                there = (head + steps * (1 - 2 * (seq % 2))) % N_PART
                pairs.append((seq * N_PART + head, (seq ^ swap) * N_PART + there))
        return lax.ppermute(array, ("seq", "head"), pairs)

    gated, far = call(
        gate_kernel,
        [SMEM] + [VMEM] * 5 + [HBM],
        [slab, slab],
        (me, entries, *needed, out_weight),
        scratch=[jax.ShapeDtypeStruct((channels, features), BF16)],
        flops=2 * tokens * channels * features,
        moved=2**21,
        limit=50,
    )
    other = send(gated, 0, 1)
    flow = send(far, 1, 0)
    steps = N_PART // 2 - 1
    chunks, base = call(
        chunks_kernel,
        [SMEM, SMEM, VMEM, VMEM, HBM],
        [((steps, 2, tokens, features), BF16), ((tokens, features), BF16)],
        (me, way, gated, other, out_weight),
        scratch=[jax.ShapeDtypeStruct((steps + 1, channels, features), BF16)],
        flops=14 * tokens * channels * features,
        moved=2**22,
        limit=50,
    )
    for step in range(steps):
        flow = call(
            functools.partial(join_kernel, step),
            [VMEM] * 4,
            [slabs] if step < steps - 1 else [slab, slab],
            (chunks, gated, other, flow),
            moved=2**20,
        )
        if step < steps - 1:
            flow = send(flow[0], 1, 0)
    (out,) = call(
        functools.partial(end_kernel, channels * N_PART),
        [VMEM] * 4,
        [((tokens, features), BF16)],
        (base, gated, send(flow[0], 1, 0), send(flow[1], 1, 1)),
        moved=2**20,
    )
    return out


def solution(mesh):
    in_specs = (
        P("seq", "head"),
        P("seq", "head"),
        P("seq", None),
        P("seq", None),
        P("seq", "head"),
        P("seq"),
        P("head"),
        P("head"),
        P("head"),
        P("head"),
        P("head", None),
    )
    out_specs = P("seq", "head")
    return jax.shard_map(body, mesh=mesh, in_specs=in_specs, out_specs=out_specs, check_vma=False)
```

```python
import functools

import jax
import jax.numpy as jnp
from jax import lax
from jax.experimental import pallas as pl
from jax.experimental.pallas import tpu as pltpu
from jax.sharding import PartitionSpec as P

SPAN = 256
N_ROW = 8
N_PART = 8
PAD = 16
F32, BF16 = (jnp.float32, jnp.bfloat16)
VMEM = pl.BlockSpec(memory_space=pltpu.VMEM)
SMEM = pl.BlockSpec(memory_space=pltpu.SMEM)
HBM = pl.BlockSpec(memory_space=pltpu.HBM)
ANY = pl.BlockSpec(memory_space=pl.ANY)


def column_of(row, shape):
    count = shape[0]
    spread = jnp.broadcast_to(row, (count, count))
    same = lax.broadcasted_iota(jnp.int32, spread.shape, 0) == lax.broadcasted_iota(jnp.int32, spread.shape, 1)
    return jnp.broadcast_to(jnp.sum(jnp.where(same, spread, 0.0), axis=1, keepdims=True), shape)


def fetch(sources, targets, sems):
    copies = [pltpu.make_async_copy(s, t, sems.at[i]) for i, (s, t) in enumerate(zip(sources, targets))]
    for copy in copies:
        copy.start()
    return copies


def running_sum(rows):
    lanes = lax.broadcasted_iota(jnp.int32, rows.shape, 1)
    step = 1
    while step < rows.shape[1]:
        rows = rows + jnp.where(lanes >= step, pltpu.roll(rows, step, 1), 0.0)
        step *= 2
    return rows


def keep_rows(keep):
    high = keep.astype(BF16).astype(F32)
    middle = (keep - high).astype(BF16).astype(F32)
    low = keep - high - middle
    rows = lax.broadcasted_iota(jnp.int32, (PAD, keep.shape[1]), 0)
    out = jnp.where(rows == 0, high, jnp.where(rows == 1, middle, jnp.where(rows == 2, low, 0.0)))
    return out.astype(BF16)


def piece(ref, index, state_rows):
    state = ref[index, :state_rows, :].astype(F32)
    keep = jnp.sum(ref[index, state_rows:, :].astype(F32), axis=0, keepdims=True)
    return state, keep


def state_kernel(*refs):
    (log_rate, bias, raw_ref, flag_ref, b_ref, x_ref) = refs[9:15]
    out_ref, rows_ref, cols_ref = refs[6:9]
    copies = fetch(refs[:6], refs[9:15], refs[15])
    for copy in copies[:4]:
        copy.wait()
    heads, tokens = raw_ref.shape
    width = x_ref.shape[1] // heads
    raw = raw_ref[...]
    dt = jax.nn.softplus(raw + column_of(bias[...], raw.shape))
    rate = -jnp.exp(column_of(log_rate[...], raw.shape))
    flags = jnp.broadcast_to(flag_ref[...].astype(F32), raw.shape)
    sums = running_sum(jnp.concatenate([rate * dt, flags], axis=0))
    running, resets = (sums[:heads], sums[heads:])
    run_last = jnp.broadcast_to(running[:, tokens - 1 :], raw.shape)
    reset_last = jnp.broadcast_to(resets[:, tokens - 1 :], raw.shape)
    weights = jnp.where(resets == reset_last, jnp.exp(run_last - running), 0.0) * dt
    opening = jnp.where(resets == 0.0, jnp.exp(running), 0.0)
    rows = jnp.concatenate([running, dt, resets, opening, weights], axis=0)
    rows_ref[...] = rows
    cols = jnp.concatenate([rows, jnp.zeros((128 - rows.shape[0], tokens), F32)], axis=0).T
    cols_ref[...] = cols
    through = jnp.where(reset_last == 0.0, jnp.exp(run_last), 0.0)
    spread = jnp.concatenate(
        [
            jnp.broadcast_to(cols[:, 4 * heads + h : 4 * heads + h + 1], (tokens, width))
            for h in range(heads)
        ],
        axis=1,
    )
    for copy in copies[4:]:
        copy.wait()
    scaled = (spread * x_ref[...].astype(F32)).astype(BF16)
    states = lax.dot_general(scaled, b_ref[...], (((0,), (0,)), ((), ())), preferred_element_type=F32)
    for h in range(heads):
        out_ref[h, :width, :] = states[h * width : (h + 1) * width].astype(BF16)
        out_ref[h, width:, :] = keep_rows(through[h : h + 1, :128])


def intra_kernel(*refs):
    own_ref, open_ref = refs[8:10]
    c_ref, b_ref, rows_ref, cols_ref, skip_ref, x_ref, z_ref = refs[10:17]
    for copy in fetch(refs[1:8], refs[10:17], refs[17]):
        copy.wait()
    tokens = x_ref.shape[0]
    heads = skip_ref.shape[1]
    width = x_ref.shape[1] // heads
    skip = skip_ref[...]
    scores = lax.dot_general(c_ref[...], b_ref[...], (((1,), (1,)), ((), ())), preferred_element_type=F32)
    reset_row = rows_ref[2 * heads : 2 * heads + 1, :]
    reset_col = cols_ref[:, 2 * heads : 2 * heads + 1]
    later = lax.broadcasted_iota(jnp.int32, scores.shape, 0)
    earlier = lax.broadcasted_iota(jnp.int32, scores.shape, 1)
    allowed = (later >= earlier) & (reset_col == reset_row)
    scores = jnp.where(allowed, scores, 0.0)
    for h in range(heads):
        span = slice(h * width, (h + 1) * width)
        spread = cols_ref[:, h : h + 1] - rows_ref[h : h + 1, :]
        decays = jnp.exp(jnp.where(allowed, spread, 0.0))
        mixing = (scores * decays * rows_ref[heads + h : heads + h + 1, :]).astype(BF16)
        x_h = x_ref[:, span]
        out = jnp.dot(mixing, x_h, preferred_element_type=F32) + skip[:, h : h + 1] * x_h.astype(F32)
        v = z_ref[:, span].astype(F32)
        gate = v / (1.0 + jnp.exp(-v))
        own_ref[:, span] = out * gate
        open_ref[:, span] = gate * cols_ref[:, 3 * heads + h : 3 * heads + h + 1]


def plane_kernel(got_ref, out_ref):
    count, rows, lanes = got_ref.shape
    state_rows = rows - PAD
    total, keep = piece(got_ref, 0, state_rows)
    for i in range(1, count):
        state, factor = piece(got_ref, i, state_rows)
        total = factor * total + state
        keep = keep * factor
    total, keep = (total.astype(BF16), keep_rows(keep))
    for i in range(out_ref.shape[0]):
        out_ref[i, :state_rows, :] = total
        out_ref[i, state_rows:, :] = keep


def entry_kernel(plane, got_ref, planes_ref, out_ref):
    count, rows, lanes = got_ref.shape
    state_rows = rows - PAD
    mine = plane[0]
    entry = jnp.zeros((state_rows, lanes), F32)
    for i in range(planes_ref.shape[0] - 1):
        state, factor = piece(planes_ref, i, state_rows)
        entry = jnp.where(i < mine, factor * entry + state, entry)
    out_ref[0] = entry.astype(BF16)
    for i in range(count - 1):
        state, factor = piece(got_ref, i, state_rows)
        entry = factor * entry + state
        out_ref[i + 1] = entry.astype(BF16)


def bring_kernel(*refs):
    count = len(refs) // 2 - 1
    for copy in fetch(refs[1 : count + 1], refs[count + 1 : -1], refs[-1]):
        copy.wait()


def put_squares(ref, squares):
    high = squares.astype(BF16).astype(F32)
    middle = (squares - high).astype(BF16).astype(F32)
    low = squares - high - middle
    first = jnp.concatenate([high, middle], axis=1)
    second = jnp.concatenate([low, jnp.zeros_like(low)], axis=1)
    row = lax.broadcasted_iota(jnp.int32, (PAD, ref.shape[1]), 0)
    rows = jnp.where(row == 0, first, jnp.where(row == 1, second, 0.0))
    ref[ref.shape[0] - PAD :, :] = rows.astype(BF16)


def get_squares(ref):
    rows = jnp.sum(ref[ref.shape[0] - PAD :, :].astype(F32), axis=0, keepdims=True)
    half = ref.shape[1] // 2
    return rows[:, :half] + rows[:, half:]


def columns(w_hbm, me, away, features):
    place = (me + away + N_PART) % N_PART
    return w_hbm.at[:, pl.ds(pl.multiple_of(place * features, features), features)]


def gate_kernel(me, entry_ref, c_ref, own_ref, open_ref, gain_ref, w_hbm, gated_ref, far_ref, w_ref, sems):
    heads, width, lanes = entry_ref.shape
    tokens = own_ref.shape[0]
    (copy,) = fetch([columns(w_hbm, me[0], N_PART // 2, w_ref.shape[1])], [w_ref], sems)
    entries = entry_ref[...].reshape(heads * width, lanes)
    carried = lax.dot_general(c_ref[...], entries, (((1,), (1,)), ((), ())), preferred_element_type=F32)
    gated = own_ref[...] + open_ref[...] * carried
    scaled = (gated * gain_ref[...]).astype(BF16)
    gated_ref[:tokens] = scaled
    squares = jnp.sum(gated * gated, axis=1, keepdims=True)
    squares = jnp.broadcast_to(squares, (tokens, 128)).T[:1]
    put_squares(gated_ref, squares)
    put_squares(far_ref, squares)
    copy.wait()
    far_ref[:tokens] = jnp.dot(scaled, w_ref[...], preferred_element_type=F32).astype(BF16)


def chunks_kernel(me, way, own_ref, other_ref, w_hbm, out_ref, base_ref, w_ref, sems):
    steps, _, tokens, features = out_ref.shape
    away = [(steps - i) * way[0] for i in range(steps + 1)]
    copies = fetch([columns(w_hbm, me[0], a, features) for a in away], [w_ref.at[i] for i in range(steps + 1)], sems)
    for i in range(steps + 1):
        copies[i].wait()
        for j, ref in enumerate((own_ref, other_ref)):
            if i < steps:
                out_ref[i, j] = jnp.dot(ref[:tokens], w_ref[i], preferred_element_type=F32).astype(BF16)
            elif j == 0:
                base_ref[...] = jnp.dot(ref[:tokens], w_ref[i], preferred_element_type=F32).astype(BF16)


def join_kernel(index, slab, chunks_ref, gated_ref, *refs):
    got_refs, out_ref = refs[:-1], refs[-1]
    tokens = chunks_ref.shape[2]
    squares = get_squares(gated_ref)
    total = chunks_ref[index, slab].astype(F32)
    for ref in got_refs:
        squares = squares + get_squares(ref)
        total = total + ref[:tokens].astype(F32)
    out_ref[:tokens] = total.astype(BF16)
    put_squares(out_ref, squares)


def end_kernel(inner, base_ref, own_ref, right_ref, left_ref, out_ref):
    tokens, features = out_ref.shape
    squares = get_squares(own_ref) + get_squares(right_ref) + get_squares(left_ref)
    factor = lax.rsqrt(squares * (1.0 / inner) + 1e-05)
    factor = jnp.broadcast_to(factor, (128, tokens)).T
    for i in range(features // 128):
        span = slice(i * 128, (i + 1) * 128)
        total = base_ref[:, span].astype(F32)
        total = total + right_ref[:tokens, span].astype(F32) + left_ref[:tokens, span].astype(F32)
        out_ref[:, span] = (total * factor).astype(BF16)


def call(kernel, ins, outs, args, scratch=(), flops=0, moved=0, limit=24):
    return pl.pallas_call(
        kernel,
        in_specs=ins,
        out_specs=[VMEM] * len(outs),
        out_shape=[jax.ShapeDtypeStruct(*o) for o in outs],
        scratch_shapes=[pltpu.VMEM(a.shape, a.dtype) for a in scratch] + [pltpu.SemaphoreType.DMA((8,))] * (HBM in ins),
        cost_estimate=pl.CostEstimate(flops=flops, bytes_accessed=moved, transcendentals=0),
        compiler_params=pltpu.CompilerParams(vmem_limit_bytes=limit * 2**20),
    )(*args)


def body(
    input_x, input_z, input_b, input_c, step_raw, doc_starts, log_rate, step_bias, skip_gain, norm_gain, out_weight
):
    tokens, channels = input_x.shape
    heads = log_rate.shape[0]
    width = channels // heads
    state_width = input_b.shape[1]
    devices = lax.axis_size("seq")
    planes = devices // N_ROW
    in_plane = [[p * N_ROW + i for i in range(N_ROW)] for p in range(planes)]
    across = [[p * N_ROW + i for p in range(planes)] for i in range(N_ROW)]
    sent = (width + PAD, state_width)

    local = (
        log_rate.reshape(1, heads),
        step_bias.reshape(1, heads),
        step_raw.T,
        doc_starts.reshape(1, tokens),
        input_b,
        input_x,
    )
    pieces, rows, cols = call(
        state_kernel,
        [HBM] * 6,
        [((heads, *sent), BF16), ((5 * heads, tokens), F32), ((tokens, 128), F32)],
        local,
        scratch=local,
        limit=60,
        flops=2 * tokens * channels * state_width,
        moved=2 * tokens * channels,
    )
    got = lax.all_to_all(pieces, "seq", 0, 0, axis_index_groups=in_plane)
    skip = skip_gain.reshape(1, heads)
    gain = norm_gain.reshape(1, channels)
    (totals,) = call(plane_kernel, [VMEM], [((planes, *sent), BF16)], (got,), moved=2**19)
    near = (input_c, input_b, rows, cols, skip, input_x, input_z)
    own, opened = call(
        intra_kernel,
        [ANY] + [HBM] * 7,
        [((tokens, channels), F32)] * 2,
        (totals, *near),
        scratch=near,
        limit=60,
        flops=2 * tokens * tokens * channels,
        moved=8 * 2**20,
    )
    got_planes = lax.all_to_all(totals, "seq", 0, 0, axis_index_groups=across)
    got_planes, own = lax.optimization_barrier((got_planes, own))
    plane = lax.div(lax.axis_index("seq"), N_ROW).reshape(1)
    (entries,) = call(
        entry_kernel, [SMEM, VMEM, VMEM], [((N_ROW, width, state_width), BF16)], (plane, got, got_planes), moved=2**19
    )
    needed = (input_c, own, opened, gain)
    needed = call(
        bring_kernel,
        [ANY] + [HBM] * len(needed),
        [(a.shape, a.dtype) for a in needed],
        (entries, *needed),
        moved=2**21,
        limit=48,
    )
    entries = lax.all_to_all(entries, "seq", 0, 0, axis_index_groups=in_plane)
    me = lax.axis_index("head").reshape(1)
    features = out_weight.shape[1] // N_PART
    slab = ((tokens + PAD, features), BF16)
    way = (1 - 2 * lax.rem(lax.axis_index("seq"), 2)).reshape(1)

    def send(array, steps, swap):
        pairs = []
        for seq in range(devices):
            for head in range(N_PART):
                there = (head + steps * (1 - 2 * (seq % 2))) % N_PART
                pairs.append((seq * N_PART + head, (seq ^ swap) * N_PART + there))
        return lax.ppermute(array, ("seq", "head"), pairs)

    gated, far = call(
        gate_kernel,
        [SMEM] + [VMEM] * 5 + [HBM],
        [slab, slab],
        (me, entries, *needed, out_weight),
        scratch=[jax.ShapeDtypeStruct((channels, features), BF16)],
        flops=2 * tokens * channels * features,
        moved=2**21,
        limit=50,
    )
    other = send(gated, 0, 1)
    flow = send(far, 1, 0)
    steps = N_PART // 2 - 1
    chunks, base = call(
        chunks_kernel,
        [SMEM, SMEM, VMEM, VMEM, HBM],
        [((steps, 2, tokens, features), BF16), ((tokens, features), BF16)],
        (me, way, gated, other, out_weight),
        scratch=[jax.ShapeDtypeStruct((steps + 1, channels, features), BF16)],
        flops=14 * tokens * channels * features,
        moved=2**22,
        limit=50,
    )
    flows = [[flow], []]
    for step in range(steps):
        for slab_index in (1, 0):
            got = flows[slab_index]
            (joined,) = call(
                functools.partial(join_kernel, step, slab_index),
                [VMEM] * (2 + len(got)),
                [slab],
                (chunks, (gated, other)[slab_index], *got),
                moved=2**19,
            )
            flows[slab_index] = [send(joined, 1, slab_index if step == steps - 1 else 0)]
    (out,) = call(
        functools.partial(end_kernel, channels * N_PART),
        [VMEM] * 4,
        [((tokens, features), BF16)],
        (base, gated, *flows[0], *flows[1]),
        moved=2**20,
    )
    return out


def solution(mesh):
    in_specs = (
        P("seq", "head"),
        P("seq", "head"),
        P("seq", None),
        P("seq", None),
        P("seq", "head"),
        P("seq"),
        P("head"),
        P("head"),
        P("head"),
        P("head"),
        P("head", None),
    )
    out_specs = P("seq", "head")
    return jax.shard_map(body, mesh=mesh, in_specs=in_specs, out_specs=out_specs, check_vma=False)
```

```python
import functools

import jax
import jax.numpy as jnp
from jax import lax
from jax.experimental import pallas as pl
from jax.experimental.pallas import tpu as pltpu
from jax.sharding import PartitionSpec as P

SPAN = 256
N_ROW = 8
N_PART = 8
PAD = 16
F32, BF16 = (jnp.float32, jnp.bfloat16)
VMEM = pl.BlockSpec(memory_space=pltpu.VMEM)
SMEM = pl.BlockSpec(memory_space=pltpu.SMEM)
HBM = pl.BlockSpec(memory_space=pltpu.HBM)
ANY = pl.BlockSpec(memory_space=pl.ANY)


def column_of(row, shape):
    count = shape[0]
    spread = jnp.broadcast_to(row, (count, count))
    same = lax.broadcasted_iota(jnp.int32, spread.shape, 0) == lax.broadcasted_iota(jnp.int32, spread.shape, 1)
    return jnp.broadcast_to(jnp.sum(jnp.where(same, spread, 0.0), axis=1, keepdims=True), shape)


def fetch(sources, targets, sems):
    copies = [pltpu.make_async_copy(s, t, sems.at[i]) for i, (s, t) in enumerate(zip(sources, targets))]
    for copy in copies:
        copy.start()
    return copies


def running_sum(rows):
    lanes = lax.broadcasted_iota(jnp.int32, rows.shape, 1)
    step = 1
    while step < rows.shape[1]:
        rows = rows + jnp.where(lanes >= step, pltpu.roll(rows, step, 1), 0.0)
        step *= 2
    return rows


def keep_rows(keep):
    high = keep.astype(BF16).astype(F32)
    middle = (keep - high).astype(BF16).astype(F32)
    low = keep - high - middle
    rows = lax.broadcasted_iota(jnp.int32, (PAD, keep.shape[1]), 0)
    out = jnp.where(rows == 0, high, jnp.where(rows == 1, middle, jnp.where(rows == 2, low, 0.0)))
    return out.astype(BF16)


def piece(ref, index, state_rows):
    state = ref[index, :state_rows, :].astype(F32)
    keep = jnp.sum(ref[index, state_rows:, :].astype(F32), axis=0, keepdims=True)
    return state, keep


def state_kernel(*refs):
    (log_rate, bias, raw_ref, flag_ref, b_ref, x_ref) = refs[9:15]
    out_ref, rows_ref, cols_ref = refs[6:9]
    copies = fetch(refs[:6], refs[9:15], refs[15])
    for copy in copies[:4]:
        copy.wait()
    heads, tokens = raw_ref.shape
    width = x_ref.shape[1] // heads
    raw = raw_ref[...]
    dt = jax.nn.softplus(raw + column_of(bias[...], raw.shape))
    rate = -jnp.exp(column_of(log_rate[...], raw.shape))
    flags = jnp.broadcast_to(flag_ref[...].astype(F32), raw.shape)
    sums = running_sum(jnp.concatenate([rate * dt, flags], axis=0))
    running, resets = (sums[:heads], sums[heads:])
    run_last = jnp.broadcast_to(running[:, tokens - 1 :], raw.shape)
    reset_last = jnp.broadcast_to(resets[:, tokens - 1 :], raw.shape)
    weights = jnp.where(resets == reset_last, jnp.exp(run_last - running), 0.0) * dt
    opening = jnp.where(resets == 0.0, jnp.exp(running), 0.0)
    rows = jnp.concatenate([running, dt, resets, opening, weights], axis=0)
    rows_ref[...] = rows
    cols = jnp.concatenate([rows, jnp.zeros((128 - rows.shape[0], tokens), F32)], axis=0).T
    cols_ref[...] = cols
    through = jnp.where(reset_last == 0.0, jnp.exp(run_last), 0.0)
    spread = jnp.concatenate(
        [
            jnp.broadcast_to(cols[:, 4 * heads + h : 4 * heads + h + 1], (tokens, width))
            for h in range(heads)
        ],
        axis=1,
    )
    for copy in copies[4:]:
        copy.wait()
    scaled = (spread * x_ref[...].astype(F32)).astype(BF16)
    states = lax.dot_general(scaled, b_ref[...], (((0,), (0,)), ((), ())), preferred_element_type=F32)
    for h in range(heads):
        out_ref[h, :width, :] = states[h * width : (h + 1) * width].astype(BF16)
        out_ref[h, width:, :] = keep_rows(through[h : h + 1, :128])


def intra_kernel(*refs):
    own_ref, open_ref = refs[8:10]
    c_ref, b_ref, rows_ref, cols_ref, skip_ref, x_ref, z_ref = refs[10:17]
    for copy in fetch(refs[1:8], refs[10:17], refs[17]):
        copy.wait()
    tokens = x_ref.shape[0]
    heads = skip_ref.shape[1]
    width = x_ref.shape[1] // heads
    skip = skip_ref[...]
    scores = lax.dot_general(c_ref[...], b_ref[...], (((1,), (1,)), ((), ())), preferred_element_type=F32)
    reset_row = rows_ref[2 * heads : 2 * heads + 1, :]
    reset_col = cols_ref[:, 2 * heads : 2 * heads + 1]
    later = lax.broadcasted_iota(jnp.int32, scores.shape, 0)
    earlier = lax.broadcasted_iota(jnp.int32, scores.shape, 1)
    allowed = (later >= earlier) & (reset_col == reset_row)
    scores = jnp.where(allowed, scores, 0.0)
    for h in range(heads):
        span = slice(h * width, (h + 1) * width)
        spread = cols_ref[:, h : h + 1] - rows_ref[h : h + 1, :]
        decays = jnp.exp(jnp.where(allowed, spread, 0.0))
        mixing = (scores * decays * rows_ref[heads + h : heads + h + 1, :]).astype(BF16)
        x_h = x_ref[:, span]
        out = jnp.dot(mixing, x_h, preferred_element_type=F32) + skip[:, h : h + 1] * x_h.astype(F32)
        v = z_ref[:, span].astype(F32)
        gate = v / (1.0 + jnp.exp(-v))
        own_ref[:, span] = out * gate
        open_ref[:, span] = gate * cols_ref[:, 3 * heads + h : 3 * heads + h + 1]


def plane_kernel(got_ref, out_ref):
    count, rows, lanes = got_ref.shape
    state_rows = rows - PAD
    total, keep = piece(got_ref, 0, state_rows)
    for i in range(1, count):
        state, factor = piece(got_ref, i, state_rows)
        total = factor * total + state
        keep = keep * factor
    total, keep = (total.astype(BF16), keep_rows(keep))
    for i in range(out_ref.shape[0]):
        out_ref[i, :state_rows, :] = total
        out_ref[i, state_rows:, :] = keep


def entry_kernel(plane, got_ref, planes_ref, out_ref):
    count, rows, lanes = got_ref.shape
    state_rows = rows - PAD
    mine = plane[0]
    entry = jnp.zeros((state_rows, lanes), F32)
    for i in range(planes_ref.shape[0] - 1):
        state, factor = piece(planes_ref, i, state_rows)
        entry = jnp.where(i < mine, factor * entry + state, entry)
    out_ref[0] = entry.astype(BF16)
    for i in range(count - 1):
        state, factor = piece(got_ref, i, state_rows)
        entry = factor * entry + state
        out_ref[i + 1] = entry.astype(BF16)


def bring_kernel(*refs):
    count = len(refs) // 2 - 1
    for copy in fetch(refs[1 : count + 1], refs[count + 1 : -1], refs[-1]):
        copy.wait()


def put_squares(ref, squares):
    high = squares.astype(BF16).astype(F32)
    middle = (squares - high).astype(BF16).astype(F32)
    low = squares - high - middle
    first = jnp.concatenate([high, middle], axis=1)
    second = jnp.concatenate([low, jnp.zeros_like(low)], axis=1)
    row = lax.broadcasted_iota(jnp.int32, (PAD, ref.shape[1]), 0)
    rows = jnp.where(row == 0, first, jnp.where(row == 1, second, 0.0))
    ref[ref.shape[0] - PAD :, :] = rows.astype(BF16)


def get_squares(ref):
    rows = jnp.sum(ref[ref.shape[0] - PAD :, :].astype(F32), axis=0, keepdims=True)
    half = ref.shape[1] // 2
    return rows[:, :half] + rows[:, half:]


def columns(w_hbm, me, away, features):
    place = (me + away + N_PART) % N_PART
    return w_hbm.at[:, pl.ds(pl.multiple_of(place * features, features), features)]


def put_halves(refs, total, squares):
    half = total.shape[0] // 2
    first = lax.broadcasted_iota(jnp.int32, squares.shape, 1) < half
    for i, ref in enumerate(refs):
        ref[:half] = total[i * half : (i + 1) * half]
        put_squares(ref, jnp.where(first == (i == 0), squares, 0.0))


def gate_kernel(me, way, entry_ref, c_ref, own_ref, open_ref, gain_ref, w_hbm, gated_ref, *refs):
    next_ref, w_ref, sems = refs[2:]
    heads, width, lanes = entry_ref.shape
    tokens = own_ref.shape[0]
    features = w_ref.shape[1]
    wanted = [columns(w_hbm, me[0], away, features) for away in (N_PART // 2, (N_PART // 2 - 1) * way[0])]
    copies = fetch(wanted, [w_ref, next_ref], sems)
    entries = entry_ref[...].reshape(heads * width, lanes)
    carried = lax.dot_general(c_ref[...], entries, (((1,), (1,)), ((), ())), preferred_element_type=F32)
    gated = own_ref[...] + open_ref[...] * carried
    scaled = (gated * gain_ref[...]).astype(BF16)
    gated_ref[:tokens] = scaled
    squares = jnp.sum(gated * gated, axis=1, keepdims=True)
    squares = jnp.broadcast_to(squares, (tokens, 128)).T[:1]
    put_squares(gated_ref, squares)
    copies[0].wait()
    put_halves(refs[:2], jnp.dot(scaled, w_ref[...], preferred_element_type=F32).astype(BF16), squares)
    copies[1].wait()


def begin_kernel(own_ref, other_ref, w_ref, chunk_ref, out_ref):
    tokens = chunk_ref.shape[0]
    out_ref[:tokens] = jnp.dot(other_ref[:tokens], w_ref[...], preferred_element_type=F32).astype(BF16)
    out_ref[tokens:] = other_ref[tokens:]
    chunk_ref[...] = jnp.dot(own_ref[:tokens], w_ref[...], preferred_element_type=F32).astype(BF16)


def chunks_kernel(me, way, own_ref, other_ref, w_hbm, out_ref, base_ref, w_ref, sems):
    steps, _, tokens, features = out_ref.shape
    order = [*range(steps, 0, -1), 0]
    copies = fetch([columns(w_hbm, me[0], a * way[0], features) for a in order], [w_ref.at[a] for a in order], sems)
    for a, copy in zip(order, copies):
        copy.wait()
        if a == 0:
            base_ref[...] = jnp.dot(own_ref[:tokens], w_ref[a], preferred_element_type=F32).astype(BF16)
        else:
            for j, ref in enumerate((own_ref, other_ref)):
                out_ref[a - 1, j] = jnp.dot(ref[:tokens], w_ref[a], preferred_element_type=F32).astype(BF16)


def join_kernel(place, chunks_ref, gated_ref, *refs):
    tokens = gated_ref.shape[0] - PAD
    half = tokens // 2
    got_refs = [ref for ref in refs[:-2] if ref is not None]
    squares = get_squares(gated_ref)
    total = (chunks_ref if place is None else chunks_ref.at[place])[...].astype(F32)
    for ref in got_refs:
        squares = squares + get_squares(ref)
    if len(got_refs) == 2:
        total = total + jnp.concatenate([ref[:half].astype(F32) for ref in got_refs], axis=0)
    else:
        total = total + got_refs[0][:tokens].astype(F32)
    total = total.astype(BF16)
    if refs[-1] is None:
        refs[-2][:tokens] = total
        put_squares(refs[-2], squares)
    else:
        put_halves(refs[-2:], total, squares)


def end_kernel(inner, base_ref, own_ref, first_ref, second_ref, other_ref, out_ref):
    tokens, features = out_ref.shape
    half = tokens // 2
    squares = get_squares(own_ref) + get_squares(first_ref) + get_squares(second_ref) + get_squares(other_ref)
    factor = lax.rsqrt(squares * (1.0 / inner) + 1e-05)
    factor = jnp.broadcast_to(factor, (128, tokens)).T
    for j, ref in enumerate((first_ref, second_ref)):
        rows = slice(j * half, (j + 1) * half)
        for i in range(features // 128):
            span = slice(i * 128, (i + 1) * 128)
            total = base_ref[rows, span].astype(F32) + ref[:half, span].astype(F32) + other_ref[rows, span].astype(F32)
            out_ref[rows, span] = (total * factor[rows]).astype(BF16)


def call(kernel, ins, outs, args, scratch=(), flops=0, moved=0, limit=24):
    return pl.pallas_call(
        kernel,
        in_specs=ins,
        out_specs=[VMEM] * len(outs),
        out_shape=[jax.ShapeDtypeStruct(*o) for o in outs],
        scratch_shapes=[pltpu.VMEM(a.shape, a.dtype) for a in scratch] + [pltpu.SemaphoreType.DMA((8,))] * (HBM in ins),
        cost_estimate=pl.CostEstimate(flops=flops, bytes_accessed=moved, transcendentals=0),
        compiler_params=pltpu.CompilerParams(vmem_limit_bytes=limit * 2**20),
    )(*args)


def body(
    input_x, input_z, input_b, input_c, step_raw, doc_starts, log_rate, step_bias, skip_gain, norm_gain, out_weight
):
    tokens, channels = input_x.shape
    heads = log_rate.shape[0]
    width = channels // heads
    state_width = input_b.shape[1]
    devices = lax.axis_size("seq")
    planes = devices // N_ROW
    in_plane = [[p * N_ROW + i for i in range(N_ROW)] for p in range(planes)]
    across = [[p * N_ROW + i for p in range(planes)] for i in range(N_ROW)]
    sent = (width + PAD, state_width)

    local = (
        log_rate.reshape(1, heads),
        step_bias.reshape(1, heads),
        step_raw.T,
        doc_starts.reshape(1, tokens),
        input_b,
        input_x,
    )
    pieces, rows, cols = call(
        state_kernel,
        [HBM] * 6,
        [((heads, *sent), BF16), ((5 * heads, tokens), F32), ((tokens, 128), F32)],
        local,
        scratch=local,
        limit=60,
        flops=2 * tokens * channels * state_width,
        moved=2 * tokens * channels,
    )
    got = lax.all_to_all(pieces, "seq", 0, 0, axis_index_groups=in_plane)
    skip = skip_gain.reshape(1, heads)
    gain = norm_gain.reshape(1, channels)
    (totals,) = call(plane_kernel, [VMEM], [((planes, *sent), BF16)], (got,), moved=2**19)
    near = (input_c, input_b, rows, cols, skip, input_x, input_z)
    own, opened = call(
        intra_kernel,
        [ANY] + [HBM] * 7,
        [((tokens, channels), F32)] * 2,
        (totals, *near),
        scratch=near,
        limit=60,
        flops=2 * tokens * tokens * channels,
        moved=8 * 2**20,
    )
    got_planes = lax.all_to_all(totals, "seq", 0, 0, axis_index_groups=across)
    got_planes, own = lax.optimization_barrier((got_planes, own))
    plane = lax.div(lax.axis_index("seq"), N_ROW).reshape(1)
    (entries,) = call(
        entry_kernel, [SMEM, VMEM, VMEM], [((N_ROW, width, state_width), BF16)], (plane, got, got_planes), moved=2**19
    )
    needed = (input_c, own, opened, gain)
    needed = call(
        bring_kernel,
        [ANY] + [HBM] * len(needed),
        [(a.shape, a.dtype) for a in needed],
        (entries, *needed),
        moved=2**21,
        limit=48,
    )
    entries = lax.all_to_all(entries, "seq", 0, 0, axis_index_groups=in_plane)
    me = lax.axis_index("head").reshape(1)
    features = out_weight.shape[1] // N_PART
    slab = ((tokens + PAD, features), BF16)
    way = (1 - 2 * lax.rem(lax.axis_index("seq"), 2)).reshape(1)

    def send(array, steps, swap):
        pairs = []
        for seq in range(devices):
            for head in range(N_PART):
                there = (head + steps * (1 - 2 * (seq % 2))) % N_PART
                pairs.append((seq * N_PART + head, (seq ^ swap) * N_PART + there))
        return lax.ppermute(array, ("seq", "head"), pairs)

    half_slab = ((tokens // 2 + PAD, features), BF16)
    gated, far_first, far_second, w_next = call(
        gate_kernel,
        [SMEM] * 2 + [VMEM] * 5 + [HBM],
        [slab, half_slab, half_slab, ((channels, features), BF16)],
        (me, way, entries, *needed, out_weight),
        scratch=[jax.ShapeDtypeStruct((channels, features), BF16)],
        flops=2 * tokens * channels * features,
        moved=2**21,
        limit=50,
    )
    other = send(gated, 0, 1)
    own_got = [send(far_first, 1, 0), send(far_second, 1, 0)]
    begin, other_sent = call(
        begin_kernel,
        [VMEM] * 3,
        [((tokens, features), BF16), slab],
        (gated, other, w_next),
        flops=4 * tokens * channels * features,
        moved=2**20,
    )
    other_got = send(other_sent, 1, 0)
    steps = N_PART // 2 - 2
    chunks, base = call(
        chunks_kernel,
        [SMEM, SMEM, VMEM, VMEM, HBM],
        [((steps, 2, tokens, features), BF16), ((tokens, features), BF16)],
        (me, way, gated, other, out_weight),
        scratch=[jax.ShapeDtypeStruct((steps + 1, channels, features), BF16)],
        flops=10 * tokens * channels * features,
        moved=2**21,
        limit=50,
    )

    def join(chunk, place, mine, got, halves):
        def kernel(*refs):
            outs = refs[2 + len(got) :]
            join_kernel(place, *refs[: 2 + len(got)], *(outs if halves else (*outs, None)))

        return call(
            kernel, [VMEM] * (2 + len(got)), [half_slab] * 2 if halves else [slab], (chunk, mine, *got), moved=2**19
        )

    own_got = [send(*join(begin, None, gated, own_got, False), 1, 0)]
    for away in range(steps, 0, -1):
        last = away == 1
        other_got = send(*join(chunks, (away - 1, 1), other, [other_got], False), 1, int(last))
        own_got = [send(part, 1, 0) for part in join(chunks, (away - 1, 0), gated, own_got, last)]
    (out,) = call(
        functools.partial(end_kernel, channels * N_PART),
        [VMEM] * 5,
        [((tokens, features), BF16)],
        (base, gated, *own_got, other_got),
        moved=2**20,
    )
    return out


def solution(mesh):
    in_specs = (
        P("seq", "head"),
        P("seq", "head"),
        P("seq", None),
        P("seq", None),
        P("seq", "head"),
        P("seq"),
        P("head"),
        P("head"),
        P("head"),
        P("head"),
        P("head", None),
    )
    out_specs = P("seq", "head")
    return jax.shard_map(body, mesh=mesh, in_specs=in_specs, out_specs=out_specs, check_vma=False)
```

```python
import functools

import jax
import jax.numpy as jnp
from jax import lax
from jax.experimental import pallas as pl
from jax.experimental.pallas import tpu as pltpu
from jax.sharding import PartitionSpec as P

SPAN = 256
N_ROW = 8
N_PART = 8
PAD = 16
F32, BF16 = (jnp.float32, jnp.bfloat16)
VMEM = pl.BlockSpec(memory_space=pltpu.VMEM)
SMEM = pl.BlockSpec(memory_space=pltpu.SMEM)
HBM = pl.BlockSpec(memory_space=pltpu.HBM)
ANY = pl.BlockSpec(memory_space=pl.ANY)


def column_of(row, shape):
    count = shape[0]
    spread = jnp.broadcast_to(row, (count, count))
    same = lax.broadcasted_iota(jnp.int32, spread.shape, 0) == lax.broadcasted_iota(jnp.int32, spread.shape, 1)
    return jnp.broadcast_to(jnp.sum(jnp.where(same, spread, 0.0), axis=1, keepdims=True), shape)


def fetch(sources, targets, sems):
    copies = [pltpu.make_async_copy(s, t, sems.at[i]) for i, (s, t) in enumerate(zip(sources, targets))]
    for copy in copies:
        copy.start()
    return copies


def running_sum(rows):
    lanes = lax.broadcasted_iota(jnp.int32, rows.shape, 1)
    step = 1
    while step < rows.shape[1]:
        rows = rows + jnp.where(lanes >= step, pltpu.roll(rows, step, 1), 0.0)
        step *= 2
    return rows


def keep_rows(keep):
    high = keep.astype(BF16).astype(F32)
    middle = (keep - high).astype(BF16).astype(F32)
    low = keep - high - middle
    rows = lax.broadcasted_iota(jnp.int32, (PAD, keep.shape[1]), 0)
    out = jnp.where(rows == 0, high, jnp.where(rows == 1, middle, jnp.where(rows == 2, low, 0.0)))
    return out.astype(BF16)


def piece(ref, index, state_rows):
    state = ref[index, :state_rows, :].astype(F32)
    keep = jnp.sum(ref[index, state_rows:, :].astype(F32), axis=0, keepdims=True)
    return state, keep


def state_kernel(*refs):
    (log_rate, bias, raw_ref, flag_ref, b_ref, x_ref) = refs[9:15]
    out_ref, rows_ref, cols_ref = refs[6:9]
    copies = fetch(refs[:6], refs[9:15], refs[15])
    for copy in copies[:4]:
        copy.wait()
    heads, tokens = raw_ref.shape
    width = x_ref.shape[1] // heads
    raw = raw_ref[...]
    dt = jax.nn.softplus(raw + column_of(bias[...], raw.shape))
    rate = -jnp.exp(column_of(log_rate[...], raw.shape))
    flags = jnp.broadcast_to(flag_ref[...].astype(F32), raw.shape)
    sums = running_sum(jnp.concatenate([rate * dt, flags], axis=0))
    running, resets = (sums[:heads], sums[heads:])
    run_last = jnp.broadcast_to(running[:, tokens - 1 :], raw.shape)
    reset_last = jnp.broadcast_to(resets[:, tokens - 1 :], raw.shape)
    weights = jnp.where(resets == reset_last, jnp.exp(run_last - running), 0.0) * dt
    opening = jnp.where(resets == 0.0, jnp.exp(running), 0.0)
    rows = jnp.concatenate([running, dt, resets, opening, weights], axis=0)
    rows_ref[...] = rows
    cols = jnp.concatenate([rows, jnp.zeros((128 - rows.shape[0], tokens), F32)], axis=0).T
    cols_ref[...] = cols
    through = jnp.where(reset_last == 0.0, jnp.exp(run_last), 0.0)
    spread = jnp.concatenate(
        [
            jnp.broadcast_to(cols[:, 4 * heads + h : 4 * heads + h + 1], (tokens, width))
            for h in range(heads)
        ],
        axis=1,
    )
    for copy in copies[4:]:
        copy.wait()
    scaled = (spread * x_ref[...].astype(F32)).astype(BF16)
    states = lax.dot_general(scaled, b_ref[...], (((0,), (0,)), ((), ())), preferred_element_type=F32)
    for h in range(heads):
        out_ref[h, :width, :] = states[h * width : (h + 1) * width].astype(BF16)
        out_ref[h, width:, :] = keep_rows(through[h : h + 1, :128])


def intra_kernel(*refs):
    own_ref, open_ref = refs[8:10]
    c_ref, b_ref, rows_ref, cols_ref, skip_ref, x_ref, z_ref = refs[10:17]
    for copy in fetch(refs[1:8], refs[10:17], refs[17]):
        copy.wait()
    tokens = x_ref.shape[0]
    heads = skip_ref.shape[1]
    width = x_ref.shape[1] // heads
    skip = skip_ref[...]
    scores = lax.dot_general(c_ref[...], b_ref[...], (((1,), (1,)), ((), ())), preferred_element_type=F32)
    reset_row = rows_ref[2 * heads : 2 * heads + 1, :]
    reset_col = cols_ref[:, 2 * heads : 2 * heads + 1]
    later = lax.broadcasted_iota(jnp.int32, scores.shape, 0)
    earlier = lax.broadcasted_iota(jnp.int32, scores.shape, 1)
    allowed = (later >= earlier) & (reset_col == reset_row)
    scores = jnp.where(allowed, scores, 0.0)
    for h in range(heads):
        span = slice(h * width, (h + 1) * width)
        spread = cols_ref[:, h : h + 1] - rows_ref[h : h + 1, :]
        decays = jnp.exp(jnp.where(allowed, spread, 0.0))
        mixing = (scores * decays * rows_ref[heads + h : heads + h + 1, :]).astype(BF16)
        x_h = x_ref[:, span]
        out = jnp.dot(mixing, x_h, preferred_element_type=F32) + skip[:, h : h + 1] * x_h.astype(F32)
        v = z_ref[:, span].astype(F32)
        gate = v / (1.0 + jnp.exp(-v))
        own_ref[:, span] = out * gate
        open_ref[:, span] = gate * cols_ref[:, 3 * heads + h : 3 * heads + h + 1]


def plane_kernel(got_ref, out_ref):
    count, rows, lanes = got_ref.shape
    state_rows = rows - PAD
    total, keep = piece(got_ref, 0, state_rows)
    for i in range(1, count):
        state, factor = piece(got_ref, i, state_rows)
        total = factor * total + state
        keep = keep * factor
    total, keep = (total.astype(BF16), keep_rows(keep))
    for i in range(out_ref.shape[0]):
        out_ref[i, :state_rows, :] = total
        out_ref[i, state_rows:, :] = keep


def entry_kernel(plane, got_ref, planes_ref, out_ref):
    count, rows, lanes = got_ref.shape
    state_rows = rows - PAD
    mine = plane[0]
    entry = jnp.zeros((state_rows, lanes), F32)
    for i in range(planes_ref.shape[0] - 1):
        state, factor = piece(planes_ref, i, state_rows)
        entry = jnp.where(i < mine, factor * entry + state, entry)
    out_ref[0] = entry.astype(BF16)
    for i in range(count - 1):
        state, factor = piece(got_ref, i, state_rows)
        entry = factor * entry + state
        out_ref[i + 1] = entry.astype(BF16)


def bring_kernel(*refs):
    count = len(refs) // 2 - 1
    for copy in fetch(refs[1 : count + 1], refs[count + 1 : -1], refs[-1]):
        copy.wait()


def put_squares(ref, squares):
    high = squares.astype(BF16).astype(F32)
    middle = (squares - high).astype(BF16).astype(F32)
    low = squares - high - middle
    first = jnp.concatenate([high, middle], axis=1)
    second = jnp.concatenate([low, jnp.zeros_like(low)], axis=1)
    row = lax.broadcasted_iota(jnp.int32, (PAD, ref.shape[1]), 0)
    rows = jnp.where(row == 0, first, jnp.where(row == 1, second, 0.0))
    ref[ref.shape[0] - PAD :, :] = rows.astype(BF16)


def get_squares(ref):
    rows = jnp.sum(ref[ref.shape[0] - PAD :, :].astype(F32), axis=0, keepdims=True)
    half = ref.shape[1] // 2
    return rows[:, :half] + rows[:, half:]


def columns(w_hbm, me, away, features):
    place = (me + away + N_PART) % N_PART
    return w_hbm.at[:, pl.ds(pl.multiple_of(place * features, features), features)]


def gate_kernel(me, way, entry_ref, c_ref, own_ref, open_ref, gain_ref, w_hbm, *refs):
    gated_ref, far_ref, next_ref, w_ref, sems = refs
    heads, width, lanes = entry_ref.shape
    tokens = own_ref.shape[0]
    features = w_ref.shape[1]
    wanted = [columns(w_hbm, me[0], away, features) for away in (N_PART // 2, (N_PART // 2 - 1) * way[0])]
    copies = fetch(wanted, [w_ref, next_ref], sems)
    entries = entry_ref[...].reshape(heads * width, lanes)
    carried = lax.dot_general(c_ref[...], entries, (((1,), (1,)), ((), ())), preferred_element_type=F32)
    gated = own_ref[...] + open_ref[...] * carried
    scaled = (gated * gain_ref[...]).astype(BF16)
    gated_ref[:tokens] = scaled
    squares = jnp.sum(gated * gated, axis=1, keepdims=True)
    squares = jnp.broadcast_to(squares, (tokens, 128)).T[:1]
    put_squares(gated_ref, squares)
    put_squares(far_ref, squares)
    copies[0].wait()
    far_ref[:tokens] = jnp.dot(scaled, w_ref[...], preferred_element_type=F32).astype(BF16)
    copies[1].wait()


def begin_kernel(own_ref, other_ref, w_ref, chunk_ref, out_ref):
    tokens = chunk_ref.shape[0]
    out_ref[:tokens] = jnp.dot(other_ref[:tokens], w_ref[...], preferred_element_type=F32).astype(BF16)
    out_ref[tokens:] = other_ref[tokens:]
    chunk_ref[...] = jnp.dot(own_ref[:tokens], w_ref[...], preferred_element_type=F32).astype(BF16)


def chunks_kernel(me, way, own_ref, other_ref, w_hbm, out_ref, base_ref, w_ref, sems):
    steps, _, tokens, features = out_ref.shape
    order = [*range(steps, 0, -1), 0]
    copies = fetch([columns(w_hbm, me[0], a * way[0], features) for a in order], [w_ref.at[a] for a in order], sems)
    for a, copy in zip(order, copies):
        copy.wait()
        if a == 0:
            base_ref[...] = jnp.dot(own_ref[:tokens], w_ref[a], preferred_element_type=F32).astype(BF16)
        else:
            for j, ref in enumerate((own_ref, other_ref)):
                out_ref[a - 1, j] = jnp.dot(ref[:tokens], w_ref[a], preferred_element_type=F32).astype(BF16)


def join_kernel(place, chunk_ref, gated_ref, got_ref, out_ref):
    tokens = gated_ref.shape[0] - PAD
    chunk = (chunk_ref if place is None else chunk_ref.at[place])[...]
    out_ref[:tokens] = (chunk.astype(F32) + got_ref[:tokens].astype(F32)).astype(BF16)
    put_squares(out_ref, get_squares(gated_ref) + get_squares(got_ref))


def end_kernel(inner, base_ref, own_ref, right_ref, left_ref, out_ref):
    tokens, features = out_ref.shape
    squares = get_squares(own_ref) + get_squares(right_ref) + get_squares(left_ref)
    factor = lax.rsqrt(squares * (1.0 / inner) + 1e-05)
    factor = jnp.broadcast_to(factor, (128, tokens)).T
    for i in range(features // 128):
        span = slice(i * 128, (i + 1) * 128)
        total = base_ref[:, span].astype(F32)
        total = total + right_ref[:tokens, span].astype(F32) + left_ref[:tokens, span].astype(F32)
        out_ref[:, span] = (total * factor).astype(BF16)


def call(kernel, ins, outs, args, scratch=(), flops=0, moved=0, limit=24):
    return pl.pallas_call(
        kernel,
        in_specs=ins,
        out_specs=[VMEM] * len(outs),
        out_shape=[jax.ShapeDtypeStruct(*o) for o in outs],
        scratch_shapes=[pltpu.VMEM(a.shape, a.dtype) for a in scratch] + [pltpu.SemaphoreType.DMA((8,))] * (HBM in ins),
        cost_estimate=pl.CostEstimate(flops=flops, bytes_accessed=moved, transcendentals=0),
        compiler_params=pltpu.CompilerParams(vmem_limit_bytes=limit * 2**20),
    )(*args)


def body(
    input_x, input_z, input_b, input_c, step_raw, doc_starts, log_rate, step_bias, skip_gain, norm_gain, out_weight
):
    tokens, channels = input_x.shape
    heads = log_rate.shape[0]
    width = channels // heads
    state_width = input_b.shape[1]
    devices = lax.axis_size("seq")
    planes = devices // N_ROW
    in_plane = [[p * N_ROW + i for i in range(N_ROW)] for p in range(planes)]
    across = [[p * N_ROW + i for p in range(planes)] for i in range(N_ROW)]
    sent = (width + PAD, state_width)

    local = (
        log_rate.reshape(1, heads),
        step_bias.reshape(1, heads),
        step_raw.T,
        doc_starts.reshape(1, tokens),
        input_b,
        input_x,
    )
    pieces, rows, cols = call(
        state_kernel,
        [HBM] * 6,
        [((heads, *sent), BF16), ((5 * heads, tokens), F32), ((tokens, 128), F32)],
        local,
        scratch=local,
        limit=60,
        flops=2 * tokens * channels * state_width,
        moved=2 * tokens * channels,
    )
    got = lax.all_to_all(pieces, "seq", 0, 0, axis_index_groups=in_plane)
    skip = skip_gain.reshape(1, heads)
    gain = norm_gain.reshape(1, channels)
    (totals,) = call(plane_kernel, [VMEM], [((planes, *sent), BF16)], (got,), moved=2**19)
    near = (input_c, input_b, rows, cols, skip, input_x, input_z)
    own, opened = call(
        intra_kernel,
        [ANY] + [HBM] * 7,
        [((tokens, channels), F32)] * 2,
        (totals, *near),
        scratch=near,
        limit=60,
        flops=2 * tokens * tokens * channels,
        moved=8 * 2**20,
    )
    got_planes = lax.all_to_all(totals, "seq", 0, 0, axis_index_groups=across)
    got_planes, own = lax.optimization_barrier((got_planes, own))
    plane = lax.div(lax.axis_index("seq"), N_ROW).reshape(1)
    (entries,) = call(
        entry_kernel, [SMEM, VMEM, VMEM], [((N_ROW, width, state_width), BF16)], (plane, got, got_planes), moved=2**19
    )
    needed = (input_c, own, opened, gain)
    needed = call(
        bring_kernel,
        [ANY] + [HBM] * len(needed),
        [(a.shape, a.dtype) for a in needed],
        (entries, *needed),
        moved=2**21,
        limit=48,
    )
    entries = lax.all_to_all(entries, "seq", 0, 0, axis_index_groups=in_plane)
    me = lax.axis_index("head").reshape(1)
    features = out_weight.shape[1] // N_PART
    slab = ((tokens + PAD, features), BF16)
    way = (1 - 2 * lax.rem(lax.axis_index("seq"), 2)).reshape(1)

    def send(array, steps, swap):
        pairs = []
        for seq in range(devices):
            for head in range(N_PART):
                there = (head + steps * (1 - 2 * (seq % 2))) % N_PART
                pairs.append((seq * N_PART + head, (seq ^ swap) * N_PART + there))
        return lax.ppermute(array, ("seq", "head"), pairs)

    gated, far, w_next = call(
        gate_kernel,
        [SMEM] * 2 + [VMEM] * 5 + [HBM],
        [slab, slab, ((channels, features), BF16)],
        (me, way, entries, *needed, out_weight),
        scratch=[jax.ShapeDtypeStruct((channels, features), BF16)],
        flops=2 * tokens * channels * features,
        moved=2**21,
        limit=50,
    )
    other = send(gated, 0, 1)
    own_got = send(far, 1, 0)
    begin, other_sent = call(
        begin_kernel,
        [VMEM] * 3,
        [((tokens, features), BF16), slab],
        (gated, other, w_next),
        flops=4 * tokens * channels * features,
        moved=2**20,
    )
    other_got = send(other_sent, 1, 0)

    steps = N_PART // 2 - 2
    chunks, base = call(
        chunks_kernel,
        [SMEM, SMEM, VMEM, VMEM, HBM],
        [((steps, 2, tokens, features), BF16), ((tokens, features), BF16)],
        (me, way, gated, other, out_weight),
        scratch=[jax.ShapeDtypeStruct((steps + 1, channels, features), BF16)],
        flops=10 * tokens * channels * features,
        moved=2**21,
        limit=50,
    )

    def join(place, chunk, mine, got):
        return call(functools.partial(join_kernel, place), [VMEM] * 3, [slab], (chunk, mine, got), moved=2**19)[0]

    own_got = send(join(None, begin, gated, own_got), 1, 0)
    for away in range(steps, 0, -1):
        other_got = send(join((away - 1, 1), chunks, other, other_got), 1, int(away == 1))
        own_got = send(join((away - 1, 0), chunks, gated, own_got), 1, 0)
    (out,) = call(
        functools.partial(end_kernel, channels * N_PART),
        [VMEM] * 4,
        [((tokens, features), BF16)],
        (base, gated, own_got, other_got),
        moved=2**20,
    )
    return out


def solution(mesh):
    in_specs = (
        P("seq", "head"),
        P("seq", "head"),
        P("seq", None),
        P("seq", None),
        P("seq", "head"),
        P("seq"),
        P("head"),
        P("head"),
        P("head"),
        P("head"),
        P("head", None),
    )
    out_specs = P("seq", "head")
    return jax.shard_map(body, mesh=mesh, in_specs=in_specs, out_specs=out_specs, check_vma=False)
```

```python
import functools

import jax
import jax.numpy as jnp
from jax import lax
from jax.experimental import pallas as pl
from jax.experimental.pallas import tpu as pltpu
from jax.sharding import PartitionSpec as P

SPAN = 256
N_ROW = 8
N_PART = 8
PAD = 16
F32, BF16 = (jnp.float32, jnp.bfloat16)
VMEM = pl.BlockSpec(memory_space=pltpu.VMEM)
SMEM = pl.BlockSpec(memory_space=pltpu.SMEM)
HBM = pl.BlockSpec(memory_space=pltpu.HBM)
ANY = pl.BlockSpec(memory_space=pl.ANY)


def column_of(row, shape):
    count = shape[0]
    spread = jnp.broadcast_to(row, (count, count))
    same = lax.broadcasted_iota(jnp.int32, spread.shape, 0) == lax.broadcasted_iota(jnp.int32, spread.shape, 1)
    return jnp.broadcast_to(jnp.sum(jnp.where(same, spread, 0.0), axis=1, keepdims=True), shape)


def fetch(sources, targets, sems):
    copies = [pltpu.make_async_copy(s, t, sems.at[i]) for i, (s, t) in enumerate(zip(sources, targets))]
    for copy in copies:
        copy.start()
    return copies


def running_sum(rows):
    lanes = lax.broadcasted_iota(jnp.int32, rows.shape, 1)
    step = 1
    while step < rows.shape[1]:
        rows = rows + jnp.where(lanes >= step, pltpu.roll(rows, step, 1), 0.0)
        step *= 2
    return rows


def keep_rows(keep):
    high = keep.astype(BF16).astype(F32)
    middle = (keep - high).astype(BF16).astype(F32)
    low = keep - high - middle
    rows = lax.broadcasted_iota(jnp.int32, (PAD, keep.shape[1]), 0)
    out = jnp.where(rows == 0, high, jnp.where(rows == 1, middle, jnp.where(rows == 2, low, 0.0)))
    return out.astype(BF16)


def piece(ref, index, state_rows):
    state = ref[index, :state_rows, :].astype(F32)
    keep = jnp.sum(ref[index, state_rows:, :].astype(F32), axis=0, keepdims=True)
    return state, keep


def state_kernel(*refs):
    (log_rate, bias, raw_ref, flag_ref, b_ref, x_ref) = refs[9:15]
    out_ref, rows_ref, cols_ref = refs[6:9]
    copies = fetch(refs[:6], refs[9:15], refs[15])
    for copy in copies[:4]:
        copy.wait()
    heads, tokens = raw_ref.shape
    width = x_ref.shape[1] // heads
    raw = raw_ref[...]
    dt = jax.nn.softplus(raw + column_of(bias[...], raw.shape))
    rate = -jnp.exp(column_of(log_rate[...], raw.shape))
    flags = jnp.broadcast_to(flag_ref[...].astype(F32), raw.shape)
    sums = running_sum(jnp.concatenate([rate * dt, flags], axis=0))
    running, resets = (sums[:heads], sums[heads:])
    run_last = jnp.broadcast_to(running[:, tokens - 1 :], raw.shape)
    reset_last = jnp.broadcast_to(resets[:, tokens - 1 :], raw.shape)
    weights = jnp.where(resets == reset_last, jnp.exp(run_last - running), 0.0) * dt
    opening = jnp.where(resets == 0.0, jnp.exp(running), 0.0)
    rows = jnp.concatenate([running, dt, resets, opening, weights], axis=0)
    rows_ref[...] = rows
    cols = jnp.concatenate([rows, jnp.zeros((128 - rows.shape[0], tokens), F32)], axis=0).T
    cols_ref[...] = cols
    through = jnp.where(reset_last == 0.0, jnp.exp(run_last), 0.0)
    spread = jnp.concatenate(
        [
            jnp.broadcast_to(cols[:, 4 * heads + h : 4 * heads + h + 1], (tokens, width))
            for h in range(heads)
        ],
        axis=1,
    )
    for copy in copies[4:]:
        copy.wait()
    scaled = (spread * x_ref[...].astype(F32)).astype(BF16)
    states = lax.dot_general(scaled, b_ref[...], (((0,), (0,)), ((), ())), preferred_element_type=F32)
    for h in range(heads):
        out_ref[h, :width, :] = states[h * width : (h + 1) * width].astype(BF16)
        out_ref[h, width:, :] = keep_rows(through[h : h + 1, :128])


def intra_kernel(*refs):
    own_ref, open_ref = refs[8:10]
    c_ref, b_ref, rows_ref, cols_ref, skip_ref, x_ref, z_ref = refs[10:17]
    for copy in fetch(refs[1:8], refs[10:17], refs[17]):
        copy.wait()
    tokens = x_ref.shape[0]
    heads = skip_ref.shape[1]
    width = x_ref.shape[1] // heads
    skip = skip_ref[...]
    scores = lax.dot_general(c_ref[...], b_ref[...], (((1,), (1,)), ((), ())), preferred_element_type=F32)
    reset_row = rows_ref[2 * heads : 2 * heads + 1, :]
    reset_col = cols_ref[:, 2 * heads : 2 * heads + 1]
    later = lax.broadcasted_iota(jnp.int32, scores.shape, 0)
    earlier = lax.broadcasted_iota(jnp.int32, scores.shape, 1)
    allowed = (later >= earlier) & (reset_col == reset_row)
    scores = jnp.where(allowed, scores, 0.0)
    for h in range(heads):
        span = slice(h * width, (h + 1) * width)
        spread = cols_ref[:, h : h + 1] - rows_ref[h : h + 1, :]
        decays = jnp.exp(jnp.where(allowed, spread, 0.0))
        mixing = (scores * decays * rows_ref[heads + h : heads + h + 1, :]).astype(BF16)
        x_h = x_ref[:, span]
        out = jnp.dot(mixing, x_h, preferred_element_type=F32) + skip[:, h : h + 1] * x_h.astype(F32)
        v = z_ref[:, span].astype(F32)
        gate = v / (1.0 + jnp.exp(-v))
        own_ref[:, span] = out * gate
        open_ref[:, span] = gate * cols_ref[:, 3 * heads + h : 3 * heads + h + 1]


def plane_kernel(got_ref, out_ref):
    count, rows, lanes = got_ref.shape
    state_rows = rows - PAD
    total, keep = piece(got_ref, 0, state_rows)
    for i in range(1, count):
        state, factor = piece(got_ref, i, state_rows)
        total = factor * total + state
        keep = keep * factor
    total, keep = (total.astype(BF16), keep_rows(keep))
    for i in range(out_ref.shape[0]):
        out_ref[i, :state_rows, :] = total
        out_ref[i, state_rows:, :] = keep


def entry_kernel(plane, got_ref, planes_ref, out_ref):
    count, rows, lanes = got_ref.shape
    state_rows = rows - PAD
    mine = plane[0]
    entry = jnp.zeros((state_rows, lanes), F32)
    for i in range(planes_ref.shape[0] - 1):
        state, factor = piece(planes_ref, i, state_rows)
        entry = jnp.where(i < mine, factor * entry + state, entry)
    out_ref[0] = entry.astype(BF16)
    for i in range(count - 1):
        state, factor = piece(got_ref, i, state_rows)
        entry = factor * entry + state
        out_ref[i + 1] = entry.astype(BF16)


def bring_kernel(*refs):
    count = len(refs) // 2 - 1
    for copy in fetch(refs[1 : count + 1], refs[count + 1 : -1], refs[-1]):
        copy.wait()


def put_squares(ref, squares):
    high = squares.astype(BF16).astype(F32)
    middle = (squares - high).astype(BF16).astype(F32)
    low = squares - high - middle
    first = jnp.concatenate([high, middle], axis=1)
    second = jnp.concatenate([low, jnp.zeros_like(low)], axis=1)
    row = lax.broadcasted_iota(jnp.int32, (PAD, ref.shape[1]), 0)
    rows = jnp.where(row == 0, first, jnp.where(row == 1, second, 0.0))
    ref[ref.shape[0] - PAD :, :] = rows.astype(BF16)


def get_squares(ref):
    rows = jnp.sum(ref[ref.shape[0] - PAD :, :].astype(F32), axis=0, keepdims=True)
    half = ref.shape[1] // 2
    return rows[:, :half] + rows[:, half:]


def columns(w_hbm, me, away, features):
    place = (me + away + N_PART) % N_PART
    return w_hbm.at[:, pl.ds(pl.multiple_of(place * features, features), features)]


def gate_kernel(me, way, entry_ref, c_ref, own_ref, open_ref, gain_ref, w_hbm, *refs):
    gated_ref, far_ref, next_ref, w_ref, sems = refs
    heads, width, lanes = entry_ref.shape
    tokens = own_ref.shape[0]
    features = w_ref.shape[1]
    wanted = [columns(w_hbm, me[0], away, features) for away in (N_PART // 2, (N_PART // 2 - 1) * way[0])]
    copies = fetch(wanted, [w_ref, next_ref], sems)
    entries = entry_ref[...].reshape(heads * width, lanes)
    carried = lax.dot_general(c_ref[...], entries, (((1,), (1,)), ((), ())), preferred_element_type=F32)
    gated = own_ref[...] + open_ref[...] * carried
    scaled = (gated * gain_ref[...]).astype(BF16)
    gated_ref[:tokens] = scaled
    squares = jnp.sum(gated * gated, axis=1, keepdims=True)
    squares = jnp.broadcast_to(squares, (tokens, 128)).T[:1]
    put_squares(gated_ref, squares)
    put_squares(far_ref, squares)
    copies[0].wait()
    far_ref[:tokens] = jnp.dot(scaled, w_ref[...], preferred_element_type=F32).astype(BF16)
    copies[1].wait()


def begin_kernel(own_ref, other_ref, w_ref, out_ref):
    tokens = out_ref.shape[1]
    for j, ref in enumerate((own_ref, other_ref)):
        out_ref[j] = jnp.dot(ref[:tokens], w_ref[...], preferred_element_type=F32).astype(BF16)


def chunks_kernel(me, way, own_ref, other_ref, w_hbm, out_ref, base_ref, w_ref, sems):
    steps, _, tokens, features = out_ref.shape
    order = [*range(steps, 0, -1), 0]
    copies = fetch([columns(w_hbm, me[0], a * way[0], features) for a in order], [w_ref.at[a] for a in order], sems)
    for a, copy in zip(order, copies):
        copy.wait()
        if a == 0:
            base_ref[...] = jnp.dot(own_ref[:tokens], w_ref[a], preferred_element_type=F32).astype(BF16)
        else:
            for j, ref in enumerate((own_ref, other_ref)):
                out_ref[a - 1, j] = jnp.dot(ref[:tokens], w_ref[a], preferred_element_type=F32).astype(BF16)


def join_kernel(place, chunk_ref, gated_ref, *refs):
    got_refs, out_ref = refs[:-1], refs[-1]
    tokens = gated_ref.shape[0] - PAD
    squares = get_squares(gated_ref)
    total = chunk_ref[place].astype(F32)
    for ref in got_refs:
        squares = squares + get_squares(ref)
        total = total + ref[:tokens].astype(F32)
    out_ref[:tokens] = total.astype(BF16)
    put_squares(out_ref, squares)


def sum_kernel(base_ref, own_ref, got_ref, total_ref, square_ref):
    tokens = base_ref.shape[0]
    square_ref[...] = get_squares(own_ref) + get_squares(got_ref)
    total_ref[...] = base_ref[...].astype(F32) + got_ref[:tokens].astype(F32)


def end_kernel(inner, total_ref, square_ref, got_ref, out_ref):
    tokens, features = out_ref.shape
    squares = square_ref[...] + get_squares(got_ref)
    factor = lax.rsqrt(squares * (1.0 / inner) + 1e-05)
    factor = jnp.broadcast_to(factor, (128, tokens)).T
    for i in range(features // 128):
        span = slice(i * 128, (i + 1) * 128)
        total = total_ref[:, span] + got_ref[:tokens, span].astype(F32)
        out_ref[:, span] = (total * factor).astype(BF16)


def call(kernel, ins, outs, args, scratch=(), flops=0, moved=0, limit=24):
    return pl.pallas_call(
        kernel,
        in_specs=ins,
        out_specs=[VMEM] * len(outs),
        out_shape=[jax.ShapeDtypeStruct(*o) for o in outs],
        scratch_shapes=[pltpu.VMEM(a.shape, a.dtype) for a in scratch] + [pltpu.SemaphoreType.DMA((8,))] * (HBM in ins),
        cost_estimate=pl.CostEstimate(flops=flops, bytes_accessed=moved, transcendentals=0),
        compiler_params=pltpu.CompilerParams(vmem_limit_bytes=limit * 2**20),
    )(*args)


def body(
    input_x, input_z, input_b, input_c, step_raw, doc_starts, log_rate, step_bias, skip_gain, norm_gain, out_weight
):
    tokens, channels = input_x.shape
    heads = log_rate.shape[0]
    width = channels // heads
    state_width = input_b.shape[1]
    devices = lax.axis_size("seq")
    planes = devices // N_ROW
    in_plane = [[p * N_ROW + i for i in range(N_ROW)] for p in range(planes)]
    across = [[p * N_ROW + i for p in range(planes)] for i in range(N_ROW)]
    sent = (width + PAD, state_width)

    local = (
        log_rate.reshape(1, heads),
        step_bias.reshape(1, heads),
        step_raw.T,
        doc_starts.reshape(1, tokens),
        input_b,
        input_x,
    )
    pieces, rows, cols = call(
        state_kernel,
        [HBM] * 6,
        [((heads, *sent), BF16), ((5 * heads, tokens), F32), ((tokens, 128), F32)],
        local,
        scratch=local,
        limit=60,
        flops=2 * tokens * channels * state_width,
        moved=2 * tokens * channels,
    )
    got = lax.all_to_all(pieces, "seq", 0, 0, axis_index_groups=in_plane)
    skip = skip_gain.reshape(1, heads)
    gain = norm_gain.reshape(1, channels)
    (totals,) = call(plane_kernel, [VMEM], [((planes, *sent), BF16)], (got,), moved=2**19)
    near = (input_c, input_b, rows, cols, skip, input_x, input_z)
    own, opened = call(
        intra_kernel,
        [ANY] + [HBM] * 7,
        [((tokens, channels), F32)] * 2,
        (totals, *near),
        scratch=near,
        limit=60,
        flops=2 * tokens * tokens * channels,
        moved=8 * 2**20,
    )
    got_planes = lax.all_to_all(totals, "seq", 0, 0, axis_index_groups=across)
    got_planes, own = lax.optimization_barrier((got_planes, own))
    plane = lax.div(lax.axis_index("seq"), N_ROW).reshape(1)
    (entries,) = call(
        entry_kernel, [SMEM, VMEM, VMEM], [((N_ROW, width, state_width), BF16)], (plane, got, got_planes), moved=2**19
    )
    needed = (input_c, own, opened, gain)
    needed = call(
        bring_kernel,
        [ANY] + [HBM] * len(needed),
        [(a.shape, a.dtype) for a in needed],
        (entries, *needed),
        moved=2**21,
        limit=48,
    )
    entries = lax.all_to_all(entries, "seq", 0, 0, axis_index_groups=in_plane)
    me = lax.axis_index("head").reshape(1)
    features = out_weight.shape[1] // N_PART
    slab = ((tokens + PAD, features), BF16)
    way = (1 - 2 * lax.rem(lax.axis_index("seq"), 2)).reshape(1)

    def send(array, steps, swap):
        pairs = []
        for seq in range(devices):
            for head in range(N_PART):
                there = (head + steps * (1 - 2 * (seq % 2))) % N_PART
                pairs.append((seq * N_PART + head, (seq ^ swap) * N_PART + there))
        return lax.ppermute(array, ("seq", "head"), pairs)

    gated, far, w_next = call(
        gate_kernel,
        [SMEM] * 2 + [VMEM] * 5 + [HBM],
        [slab, slab, ((channels, features), BF16)],
        (me, way, entries, *needed, out_weight),
        scratch=[jax.ShapeDtypeStruct((channels, features), BF16)],
        flops=2 * tokens * channels * features,
        moved=2**21,
        limit=50,
    )
    other = send(gated, 0, 1)
    own_got = send(far, 1, 0)
    (begin,) = call(
        begin_kernel,
        [VMEM] * 3,
        [((2, tokens, features), BF16)],
        (gated, other, w_next),
        flops=4 * tokens * channels * features,
        moved=2**22,
    )

    def join(place, chunk, mine, *got):
        kernel = functools.partial(join_kernel, place)
        return call(kernel, [VMEM] * (2 + len(got)), [slab], (chunk, mine, *got), moved=2**19)[0]

    other_sent = join(1, begin, other)
    other_got = send(other_sent, 1, 0)
    own_sent = join(0, begin, gated, own_got)
    own_got = send(own_sent, 1, 0)
    steps = N_PART // 2 - 2
    gated_then, _ = lax.optimization_barrier((gated, own_sent))
    chunks, base = call(
        chunks_kernel,
        [SMEM, SMEM, VMEM, VMEM, HBM],
        [((steps, 2, tokens, features), BF16), ((tokens, features), BF16)],
        (me, way, gated_then, other, out_weight),
        scratch=[jax.ShapeDtypeStruct((steps + 1, channels, features), BF16)],
        flops=10 * tokens * channels * features,
        moved=2**21,
        limit=50,
    )
    for away in range(steps, 0, -1):
        other_got = send(join((away - 1, 1), chunks, other, other_got), 1, int(away == 1))
        own_got = send(join((away - 1, 0), chunks, gated, own_got), 1, 0)
    total, squares = call(
        sum_kernel, [VMEM] * 3, [((tokens, features), F32), ((1, tokens), F32)], (base, gated, other_got), moved=2**20
    )
    (out,) = call(
        functools.partial(end_kernel, channels * N_PART),
        [VMEM] * 3,
        [((tokens, features), BF16)],
        (total, squares, own_got),
        moved=2**20,
    )
    return out


def solution(mesh):
    in_specs = (
        P("seq", "head"),
        P("seq", "head"),
        P("seq", None),
        P("seq", None),
        P("seq", "head"),
        P("seq"),
        P("head"),
        P("head"),
        P("head"),
        P("head"),
        P("head", None),
    )
    out_specs = P("seq", "head")
    return jax.shard_map(body, mesh=mesh, in_specs=in_specs, out_specs=out_specs, check_vma=False)
```

```python
import functools

import jax
import jax.numpy as jnp
from jax import lax
from jax.experimental import pallas as pl
from jax.experimental.pallas import tpu as pltpu
from jax.sharding import PartitionSpec as P

SPAN = 256
N_ROW = 8
N_PART = 8
PAD = 16
F32, BF16 = (jnp.float32, jnp.bfloat16)
VMEM = pl.BlockSpec(memory_space=pltpu.VMEM)
SMEM = pl.BlockSpec(memory_space=pltpu.SMEM)
HBM = pl.BlockSpec(memory_space=pltpu.HBM)
ANY = pl.BlockSpec(memory_space=pl.ANY)


def column_of(row, shape):
    count = shape[0]
    spread = jnp.broadcast_to(row, (count, count))
    same = lax.broadcasted_iota(jnp.int32, spread.shape, 0) == lax.broadcasted_iota(jnp.int32, spread.shape, 1)
    return jnp.broadcast_to(jnp.sum(jnp.where(same, spread, 0.0), axis=1, keepdims=True), shape)


def fetch(sources, targets, sems):
    copies = [pltpu.make_async_copy(s, t, sems.at[i]) for i, (s, t) in enumerate(zip(sources, targets))]
    for copy in copies:
        copy.start()
    return copies


def parts_of(rows):
    high = rows.astype(BF16).astype(F32)
    middle = (rows - high).astype(BF16).astype(F32)
    return [high, middle, rows - high - middle]


def keep_rows(keep):
    high = keep.astype(BF16).astype(F32)
    middle = (keep - high).astype(BF16).astype(F32)
    low = keep - high - middle
    rows = lax.broadcasted_iota(jnp.int32, (PAD, keep.shape[1]), 0)
    out = jnp.where(rows == 0, high, jnp.where(rows == 1, middle, jnp.where(rows == 2, low, 0.0)))
    return out.astype(BF16)


def piece(ref, index, state_rows):
    state = ref[index, :state_rows, :].astype(F32)
    keep = jnp.sum(ref[index, state_rows:, :].astype(F32), axis=0, keepdims=True)
    return state, keep


def state_kernel(*refs):
    (log_rate, bias, raw_ref, flag_ref, b_ref, x_ref) = refs[8:14]
    out_ref, rows_ref = refs[6:8]
    copies = fetch(refs[:6], refs[8:14], refs[14])
    for copy in copies[:4]:
        copy.wait()
    heads, tokens = raw_ref.shape
    channels = x_ref.shape[1]
    width = channels // heads
    raw = raw_ref[...]
    dt = jax.nn.softplus(raw + column_of(bias[...], raw.shape))
    rate = -jnp.exp(column_of(log_rate[...], raw.shape))
    flags = jnp.broadcast_to(flag_ref[...].astype(F32), raw.shape)
    steps = jnp.concatenate([*parts_of(rate * dt), flags], axis=0).astype(BF16)
    square = (tokens, tokens)
    upto = lax.broadcasted_iota(jnp.int32, square, 0) <= lax.broadcasted_iota(jnp.int32, square, 1)
    sums = jnp.dot(steps, jnp.where(upto, 1.0, 0.0).astype(BF16), preferred_element_type=F32)
    running = sums[:heads] + sums[heads : 2 * heads] + sums[2 * heads : 3 * heads]
    resets = sums[3 * heads :]
    run_last = jnp.broadcast_to(running[:, tokens - 1 :], raw.shape)
    reset_last = jnp.broadcast_to(resets[:, tokens - 1 :], raw.shape)
    weights = jnp.where(resets == reset_last, jnp.exp(run_last - running), 0.0) * dt
    opening = jnp.where(resets == 0.0, jnp.exp(running), 0.0)
    rows_ref[...] = jnp.concatenate([running, dt, resets, opening], axis=0)
    through = jnp.where(reset_last == 0.0, jnp.exp(run_last), 0.0)
    shape = (4 * heads, channels)
    row, first = lax.broadcasted_iota(jnp.int32, shape, 0), lax.broadcasted_iota(jnp.int32, shape, 1)
    for i in range(3):
        row = jnp.where(row >= heads, row - heads, row)
    mine = (first >= row * width) & (first < (row + 1) * width)
    spread = lax.dot_general(
        jnp.concatenate([*parts_of(weights), jnp.zeros_like(weights)], axis=0).astype(BF16),
        jnp.where(mine, 1.0, 0.0).astype(BF16),
        (((0,), (0,)), ((), ())),
        preferred_element_type=F32,
    )
    for copy in copies[4:]:
        copy.wait()
    scaled = (spread * x_ref[...].astype(F32)).astype(BF16)
    states = lax.dot_general(scaled, b_ref[...], (((0,), (0,)), ((), ())), preferred_element_type=F32)
    for h in range(heads):
        out_ref[h, :width, :] = states[h * width : (h + 1) * width].astype(BF16)
        out_ref[h, width:, :] = keep_rows(through[h : h + 1, :128])


def intra_kernel(*refs):
    own_ref, open_ref = refs[7:9]
    c_ref, b_ref, rows_ref, skip_ref, x_ref, z_ref, cols_ref = refs[9:16]
    for copy in fetch(refs[1:7], refs[9:15], refs[16]):
        copy.wait()
    rows = rows_ref[...]
    cols_ref[...] = jnp.concatenate([rows, jnp.zeros((128 - rows.shape[0], rows.shape[1]), F32)], axis=0).T
    tokens = x_ref.shape[0]
    heads = skip_ref.shape[1]
    width = x_ref.shape[1] // heads
    skip = skip_ref[...]
    scores = lax.dot_general(c_ref[...], b_ref[...], (((1,), (1,)), ((), ())), preferred_element_type=F32)
    reset_row = rows_ref[2 * heads : 2 * heads + 1, :]
    reset_col = cols_ref[:, 2 * heads : 2 * heads + 1]
    later = lax.broadcasted_iota(jnp.int32, scores.shape, 0)
    earlier = lax.broadcasted_iota(jnp.int32, scores.shape, 1)
    allowed = (later >= earlier) & (reset_col == reset_row)
    scores = jnp.where(allowed, scores, 0.0)
    for h in range(heads):
        span = slice(h * width, (h + 1) * width)
        spread = cols_ref[:, h : h + 1] - rows_ref[h : h + 1, :]
        decays = jnp.exp(jnp.where(allowed, spread, 0.0))
        mixing = (scores * decays * rows_ref[heads + h : heads + h + 1, :]).astype(BF16)
        x_h = x_ref[:, span]
        out = jnp.dot(mixing, x_h, preferred_element_type=F32) + skip[:, h : h + 1] * x_h.astype(F32)
        v = z_ref[:, span].astype(F32)
        gate = v / (1.0 + jnp.exp(-v))
        own_ref[:, span] = out * gate
        open_ref[:, span] = gate * cols_ref[:, 3 * heads + h : 3 * heads + h + 1]


def plane_kernel(got_ref, out_ref):
    count, rows, lanes = got_ref.shape
    state_rows = rows - PAD
    total, keep = piece(got_ref, 0, state_rows)
    for i in range(1, count):
        state, factor = piece(got_ref, i, state_rows)
        total = factor * total + state
        keep = keep * factor
    total, keep = (total.astype(BF16), keep_rows(keep))
    for i in range(out_ref.shape[0]):
        out_ref[i, :state_rows, :] = total
        out_ref[i, state_rows:, :] = keep


def entry_kernel(plane, got_ref, planes_ref, out_ref):
    count, rows, lanes = got_ref.shape
    state_rows = rows - PAD
    mine = plane[0]
    entry = jnp.zeros((state_rows, lanes), F32)
    for i in range(planes_ref.shape[0] - 1):
        state, factor = piece(planes_ref, i, state_rows)
        entry = jnp.where(i < mine, factor * entry + state, entry)
    out_ref[0] = entry.astype(BF16)
    for i in range(count - 1):
        state, factor = piece(got_ref, i, state_rows)
        entry = factor * entry + state
        out_ref[i + 1] = entry.astype(BF16)


def bring_kernel(*refs):
    count = len(refs) // 2 - 1
    for copy in fetch(refs[1 : count + 1], refs[count + 1 : -1], refs[-1]):
        copy.wait()


def put_squares(ref, squares):
    high = squares.astype(BF16).astype(F32)
    middle = (squares - high).astype(BF16).astype(F32)
    low = squares - high - middle
    first = jnp.concatenate([high, middle], axis=1)
    second = jnp.concatenate([low, jnp.zeros_like(low)], axis=1)
    row = lax.broadcasted_iota(jnp.int32, (PAD, ref.shape[1]), 0)
    rows = jnp.where(row == 0, first, jnp.where(row == 1, second, 0.0))
    ref[ref.shape[0] - PAD :, :] = rows.astype(BF16)


def get_squares(ref):
    rows = jnp.sum(ref[ref.shape[0] - PAD :, :].astype(F32), axis=0, keepdims=True)
    half = ref.shape[1] // 2
    return rows[:, :half] + rows[:, half:]


def columns(w_hbm, me, away, features):
    place = (me + away + N_PART) % N_PART
    return w_hbm.at[:, pl.ds(pl.multiple_of(place * features, features), features)]


def gate_kernel(me, way, entry_ref, c_ref, own_ref, open_ref, gain_ref, w_hbm, *refs):
    gated_ref, far_ref, next_ref, w_ref, sems = refs
    heads, width, lanes = entry_ref.shape
    tokens = own_ref.shape[0]
    features = w_ref.shape[1]
    wanted = [columns(w_hbm, me[0], away, features) for away in (N_PART // 2, (N_PART // 2 - 1) * way[0])]
    copies = fetch(wanted, [w_ref, next_ref], sems)
    entries = entry_ref[...].reshape(heads * width, lanes)
    carried = lax.dot_general(c_ref[...], entries, (((1,), (1,)), ((), ())), preferred_element_type=F32)
    gated = own_ref[...] + open_ref[...] * carried
    scaled = (gated * gain_ref[...]).astype(BF16)
    gated_ref[:tokens] = scaled
    squares = jnp.sum(gated * gated, axis=1, keepdims=True)
    squares = jnp.broadcast_to(squares, (tokens, 128)).T[:1]
    put_squares(gated_ref, squares)
    put_squares(far_ref, squares)
    copies[0].wait()
    far_ref[:tokens] = jnp.dot(scaled, w_ref[...], preferred_element_type=F32).astype(BF16)
    copies[1].wait()


def begin_kernel(own_ref, other_ref, w_ref, out_ref):
    tokens = out_ref.shape[1]
    for j, ref in enumerate((own_ref, other_ref)):
        out_ref[j] = jnp.dot(ref[:tokens], w_ref[...], preferred_element_type=F32).astype(BF16)


def chunks_kernel(me, way, own_ref, other_ref, w_hbm, out_ref, base_ref, w_ref, sems):
    steps, _, tokens, features = out_ref.shape
    order = [*range(steps, 0, -1), 0]
    copies = fetch([columns(w_hbm, me[0], a * way[0], features) for a in order], [w_ref.at[a] for a in order], sems)
    for a, copy in zip(order, copies):
        copy.wait()
        if a == 0:
            base_ref[...] = jnp.dot(own_ref[:tokens], w_ref[a], preferred_element_type=F32).astype(BF16)
        else:
            for j, ref in enumerate((own_ref, other_ref)):
                out_ref[a - 1, j] = jnp.dot(ref[:tokens], w_ref[a], preferred_element_type=F32).astype(BF16)


def join_kernel(place, chunk_ref, gated_ref, *refs):
    got_refs, out_ref = refs[:-1], refs[-1]
    tokens = gated_ref.shape[0] - PAD
    squares = get_squares(gated_ref)
    total = chunk_ref[place].astype(F32)
    for ref in got_refs:
        squares = squares + get_squares(ref)
        total = total + ref[:tokens].astype(F32)
    out_ref[:tokens] = total.astype(BF16)
    put_squares(out_ref, squares)


def sum_kernel(base_ref, own_ref, got_ref, total_ref, square_ref):
    tokens = base_ref.shape[0]
    square_ref[...] = get_squares(own_ref) + get_squares(got_ref)
    total_ref[...] = base_ref[...].astype(F32) + got_ref[:tokens].astype(F32)


def end_kernel(inner, total_ref, square_ref, got_ref, out_ref):
    tokens, features = out_ref.shape
    squares = square_ref[...] + get_squares(got_ref)
    factor = lax.rsqrt(squares * (1.0 / inner) + 1e-05)
    factor = jnp.broadcast_to(factor, (128, tokens)).T
    for i in range(features // 128):
        span = slice(i * 128, (i + 1) * 128)
        total = total_ref[:, span] + got_ref[:tokens, span].astype(F32)
        out_ref[:, span] = (total * factor).astype(BF16)


def call(kernel, ins, outs, args, scratch=(), flops=0, moved=0, limit=24):
    return pl.pallas_call(
        kernel,
        in_specs=ins,
        out_specs=[VMEM] * len(outs),
        out_shape=[jax.ShapeDtypeStruct(*o) for o in outs],
        scratch_shapes=[pltpu.VMEM(a.shape, a.dtype) for a in scratch] + [pltpu.SemaphoreType.DMA((8,))] * (HBM in ins),
        cost_estimate=pl.CostEstimate(flops=flops, bytes_accessed=moved, transcendentals=0),
        compiler_params=pltpu.CompilerParams(vmem_limit_bytes=limit * 2**20),
    )(*args)


def body(
    input_x, input_z, input_b, input_c, step_raw, doc_starts, log_rate, step_bias, skip_gain, norm_gain, out_weight
):
    tokens, channels = input_x.shape
    heads = log_rate.shape[0]
    width = channels // heads
    state_width = input_b.shape[1]
    devices = lax.axis_size("seq")
    planes = devices // N_ROW
    in_plane = [[p * N_ROW + i for i in range(N_ROW)] for p in range(planes)]
    across = [[p * N_ROW + i for p in range(planes)] for i in range(N_ROW)]
    sent = (width + PAD, state_width)

    local = (
        log_rate.reshape(1, heads),
        step_bias.reshape(1, heads),
        step_raw.T,
        doc_starts.reshape(1, tokens),
        input_b,
        input_x,
    )
    pieces, rows = call(
        state_kernel,
        [HBM] * 6,
        [((heads, *sent), BF16), ((4 * heads, tokens), F32)],
        local,
        scratch=local,
        limit=60,
        flops=2 * tokens * channels * state_width,
        moved=2 * tokens * channels,
    )
    got = lax.all_to_all(pieces, "seq", 0, 0, axis_index_groups=in_plane)
    skip = skip_gain.reshape(1, heads)
    gain = norm_gain.reshape(1, channels)
    (totals,) = call(plane_kernel, [VMEM], [((planes, *sent), BF16)], (got,), moved=2**19)
    near = (input_c, input_b, rows, skip, input_x, input_z)
    own, opened = call(
        intra_kernel,
        [ANY] + [HBM] * 6,
        [((tokens, channels), F32)] * 2,
        (totals, *near),
        scratch=(*near, jax.ShapeDtypeStruct((tokens, 128), F32)),
        limit=60,
        flops=2 * tokens * tokens * channels,
        moved=8 * 2**20,
    )
    got_planes = lax.all_to_all(totals, "seq", 0, 0, axis_index_groups=across)
    got_planes, own = lax.optimization_barrier((got_planes, own))
    plane = lax.div(lax.axis_index("seq"), N_ROW).reshape(1)
    (entries,) = call(
        entry_kernel, [SMEM, VMEM, VMEM], [((N_ROW, width, state_width), BF16)], (plane, got, got_planes), moved=2**19
    )
    needed = (input_c, own, opened, gain)
    needed = call(
        bring_kernel,
        [ANY] + [HBM] * len(needed),
        [(a.shape, a.dtype) for a in needed],
        (entries, *needed),
        moved=2**21,
        limit=48,
    )
    entries = lax.all_to_all(entries, "seq", 0, 0, axis_index_groups=in_plane)
    me = lax.axis_index("head").reshape(1)
    features = out_weight.shape[1] // N_PART
    slab = ((tokens + PAD, features), BF16)
    way = (1 - 2 * lax.rem(lax.axis_index("seq"), 2)).reshape(1)

    def send(array, steps, swap):
        pairs = []
        for seq in range(devices):
            for head in range(N_PART):
                there = (head + steps * (1 - 2 * (seq % 2))) % N_PART
                pairs.append((seq * N_PART + head, (seq ^ swap) * N_PART + there))
        return lax.ppermute(array, ("seq", "head"), pairs)

    gated, far, w_next = call(
        gate_kernel,
        [SMEM] * 2 + [VMEM] * 5 + [HBM],
        [slab, slab, ((channels, features), BF16)],
        (me, way, entries, *needed, out_weight),
        scratch=[jax.ShapeDtypeStruct((channels, features), BF16)],
        flops=2 * tokens * channels * features,
        moved=2**21,
        limit=50,
    )
    other = send(gated, 0, 1)
    own_got = send(far, 1, 0)
    (begin,) = call(
        begin_kernel,
        [VMEM] * 3,
        [((2, tokens, features), BF16)],
        (gated, other, w_next),
        flops=4 * tokens * channels * features,
        moved=2**22,
    )

    def join(place, chunk, mine, *got):
        kernel = functools.partial(join_kernel, place)
        return call(kernel, [VMEM] * (2 + len(got)), [slab], (chunk, mine, *got), moved=2**19)[0]

    other_sent = join(1, begin, other)
    other_got = send(other_sent, 1, 0)
    own_sent = join(0, begin, gated, own_got)
    own_got = send(own_sent, 1, 0)
    steps = N_PART // 2 - 2
    gated_then, _ = lax.optimization_barrier((gated, own_sent))
    chunks, base = call(
        chunks_kernel,
        [SMEM, SMEM, VMEM, VMEM, HBM],
        [((steps, 2, tokens, features), BF16), ((tokens, features), BF16)],
        (me, way, gated_then, other, out_weight),
        scratch=[jax.ShapeDtypeStruct((steps + 1, channels, features), BF16)],
        flops=10 * tokens * channels * features,
        moved=2**21,
        limit=50,
    )
    for away in range(steps, 0, -1):
        other_got = send(join((away - 1, 1), chunks, other, other_got), 1, int(away == 1))
        own_got = send(join((away - 1, 0), chunks, gated, own_got), 1, 0)
    total, squares = call(
        sum_kernel, [VMEM] * 3, [((tokens, features), F32), ((1, tokens), F32)], (base, gated, other_got), moved=2**20
    )
    (out,) = call(
        functools.partial(end_kernel, channels * N_PART),
        [VMEM] * 3,
        [((tokens, features), BF16)],
        (total, squares, own_got),
        moved=2**20,
    )
    return out


def solution(mesh):
    in_specs = (
        P("seq", "head"),
        P("seq", "head"),
        P("seq", None),
        P("seq", None),
        P("seq", "head"),
        P("seq"),
        P("head"),
        P("head"),
        P("head"),
        P("head"),
        P("head", None),
    )
    out_specs = P("seq", "head")
    return jax.shard_map(body, mesh=mesh, in_specs=in_specs, out_specs=out_specs, check_vma=False)
```

```python
import functools

import jax
import jax.numpy as jnp
from jax import lax
from jax.experimental import pallas as pl
from jax.experimental.pallas import tpu as pltpu
from jax.sharding import PartitionSpec as P

SPAN = 256
N_ROW = 8
N_PART = 8
PAD = 16
F32, BF16 = (jnp.float32, jnp.bfloat16)
VMEM = pl.BlockSpec(memory_space=pltpu.VMEM)
SMEM = pl.BlockSpec(memory_space=pltpu.SMEM)
HBM = pl.BlockSpec(memory_space=pltpu.HBM)
ANY = pl.BlockSpec(memory_space=pl.ANY)


def column_of(row, shape):
    count = shape[0]
    spread = jnp.broadcast_to(row, (count, count))
    same = lax.broadcasted_iota(jnp.int32, spread.shape, 0) == lax.broadcasted_iota(jnp.int32, spread.shape, 1)
    return jnp.broadcast_to(jnp.sum(jnp.where(same, spread, 0.0), axis=1, keepdims=True), shape)


def fetch(sources, targets, sems):
    copies = [pltpu.make_async_copy(s, t, sems.at[i]) for i, (s, t) in enumerate(zip(sources, targets))]
    for copy in copies:
        copy.start()
    return copies


def parts_of(rows):
    high = rows.astype(BF16).astype(F32)
    middle = (rows - high).astype(BF16).astype(F32)
    return [high, middle, rows - high - middle]


def keep_rows(keep):
    high = keep.astype(BF16).astype(F32)
    middle = (keep - high).astype(BF16).astype(F32)
    low = keep - high - middle
    rows = lax.broadcasted_iota(jnp.int32, (PAD, keep.shape[1]), 0)
    out = jnp.where(rows == 0, high, jnp.where(rows == 1, middle, jnp.where(rows == 2, low, 0.0)))
    return out.astype(BF16)


def piece(ref, index, state_rows):
    state = ref[index, :state_rows, :].astype(F32)
    keep = jnp.sum(ref[index, state_rows:, :].astype(F32), axis=0, keepdims=True)
    return state, keep


def state_kernel(*refs):
    (log_rate, bias, raw_ref, flag_ref, b_ref, x_ref) = refs[8:14]
    out_ref, rows_ref = refs[6:8]
    copies = fetch(refs[:6], refs[8:14], refs[14])
    for copy in copies[:4]:
        copy.wait()
    heads, tokens = raw_ref.shape
    channels = x_ref.shape[1]
    width = channels // heads
    raw = raw_ref[...]
    dt = jax.nn.softplus(raw + column_of(bias[...], raw.shape))
    rate = -jnp.exp(column_of(log_rate[...], raw.shape))
    flags = jnp.broadcast_to(flag_ref[...].astype(F32), raw.shape)
    steps = jnp.concatenate([*parts_of(rate * dt), flags], axis=0).astype(BF16)
    square = (tokens, tokens)
    upto = lax.broadcasted_iota(jnp.int32, square, 0) <= lax.broadcasted_iota(jnp.int32, square, 1)
    sums = jnp.dot(steps, jnp.where(upto, 1.0, 0.0).astype(BF16), preferred_element_type=F32)
    running = sums[:heads] + sums[heads : 2 * heads] + sums[2 * heads : 3 * heads]
    resets = sums[3 * heads :]
    run_last = jnp.broadcast_to(running[:, tokens - 1 :], raw.shape)
    reset_last = jnp.broadcast_to(resets[:, tokens - 1 :], raw.shape)
    weights = jnp.where(resets == reset_last, jnp.exp(run_last - running), 0.0) * dt
    opening = jnp.where(resets == 0.0, jnp.exp(running), 0.0)
    rows_ref[...] = jnp.concatenate([running, dt, resets, opening], axis=0)
    through = jnp.where(reset_last == 0.0, jnp.exp(run_last), 0.0)
    shape = (4 * heads, channels)
    row, first = lax.broadcasted_iota(jnp.int32, shape, 0), lax.broadcasted_iota(jnp.int32, shape, 1)
    for i in range(3):
        row = jnp.where(row >= heads, row - heads, row)
    mine = (first >= row * width) & (first < (row + 1) * width)
    spread = lax.dot_general(
        jnp.concatenate([*parts_of(weights), jnp.zeros_like(weights)], axis=0).astype(BF16),
        jnp.where(mine, 1.0, 0.0).astype(BF16),
        (((0,), (0,)), ((), ())),
        preferred_element_type=F32,
    )
    for copy in copies[4:]:
        copy.wait()
    scaled = (spread * x_ref[...].astype(F32)).astype(BF16)
    states = lax.dot_general(scaled, b_ref[...], (((0,), (0,)), ((), ())), preferred_element_type=F32)
    for h in range(heads):
        out_ref[h, :width, :] = states[h * width : (h + 1) * width].astype(BF16)
        out_ref[h, width:, :] = keep_rows(through[h : h + 1, :128])


def intra_kernel(*refs):
    own_ref, open_ref = refs[7:9]
    c_ref, b_ref, rows_ref, skip_ref, x_ref, z_ref, cols_ref = refs[9:16]
    for copy in fetch(refs[1:7], refs[9:15], refs[16]):
        copy.wait()
    rows = rows_ref[...]
    cols_ref[...] = jnp.concatenate([rows, jnp.zeros((128 - rows.shape[0], rows.shape[1]), F32)], axis=0).T
    tokens = x_ref.shape[0]
    heads = skip_ref.shape[1]
    width = x_ref.shape[1] // heads
    skip = skip_ref[...]
    scores = lax.dot_general(c_ref[...], b_ref[...], (((1,), (1,)), ((), ())), preferred_element_type=F32)
    reset_row = rows_ref[2 * heads : 2 * heads + 1, :]
    reset_col = cols_ref[:, 2 * heads : 2 * heads + 1]
    later = lax.broadcasted_iota(jnp.int32, scores.shape, 0)
    earlier = lax.broadcasted_iota(jnp.int32, scores.shape, 1)
    allowed = (later >= earlier) & (reset_col == reset_row)
    scores = jnp.where(allowed, scores, 0.0)
    for h in range(heads):
        span = slice(h * width, (h + 1) * width)
        spread = cols_ref[:, h : h + 1] - rows_ref[h : h + 1, :]
        decays = jnp.exp(jnp.where(allowed, spread, 0.0))
        mixing = (scores * decays * rows_ref[heads + h : heads + h + 1, :]).astype(BF16)
        x_h = x_ref[:, span]
        out = jnp.dot(mixing, x_h, preferred_element_type=F32) + skip[:, h : h + 1] * x_h.astype(F32)
        v = z_ref[:, span].astype(F32)
        gate = v / (1.0 + jnp.exp(-v))
        own_ref[:, span] = out * gate
        open_ref[:, span] = gate * cols_ref[:, 3 * heads + h : 3 * heads + h + 1]


def plane_kernel(got_ref, out_ref):
    count, rows, lanes = got_ref.shape
    state_rows = rows - PAD
    total, keep = piece(got_ref, 0, state_rows)
    for i in range(1, count):
        state, factor = piece(got_ref, i, state_rows)
        total = factor * total + state
        keep = keep * factor
    total, keep = (total.astype(BF16), keep_rows(keep))
    for i in range(out_ref.shape[0]):
        out_ref[i, :state_rows, :] = total
        out_ref[i, state_rows:, :] = keep


def entry_kernel(plane, got_ref, planes_ref, out_ref):
    count, rows, lanes = got_ref.shape
    state_rows = rows - PAD
    mine = plane[0]
    entry = jnp.zeros((state_rows, lanes), F32)
    for i in range(planes_ref.shape[0] - 1):
        state, factor = piece(planes_ref, i, state_rows)
        entry = jnp.where(i < mine, factor * entry + state, entry)
    out_ref[0] = entry.astype(BF16)
    for i in range(count - 1):
        state, factor = piece(got_ref, i, state_rows)
        entry = factor * entry + state
        out_ref[i + 1] = entry.astype(BF16)


def bring_kernel(*refs):
    count = len(refs) // 2 - 1
    for copy in fetch(refs[1 : count + 1], refs[count + 1 : -1], refs[-1]):
        copy.wait()


def put_squares(ref, squares):
    high = squares.astype(BF16).astype(F32)
    middle = (squares - high).astype(BF16).astype(F32)
    low = squares - high - middle
    first = jnp.concatenate([high, middle], axis=1)
    second = jnp.concatenate([low, jnp.zeros_like(low)], axis=1)
    row = lax.broadcasted_iota(jnp.int32, (PAD, ref.shape[1]), 0)
    rows = jnp.where(row == 0, first, jnp.where(row == 1, second, 0.0))
    ref[ref.shape[0] - PAD :, :] = rows.astype(BF16)


def get_squares(ref):
    rows = jnp.sum(ref[ref.shape[0] - PAD :, :].astype(F32), axis=0, keepdims=True)
    half = ref.shape[1] // 2
    return rows[:, :half] + rows[:, half:]


def columns(w_hbm, me, away, features):
    place = (me + away + N_PART) % N_PART
    return w_hbm.at[:, pl.ds(pl.multiple_of(place * features, features), features)]


def gate_kernel(me, way, entry_ref, c_ref, own_ref, open_ref, gain_ref, w_hbm, *refs):
    gated_ref, far_ref, chunk_ref, w_ref, sems = refs
    heads, width, lanes = entry_ref.shape
    tokens = own_ref.shape[0]
    features = w_ref.shape[2]
    wanted = [columns(w_hbm, me[0], away, features) for away in (N_PART // 2, (N_PART // 2 - 1) * way[0])]
    copies = fetch(wanted, [w_ref.at[0], w_ref.at[1]], sems)
    entries = entry_ref[...].reshape(heads * width, lanes)
    carried = lax.dot_general(c_ref[...], entries, (((1,), (1,)), ((), ())), preferred_element_type=F32)
    gated = own_ref[...] + open_ref[...] * carried
    scaled = (gated * gain_ref[...]).astype(BF16)
    gated_ref[:tokens] = scaled
    squares = jnp.sum(gated * gated, axis=1, keepdims=True)
    squares = jnp.broadcast_to(squares, (tokens, 128)).T[:1]
    put_squares(gated_ref, squares)
    put_squares(far_ref, squares)
    copies[0].wait()
    far_ref[:tokens] = jnp.dot(scaled, w_ref[0], preferred_element_type=F32).astype(BF16)
    copies[1].wait()
    chunk_ref[0] = jnp.dot(scaled, w_ref[1], preferred_element_type=F32).astype(BF16)


def chunks_kernel(me, way, own_ref, other_ref, w_hbm, sent_ref, out_ref, base_ref, w_ref, sems):
    steps, _, tokens, features = out_ref.shape
    order = [*range(steps + 1, 0, -1), 0]
    copies = fetch([columns(w_hbm, me[0], a * way[0], features) for a in order], [w_ref.at[a] for a in order], sems)
    for a, copy in zip(order, copies):
        copy.wait()
        if a == steps + 1:
            sent_ref[:tokens] = jnp.dot(other_ref[:tokens], w_ref[a], preferred_element_type=F32).astype(BF16)
            sent_ref[tokens:] = other_ref[tokens:]
        elif a == 0:
            base_ref[...] = jnp.dot(own_ref[:tokens], w_ref[a], preferred_element_type=F32).astype(BF16)
        else:
            for j, ref in enumerate((own_ref, other_ref)):
                out_ref[a - 1, j] = jnp.dot(ref[:tokens], w_ref[a], preferred_element_type=F32).astype(BF16)


def join_kernel(place, chunk_ref, gated_ref, *refs):
    got_refs, out_ref = refs[:-1], refs[-1]
    tokens = gated_ref.shape[0] - PAD
    squares = get_squares(gated_ref)
    total = chunk_ref[place].astype(F32)
    for ref in got_refs:
        squares = squares + get_squares(ref)
        total = total + ref[:tokens].astype(F32)
    out_ref[:tokens] = total.astype(BF16)
    put_squares(out_ref, squares)


def sum_kernel(base_ref, own_ref, got_ref, total_ref, square_ref):
    tokens = base_ref.shape[0]
    square_ref[...] = get_squares(own_ref) + get_squares(got_ref)
    total_ref[...] = base_ref[...].astype(F32) + got_ref[:tokens].astype(F32)


def end_kernel(inner, total_ref, square_ref, got_ref, out_ref):
    tokens, features = out_ref.shape
    squares = square_ref[...] + get_squares(got_ref)
    factor = lax.rsqrt(squares * (1.0 / inner) + 1e-05)
    factor = jnp.broadcast_to(factor, (128, tokens)).T
    for i in range(features // 128):
        span = slice(i * 128, (i + 1) * 128)
        total = total_ref[:, span] + got_ref[:tokens, span].astype(F32)
        out_ref[:, span] = (total * factor).astype(BF16)


def call(kernel, ins, outs, args, scratch=(), flops=0, moved=0, limit=24):
    return pl.pallas_call(
        kernel,
        in_specs=ins,
        out_specs=[VMEM] * len(outs),
        out_shape=[jax.ShapeDtypeStruct(*o) for o in outs],
        scratch_shapes=[pltpu.VMEM(a.shape, a.dtype) for a in scratch] + [pltpu.SemaphoreType.DMA((8,))] * (HBM in ins),
        cost_estimate=pl.CostEstimate(flops=flops, bytes_accessed=moved, transcendentals=0),
        compiler_params=pltpu.CompilerParams(vmem_limit_bytes=limit * 2**20),
    )(*args)


def body(
    input_x, input_z, input_b, input_c, step_raw, doc_starts, log_rate, step_bias, skip_gain, norm_gain, out_weight
):
    tokens, channels = input_x.shape
    heads = log_rate.shape[0]
    width = channels // heads
    state_width = input_b.shape[1]
    devices = lax.axis_size("seq")
    planes = devices // N_ROW
    in_plane = [[p * N_ROW + i for i in range(N_ROW)] for p in range(planes)]
    across = [[p * N_ROW + i for p in range(planes)] for i in range(N_ROW)]
    sent = (width + PAD, state_width)

    local = (
        log_rate.reshape(1, heads),
        step_bias.reshape(1, heads),
        step_raw.T,
        doc_starts.reshape(1, tokens),
        input_b,
        input_x,
    )
    pieces, rows = call(
        state_kernel,
        [HBM] * 6,
        [((heads, *sent), BF16), ((4 * heads, tokens), F32)],
        local,
        scratch=local,
        limit=60,
        flops=2 * tokens * channels * state_width,
        moved=2 * tokens * channels,
    )
    got = lax.all_to_all(pieces, "seq", 0, 0, axis_index_groups=in_plane)
    skip = skip_gain.reshape(1, heads)
    gain = norm_gain.reshape(1, channels)
    (totals,) = call(plane_kernel, [VMEM], [((planes, *sent), BF16)], (got,), moved=2**19)
    near = (input_c, input_b, rows, skip, input_x, input_z)
    own, opened = call(
        intra_kernel,
        [ANY] + [HBM] * 6,
        [((tokens, channels), F32)] * 2,
        (totals, *near),
        scratch=(*near, jax.ShapeDtypeStruct((tokens, 128), F32)),
        limit=60,
        flops=2 * tokens * tokens * channels,
        moved=8 * 2**20,
    )
    got_planes = lax.all_to_all(totals, "seq", 0, 0, axis_index_groups=across)
    got_planes, own = lax.optimization_barrier((got_planes, own))
    plane = lax.div(lax.axis_index("seq"), N_ROW).reshape(1)
    (entries,) = call(
        entry_kernel, [SMEM, VMEM, VMEM], [((N_ROW, width, state_width), BF16)], (plane, got, got_planes), moved=2**19
    )
    needed = (input_c, own, opened, gain)
    needed = call(
        bring_kernel,
        [ANY] + [HBM] * len(needed),
        [(a.shape, a.dtype) for a in needed],
        (entries, *needed),
        moved=2**21,
        limit=48,
    )
    entries = lax.all_to_all(entries, "seq", 0, 0, axis_index_groups=in_plane)
    me = lax.axis_index("head").reshape(1)
    features = out_weight.shape[1] // N_PART
    slab = ((tokens + PAD, features), BF16)
    way = (1 - 2 * lax.rem(lax.axis_index("seq"), 2)).reshape(1)

    def send(array, steps, swap):
        pairs = []
        for seq in range(devices):
            for head in range(N_PART):
                there = (head + steps * (1 - 2 * (seq % 2))) % N_PART
                pairs.append((seq * N_PART + head, (seq ^ swap) * N_PART + there))
        return lax.ppermute(array, ("seq", "head"), pairs)

    gated, far, first_chunk = call(
        gate_kernel,
        [SMEM] * 2 + [VMEM] * 5 + [HBM],
        [slab, slab, ((1, tokens, features), BF16)],
        (me, way, entries, *needed, out_weight),
        scratch=[jax.ShapeDtypeStruct((2, channels, features), BF16)],
        flops=4 * tokens * channels * features,
        moved=2**21,
        limit=50,
    )

    def join(place, chunk, mine, got):
        kernel = functools.partial(join_kernel, place)
        return call(kernel, [VMEM] * 3, [slab], (chunk, mine, got), moved=2**19)[0]

    own_got = send(far, 1, 0)
    other = send(gated, 0, 1)
    own_sent = join(0, first_chunk, gated, own_got)
    own_got = send(own_sent, 1, 0)
    steps = N_PART // 2 - 2
    gated_then, own_sent = lax.optimization_barrier((gated, own_sent))
    other_sent, chunks, base = call(
        chunks_kernel,
        [SMEM, SMEM, VMEM, VMEM, HBM],
        [slab, ((steps, 2, tokens, features), BF16), ((tokens, features), BF16)],
        (me, way, gated_then, other, out_weight),
        scratch=[jax.ShapeDtypeStruct((steps + 2, channels, features), BF16)],
        flops=12 * tokens * channels * features,
        moved=2**22,
        limit=50,
    )
    other_got = send(other_sent, 1, 0)
    for away in range(steps, 0, -1):
        own_got = send(join((away - 1, 0), chunks, gated, own_got), 1, 0)
        other_got = send(join((away - 1, 1), chunks, other, other_got), 1, int(away == 1))
    total, squares = call(
        sum_kernel, [VMEM] * 3, [((tokens, features), F32), ((1, tokens), F32)], (base, gated, own_got), moved=2**20
    )
    (out,) = call(
        functools.partial(end_kernel, channels * N_PART),
        [VMEM] * 3,
        [((tokens, features), BF16)],
        (total, squares, other_got),
        moved=2**20,
    )
    return out


def solution(mesh):
    in_specs = (
        P("seq", "head"),
        P("seq", "head"),
        P("seq", None),
        P("seq", None),
        P("seq", "head"),
        P("seq"),
        P("head"),
        P("head"),
        P("head"),
        P("head"),
        P("head", None),
    )
    out_specs = P("seq", "head")
    return jax.shard_map(body, mesh=mesh, in_specs=in_specs, out_specs=out_specs, check_vma=False)
```

```python
import functools

import jax
import jax.numpy as jnp
from jax import lax
from jax.experimental import pallas as pl
from jax.experimental.pallas import tpu as pltpu
from jax.sharding import PartitionSpec as P

SPAN = 256
N_ROW = 8
N_PART = 8
PAD = 16
F32, BF16 = (jnp.float32, jnp.bfloat16)
VMEM = pl.BlockSpec(memory_space=pltpu.VMEM)
SMEM = pl.BlockSpec(memory_space=pltpu.SMEM)
HBM = pl.BlockSpec(memory_space=pltpu.HBM)
ANY = pl.BlockSpec(memory_space=pl.ANY)


def column_of(row, shape):
    count = shape[0]
    spread = jnp.broadcast_to(row, (count, count))
    same = lax.broadcasted_iota(jnp.int32, spread.shape, 0) == lax.broadcasted_iota(jnp.int32, spread.shape, 1)
    return jnp.broadcast_to(jnp.sum(jnp.where(same, spread, 0.0), axis=1, keepdims=True), shape)


def fetch(sources, targets, sems):
    copies = [pltpu.make_async_copy(s, t, sems.at[i]) for i, (s, t) in enumerate(zip(sources, targets))]
    for copy in copies:
        copy.start()
    return copies


def parts_of(rows):
    high = rows.astype(BF16).astype(F32)
    middle = (rows - high).astype(BF16).astype(F32)
    return [high, middle, rows - high - middle]


def keep_rows(keep):
    high = keep.astype(BF16).astype(F32)
    middle = (keep - high).astype(BF16).astype(F32)
    low = keep - high - middle
    rows = lax.broadcasted_iota(jnp.int32, (PAD, keep.shape[1]), 0)
    out = jnp.where(rows == 0, high, jnp.where(rows == 1, middle, jnp.where(rows == 2, low, 0.0)))
    return out.astype(BF16)


def piece(ref, index, state_rows):
    state = ref[index, :state_rows, :].astype(F32)
    keep = jnp.sum(ref[index, state_rows:, :].astype(F32), axis=0, keepdims=True)
    return state, keep


def state_kernel(*refs):
    (log_rate, bias, raw_ref, flag_ref, b_ref, x_ref) = refs[8:14]
    out_ref, rows_ref = refs[6:8]
    copies = fetch(refs[:6], refs[8:14], refs[14])
    for copy in copies[:4]:
        copy.wait()
    heads, tokens = raw_ref.shape
    channels = x_ref.shape[1]
    width = channels // heads
    raw = raw_ref[...]
    dt = jax.nn.softplus(raw + column_of(bias[...], raw.shape))
    rate = -jnp.exp(column_of(log_rate[...], raw.shape))
    flags = jnp.broadcast_to(flag_ref[...].astype(F32), raw.shape)
    steps = jnp.concatenate([*parts_of(rate * dt), flags], axis=0).astype(BF16)
    square = (tokens, tokens)
    upto = lax.broadcasted_iota(jnp.int32, square, 0) <= lax.broadcasted_iota(jnp.int32, square, 1)
    sums = jnp.dot(steps, jnp.where(upto, 1.0, 0.0).astype(BF16), preferred_element_type=F32)
    running = sums[:heads] + sums[heads : 2 * heads] + sums[2 * heads : 3 * heads]
    resets = sums[3 * heads :]
    run_last = jnp.broadcast_to(running[:, tokens - 1 :], raw.shape)
    reset_last = jnp.broadcast_to(resets[:, tokens - 1 :], raw.shape)
    weights = jnp.where(resets == reset_last, jnp.exp(run_last - running), 0.0) * dt
    opening = jnp.where(resets == 0.0, jnp.exp(running), 0.0)
    rows_ref[...] = jnp.concatenate([running, dt, resets, opening], axis=0)
    through = jnp.where(reset_last == 0.0, jnp.exp(run_last), 0.0)
    shape = (4 * heads, channels)
    row, first = lax.broadcasted_iota(jnp.int32, shape, 0), lax.broadcasted_iota(jnp.int32, shape, 1)
    for i in range(3):
        row = jnp.where(row >= heads, row - heads, row)
    mine = (first >= row * width) & (first < (row + 1) * width)
    spread = lax.dot_general(
        jnp.concatenate([*parts_of(weights), jnp.zeros_like(weights)], axis=0).astype(BF16),
        jnp.where(mine, 1.0, 0.0).astype(BF16),
        (((0,), (0,)), ((), ())),
        preferred_element_type=F32,
    )
    for copy in copies[4:]:
        copy.wait()
    scaled = (spread * x_ref[...].astype(F32)).astype(BF16)
    states = lax.dot_general(scaled, b_ref[...], (((0,), (0,)), ((), ())), preferred_element_type=F32)
    for h in range(heads):
        out_ref[h, :width, :] = states[h * width : (h + 1) * width].astype(BF16)
        out_ref[h, width:, :] = keep_rows(through[h : h + 1, :128])


def intra_kernel(*refs):
    out_ref = refs[8]
    c_ref, b_ref, rows_ref, skip_ref, x_ref, z_ref, gain_ref, cols_ref = refs[9:17]
    for copy in fetch(refs[1:8], refs[9:16], refs[17]):
        copy.wait()
    rows = rows_ref[...]
    cols_ref[...] = jnp.concatenate([rows, jnp.zeros((128 - rows.shape[0], rows.shape[1]), F32)], axis=0).T
    tokens = x_ref.shape[0]
    heads = skip_ref.shape[1]
    width = x_ref.shape[1] // heads
    skip = skip_ref[...]
    scores = lax.dot_general(c_ref[...], b_ref[...], (((1,), (1,)), ((), ())), preferred_element_type=F32)
    reset_row = rows_ref[2 * heads : 2 * heads + 1, :]
    reset_col = cols_ref[:, 2 * heads : 2 * heads + 1]
    later = lax.broadcasted_iota(jnp.int32, scores.shape, 0)
    earlier = lax.broadcasted_iota(jnp.int32, scores.shape, 1)
    allowed = (later >= earlier) & (reset_col == reset_row)
    scores = jnp.where(allowed, scores, 0.0)
    for h in range(heads):
        span = slice(h * width, (h + 1) * width)
        spread = cols_ref[:, h : h + 1] - rows_ref[h : h + 1, :]
        decays = jnp.exp(jnp.where(allowed, spread, 0.0))
        mixing = (scores * decays * rows_ref[heads + h : heads + h + 1, :]).astype(BF16)
        x_h = x_ref[:, span]
        out = jnp.dot(mixing, x_h, preferred_element_type=F32) + skip[:, h : h + 1] * x_h.astype(F32)
        v = z_ref[:, span].astype(F32)
        gate = v / (1.0 + jnp.exp(-v))
        out_ref[:tokens, span] = out * gate
        out_ref[tokens : 2 * tokens, span] = gate * cols_ref[:, 3 * heads + h : 3 * heads + h + 1]
    out_ref[2 * tokens :] = jnp.broadcast_to(gain_ref[...], (8, x_ref.shape[1]))


def plane_kernel(got_ref, out_ref):
    count, rows, lanes = got_ref.shape
    state_rows = rows - PAD
    total, keep = piece(got_ref, 0, state_rows)
    for i in range(1, count):
        state, factor = piece(got_ref, i, state_rows)
        total = factor * total + state
        keep = keep * factor
    total, keep = (total.astype(BF16), keep_rows(keep))
    for i in range(out_ref.shape[0]):
        out_ref[i, :state_rows, :] = total
        out_ref[i, state_rows:, :] = keep


def entry_kernel(plane, got_ref, planes_ref, out_ref):
    count, rows, lanes = got_ref.shape
    state_rows = rows - PAD
    mine = plane[0]
    entry = jnp.zeros((state_rows, lanes), F32)
    for i in range(planes_ref.shape[0] - 1):
        state, factor = piece(planes_ref, i, state_rows)
        entry = jnp.where(i < mine, factor * entry + state, entry)
    out_ref[0] = entry.astype(BF16)
    for i in range(count - 1):
        state, factor = piece(got_ref, i, state_rows)
        entry = factor * entry + state
        out_ref[i + 1] = entry.astype(BF16)


def bring_kernel(*refs):
    count = len(refs) // 2 - 1
    for copy in fetch(refs[1 : count + 1], refs[count + 1 : -1], refs[-1]):
        copy.wait()


def put_squares(ref, squares):
    high = squares.astype(BF16).astype(F32)
    middle = (squares - high).astype(BF16).astype(F32)
    low = squares - high - middle
    first = jnp.concatenate([high, middle], axis=1)
    second = jnp.concatenate([low, jnp.zeros_like(low)], axis=1)
    row = lax.broadcasted_iota(jnp.int32, (PAD, ref.shape[1]), 0)
    rows = jnp.where(row == 0, first, jnp.where(row == 1, second, 0.0))
    ref[ref.shape[0] - PAD :, :] = rows.astype(BF16)


def get_squares(ref):
    rows = jnp.sum(ref[ref.shape[0] - PAD :, :].astype(F32), axis=0, keepdims=True)
    half = ref.shape[1] // 2
    return rows[:, :half] + rows[:, half:]


def columns(w_hbm, me, away, features):
    place = (me + away + N_PART) % N_PART
    return w_hbm.at[:, pl.ds(pl.multiple_of(place * features, features), features)]


def gate_kernel(me, way, entry_ref, c_ref, gates_ref, w_hbm, *refs):
    gated_ref, far_ref, next_ref, w_ref, sems = refs
    heads, width, lanes = entry_ref.shape
    tokens = c_ref.shape[0]
    features = w_ref.shape[1]
    wanted = [columns(w_hbm, me[0], away, features) for away in (N_PART // 2, (N_PART // 2 - 1) * way[0])]
    copies = fetch(wanted, [w_ref, next_ref], sems)
    entries = entry_ref[...].reshape(heads * width, lanes)
    carried = lax.dot_general(c_ref[...], entries, (((1,), (1,)), ((), ())), preferred_element_type=F32)
    gated = gates_ref[:tokens] + gates_ref[tokens : 2 * tokens] * carried
    scaled = (gated * gates_ref[2 * tokens : 2 * tokens + 1]).astype(BF16)
    gated_ref[:tokens] = scaled
    squares = jnp.sum(gated * gated, axis=1, keepdims=True)
    squares = jnp.broadcast_to(squares, (tokens, 128)).T[:1]
    put_squares(gated_ref, squares)
    put_squares(far_ref, squares)
    copies[0].wait()
    far_ref[:tokens] = jnp.dot(scaled, w_ref[...], preferred_element_type=F32).astype(BF16)
    copies[1].wait()


def begin_kernel(own_ref, other_ref, w_ref, out_ref):
    tokens = out_ref.shape[1]
    for j, ref in enumerate((own_ref, other_ref)):
        out_ref[j] = jnp.dot(ref[:tokens], w_ref[...], preferred_element_type=F32).astype(BF16)


def chunks_kernel(me, way, own_ref, other_ref, w_hbm, out_ref, base_ref, w_ref, sems):
    steps, _, tokens, features = out_ref.shape
    order = [*range(steps, 0, -1), 0]
    copies = fetch([columns(w_hbm, me[0], a * way[0], features) for a in order], [w_ref.at[a] for a in order], sems)
    for a, copy in zip(order, copies):
        copy.wait()
        if a == 0:
            base_ref[...] = jnp.dot(own_ref[:tokens], w_ref[a], preferred_element_type=F32).astype(BF16)
        else:
            for j, ref in enumerate((own_ref, other_ref)):
                out_ref[a - 1, j] = jnp.dot(ref[:tokens], w_ref[a], preferred_element_type=F32).astype(BF16)


def join_kernel(place, chunk_ref, gated_ref, *refs):
    got_refs, out_ref = refs[:-1], refs[-1]
    tokens = gated_ref.shape[0] - PAD
    squares = get_squares(gated_ref)
    total = chunk_ref[place].astype(F32)
    for ref in got_refs:
        squares = squares + get_squares(ref)
        total = total + ref[:tokens].astype(F32)
    out_ref[:tokens] = total.astype(BF16)
    put_squares(out_ref, squares)


def sum_kernel(base_ref, own_ref, got_ref, total_ref, square_ref):
    tokens = base_ref.shape[0]
    square_ref[...] = get_squares(own_ref) + get_squares(got_ref)
    total_ref[...] = base_ref[...].astype(F32) + got_ref[:tokens].astype(F32)


def end_kernel(inner, total_ref, square_ref, got_ref, out_ref):
    tokens, features = out_ref.shape
    squares = square_ref[...] + get_squares(got_ref)
    factor = lax.rsqrt(squares * (1.0 / inner) + 1e-05)
    factor = jnp.broadcast_to(factor, (128, tokens)).T
    for i in range(features // 128):
        span = slice(i * 128, (i + 1) * 128)
        total = total_ref[:, span] + got_ref[:tokens, span].astype(F32)
        out_ref[:, span] = (total * factor).astype(BF16)


def call(kernel, ins, outs, args, scratch=(), flops=0, moved=0, limit=24):
    return pl.pallas_call(
        kernel,
        in_specs=ins,
        out_specs=[VMEM] * len(outs),
        out_shape=[jax.ShapeDtypeStruct(*o) for o in outs],
        scratch_shapes=[pltpu.VMEM(a.shape, a.dtype) for a in scratch] + [pltpu.SemaphoreType.DMA((8,))] * (HBM in ins),
        cost_estimate=pl.CostEstimate(flops=flops, bytes_accessed=moved, transcendentals=0),
        compiler_params=pltpu.CompilerParams(vmem_limit_bytes=limit * 2**20),
    )(*args)


def body(
    input_x, input_z, input_b, input_c, step_raw, doc_starts, log_rate, step_bias, skip_gain, norm_gain, out_weight
):
    tokens, channels = input_x.shape
    heads = log_rate.shape[0]
    width = channels // heads
    state_width = input_b.shape[1]
    devices = lax.axis_size("seq")
    planes = devices // N_ROW
    in_plane = [[p * N_ROW + i for i in range(N_ROW)] for p in range(planes)]
    across = [[p * N_ROW + i for p in range(planes)] for i in range(N_ROW)]
    sent = (width + PAD, state_width)

    local = (
        log_rate.reshape(1, heads),
        step_bias.reshape(1, heads),
        step_raw.T,
        doc_starts.reshape(1, tokens),
        input_b,
        input_x,
    )
    pieces, rows = call(
        state_kernel,
        [HBM] * 6,
        [((heads, *sent), BF16), ((4 * heads, tokens), F32)],
        local,
        scratch=local,
        limit=60,
        flops=2 * tokens * channels * state_width,
        moved=2 * tokens * channels,
    )
    got = lax.all_to_all(pieces, "seq", 0, 0, axis_index_groups=in_plane)
    skip = skip_gain.reshape(1, heads)
    gain = norm_gain.reshape(1, channels)
    (totals,) = call(plane_kernel, [VMEM], [((planes, *sent), BF16)], (got,), moved=2**19)
    near = (input_c, input_b, rows, skip, input_x, input_z, gain)
    (gates,) = call(
        intra_kernel,
        [ANY] + [HBM] * 7,
        [((2 * tokens + 8, channels), F32)],
        (totals, *near),
        scratch=(*near, jax.ShapeDtypeStruct((tokens, 128), F32)),
        limit=60,
        flops=2 * tokens * tokens * channels,
        moved=8 * 2**20,
    )
    got_planes = lax.all_to_all(totals, "seq", 0, 0, axis_index_groups=across)
    got_planes, gates = lax.optimization_barrier((got_planes, gates))
    plane = lax.div(lax.axis_index("seq"), N_ROW).reshape(1)
    (entries,) = call(
        entry_kernel, [SMEM, VMEM, VMEM], [((N_ROW, width, state_width), BF16)], (plane, got, got_planes), moved=2**19
    )
    needed = (input_c, gates)
    needed = call(
        bring_kernel,
        [ANY] + [HBM] * len(needed),
        [(a.shape, a.dtype) for a in needed],
        (entries, *needed),
        moved=2**21,
        limit=48,
    )
    entries = lax.all_to_all(entries, "seq", 0, 0, axis_index_groups=in_plane)
    me = lax.axis_index("head").reshape(1)
    features = out_weight.shape[1] // N_PART
    slab = ((tokens + PAD, features), BF16)
    way = (1 - 2 * lax.rem(lax.axis_index("seq"), 2)).reshape(1)

    def send(array, steps, swap):
        pairs = []
        for seq in range(devices):
            for head in range(N_PART):
                there = (head + steps * (1 - 2 * (seq % 2))) % N_PART
                pairs.append((seq * N_PART + head, (seq ^ swap) * N_PART + there))
        return lax.ppermute(array, ("seq", "head"), pairs)

    gated, far, w_next = call(
        gate_kernel,
        [SMEM] * 2 + [VMEM] * 3 + [HBM],
        [slab, slab, ((channels, features), BF16)],
        (me, way, entries, *needed, out_weight),
        scratch=[jax.ShapeDtypeStruct((channels, features), BF16)],
        flops=2 * tokens * channels * features,
        moved=2**21,
        limit=50,
    )
    other = send(gated, 0, 1)
    own_got = send(far, 1, 0)
    (begin,) = call(
        begin_kernel,
        [VMEM] * 3,
        [((2, tokens, features), BF16)],
        (gated, other, w_next),
        flops=4 * tokens * channels * features,
        moved=2**22,
    )

    def join(place, chunk, mine, *got):
        kernel = functools.partial(join_kernel, place)
        return call(kernel, [VMEM] * (2 + len(got)), [slab], (chunk, mine, *got), moved=2**19)[0]

    other_sent = join(1, begin, other)
    other_got = send(other_sent, 1, 0)
    own_sent = join(0, begin, gated, own_got)
    own_got = send(own_sent, 1, 0)
    steps = N_PART // 2 - 2
    gated_then, _ = lax.optimization_barrier((gated, own_sent))
    chunks, base = call(
        chunks_kernel,
        [SMEM, SMEM, VMEM, VMEM, HBM],
        [((steps, 2, tokens, features), BF16), ((tokens, features), BF16)],
        (me, way, gated_then, other, out_weight),
        scratch=[jax.ShapeDtypeStruct((steps + 1, channels, features), BF16)],
        flops=10 * tokens * channels * features,
        moved=2**21,
        limit=50,
    )
    for away in range(steps, 0, -1):
        other_got = send(join((away - 1, 1), chunks, other, other_got), 1, int(away == 1))
        own_got = send(join((away - 1, 0), chunks, gated, own_got), 1, 0)
    total, squares = call(
        sum_kernel, [VMEM] * 3, [((tokens, features), F32), ((1, tokens), F32)], (base, gated, other_got), moved=2**20
    )
    (out,) = call(
        functools.partial(end_kernel, channels * N_PART),
        [VMEM] * 3,
        [((tokens, features), BF16)],
        (total, squares, own_got),
        moved=2**20,
    )
    return out


def solution(mesh):
    in_specs = (
        P("seq", "head"),
        P("seq", "head"),
        P("seq", None),
        P("seq", None),
        P("seq", "head"),
        P("seq"),
        P("head"),
        P("head"),
        P("head"),
        P("head"),
        P("head", None),
    )
    out_specs = P("seq", "head")
    return jax.shard_map(body, mesh=mesh, in_specs=in_specs, out_specs=out_specs, check_vma=False)
```

```python
import functools

import jax
import jax.numpy as jnp
from jax import lax
from jax.experimental import pallas as pl
from jax.experimental.pallas import tpu as pltpu
from jax.sharding import PartitionSpec as P

SPAN = 256
N_ROW = 8
N_PART = 8
PAD = 16
F32, BF16 = (jnp.float32, jnp.bfloat16)
VMEM = pl.BlockSpec(memory_space=pltpu.VMEM)
SMEM = pl.BlockSpec(memory_space=pltpu.SMEM)
HBM = pl.BlockSpec(memory_space=pltpu.HBM)
ANY = pl.BlockSpec(memory_space=pl.ANY)


def column_of(row, shape):
    count = shape[0]
    spread = jnp.broadcast_to(row, (count, count))
    same = lax.broadcasted_iota(jnp.int32, spread.shape, 0) == lax.broadcasted_iota(jnp.int32, spread.shape, 1)
    return jnp.broadcast_to(jnp.sum(jnp.where(same, spread, 0.0), axis=1, keepdims=True), shape)


def fetch(sources, targets, sems):
    copies = [pltpu.make_async_copy(s, t, sems.at[i]) for i, (s, t) in enumerate(zip(sources, targets))]
    for copy in copies:
        copy.start()
    return copies


def parts_of(rows):
    high = rows.astype(BF16).astype(F32)
    middle = (rows - high).astype(BF16).astype(F32)
    return [high, middle, rows - high - middle]


def keep_rows(keep):
    high = keep.astype(BF16).astype(F32)
    middle = (keep - high).astype(BF16).astype(F32)
    low = keep - high - middle
    rows = lax.broadcasted_iota(jnp.int32, (PAD, keep.shape[1]), 0)
    out = jnp.where(rows == 0, high, jnp.where(rows == 1, middle, jnp.where(rows == 2, low, 0.0)))
    return out.astype(BF16)


def piece(ref, index, state_rows):
    state = ref[index, :state_rows, :].astype(F32)
    keep = jnp.sum(ref[index, state_rows:, :].astype(F32), axis=0, keepdims=True)
    return state, keep


def state_kernel(*refs):
    (log_rate, bias, raw_ref, flag_ref, b_ref, x_ref) = refs[8:14]
    out_ref, rows_ref = refs[6:8]
    copies = fetch(refs[:6], refs[8:14], refs[14])
    for copy in copies[:4]:
        copy.wait()
    heads, tokens = raw_ref.shape
    channels = x_ref.shape[1]
    width = channels // heads
    raw = raw_ref[...]
    dt = jax.nn.softplus(raw + column_of(bias[...], raw.shape))
    rate = -jnp.exp(column_of(log_rate[...], raw.shape))
    flags = jnp.broadcast_to(flag_ref[...].astype(F32), raw.shape)
    steps = jnp.concatenate([*parts_of(rate * dt), flags], axis=0).astype(BF16)
    square = (tokens, tokens)
    upto = lax.broadcasted_iota(jnp.int32, square, 0) <= lax.broadcasted_iota(jnp.int32, square, 1)
    sums = jnp.dot(steps, jnp.where(upto, 1.0, 0.0).astype(BF16), preferred_element_type=F32)
    running = sums[:heads] + sums[heads : 2 * heads] + sums[2 * heads : 3 * heads]
    resets = sums[3 * heads :]
    run_last = jnp.broadcast_to(running[:, tokens - 1 :], raw.shape)
    reset_last = jnp.broadcast_to(resets[:, tokens - 1 :], raw.shape)
    weights = jnp.where(resets == reset_last, jnp.exp(run_last - running), 0.0) * dt
    opening = jnp.where(resets == 0.0, jnp.exp(running), 0.0)
    rows_ref[...] = jnp.concatenate([running, dt, resets, opening], axis=0)
    through = jnp.where(reset_last == 0.0, jnp.exp(run_last), 0.0)
    shape = (4 * heads, channels)
    row, first = lax.broadcasted_iota(jnp.int32, shape, 0), lax.broadcasted_iota(jnp.int32, shape, 1)
    for i in range(3):
        row = jnp.where(row >= heads, row - heads, row)
    mine = (first >= row * width) & (first < (row + 1) * width)
    spread = lax.dot_general(
        jnp.concatenate([*parts_of(weights), jnp.zeros_like(weights)], axis=0).astype(BF16),
        jnp.where(mine, 1.0, 0.0).astype(BF16),
        (((0,), (0,)), ((), ())),
        preferred_element_type=F32,
    )
    for copy in copies[4:]:
        copy.wait()
    scaled = (spread * x_ref[...].astype(F32)).astype(BF16)
    states = lax.dot_general(scaled, b_ref[...], (((0,), (0,)), ((), ())), preferred_element_type=F32)
    for h in range(heads):
        out_ref[h, :width, :] = states[h * width : (h + 1) * width].astype(BF16)
        out_ref[h, width:, :] = keep_rows(through[h : h + 1, :128])


def intra_kernel(*refs):
    out_ref = refs[8]
    c_ref, b_ref, rows_ref, skip_ref, x_ref, z_ref, gain_ref, cols_ref = refs[9:17]
    for copy in fetch(refs[1:8], refs[9:16], refs[17]):
        copy.wait()
    rows = rows_ref[...]
    cols_ref[...] = jnp.concatenate([rows, jnp.zeros((128 - rows.shape[0], rows.shape[1]), F32)], axis=0).T
    tokens = x_ref.shape[0]
    heads = skip_ref.shape[1]
    width = x_ref.shape[1] // heads
    skip = skip_ref[...]
    scores = lax.dot_general(c_ref[...], b_ref[...], (((1,), (1,)), ((), ())), preferred_element_type=F32)
    reset_row = rows_ref[2 * heads : 2 * heads + 1, :]
    reset_col = cols_ref[:, 2 * heads : 2 * heads + 1]
    later = lax.broadcasted_iota(jnp.int32, scores.shape, 0)
    earlier = lax.broadcasted_iota(jnp.int32, scores.shape, 1)
    allowed = (later >= earlier) & (reset_col == reset_row)
    scores = jnp.where(allowed, scores, 0.0)
    for h in range(heads):
        span = slice(h * width, (h + 1) * width)
        spread = cols_ref[:, h : h + 1] - rows_ref[h : h + 1, :]
        decays = jnp.exp(jnp.where(allowed, spread, 0.0))
        mixing = (scores * decays * rows_ref[heads + h : heads + h + 1, :]).astype(BF16)
        x_h = x_ref[:, span]
        out = jnp.dot(mixing, x_h, preferred_element_type=F32) + skip[:, h : h + 1] * x_h.astype(F32)
        v = z_ref[:, span].astype(F32)
        gate = v / (1.0 + jnp.exp(-v))
        out_ref[:tokens, span] = out * gate
        out_ref[tokens : 2 * tokens, span] = gate * cols_ref[:, 3 * heads + h : 3 * heads + h + 1]
    out_ref[2 * tokens :] = jnp.broadcast_to(gain_ref[...], (8, x_ref.shape[1]))


def plane_kernel(got_ref, out_ref):
    count, rows, lanes = got_ref.shape
    state_rows = rows - PAD
    total, keep = piece(got_ref, 0, state_rows)
    for i in range(1, count):
        state, factor = piece(got_ref, i, state_rows)
        total = factor * total + state
        keep = keep * factor
    total, keep = (total.astype(BF16), keep_rows(keep))
    for i in range(out_ref.shape[0]):
        out_ref[i, :state_rows, :] = total
        out_ref[i, state_rows:, :] = keep


def entry_kernel(plane, got_ref, planes_ref, out_ref):
    count, rows, lanes = got_ref.shape
    state_rows = rows - PAD
    mine = plane[0]
    entry = jnp.zeros((state_rows, lanes), F32)
    for i in range(planes_ref.shape[0] - 1):
        state, factor = piece(planes_ref, i, state_rows)
        entry = jnp.where(i < mine, factor * entry + state, entry)
    out_ref[0] = entry.astype(BF16)
    for i in range(count - 1):
        state, factor = piece(got_ref, i, state_rows)
        entry = factor * entry + state
        out_ref[i + 1] = entry.astype(BF16)


def bring_kernel(me, way, after_ref, c_hbm, gates_hbm, w_hbm, c_ref, gates_ref, w_ref, sems):
    count, _, features = w_ref.shape
    sources = [c_hbm, gates_hbm] + [columns(w_hbm, me[0], a * way[0], features) for a in range(count)]
    for copy in fetch(sources, [c_ref, gates_ref] + [w_ref.at[a] for a in range(count)], sems):
        copy.wait()


def put_squares(ref, squares):
    high = squares.astype(BF16).astype(F32)
    middle = (squares - high).astype(BF16).astype(F32)
    low = squares - high - middle
    first = jnp.concatenate([high, middle], axis=1)
    second = jnp.concatenate([low, jnp.zeros_like(low)], axis=1)
    row = lax.broadcasted_iota(jnp.int32, (PAD, ref.shape[1]), 0)
    rows = jnp.where(row == 0, first, jnp.where(row == 1, second, 0.0))
    ref[ref.shape[0] - PAD :, :] = rows.astype(BF16)


def get_squares(ref):
    rows = jnp.sum(ref[ref.shape[0] - PAD :, :].astype(F32), axis=0, keepdims=True)
    half = ref.shape[1] // 2
    return rows[:, :half] + rows[:, half:]


def columns(w_hbm, me, away, features):
    place = (me + away + N_PART) % N_PART
    return w_hbm.at[:, pl.ds(pl.multiple_of(place * features, features), features)]


def gate_kernel(me, way, entry_ref, c_ref, gates_ref, w_hbm, *refs):
    gated_ref, far_ref, next_ref, w_ref, sems = refs
    heads, width, lanes = entry_ref.shape
    tokens = c_ref.shape[0]
    features = w_ref.shape[1]
    wanted = [columns(w_hbm, me[0], away, features) for away in (N_PART // 2, (N_PART // 2 - 1) * way[0])]
    copies = fetch(wanted, [w_ref, next_ref], sems)
    entries = entry_ref[...].reshape(heads * width, lanes)
    carried = lax.dot_general(c_ref[...], entries, (((1,), (1,)), ((), ())), preferred_element_type=F32)
    gated = gates_ref[:tokens] + gates_ref[tokens : 2 * tokens] * carried
    scaled = (gated * gates_ref[2 * tokens : 2 * tokens + 1]).astype(BF16)
    gated_ref[:tokens] = scaled
    squares = jnp.sum(gated * gated, axis=1, keepdims=True)
    squares = jnp.broadcast_to(squares, (tokens, 128)).T[:1]
    put_squares(gated_ref, squares)
    put_squares(far_ref, squares)
    copies[0].wait()
    far_ref[:tokens] = jnp.dot(scaled, w_ref[...], preferred_element_type=F32).astype(BF16)
    copies[1].wait()


def begin_kernel(own_ref, other_ref, w_ref, out_ref):
    tokens = out_ref.shape[1]
    for j, ref in enumerate((own_ref, other_ref)):
        out_ref[j] = jnp.dot(ref[:tokens], w_ref[...], preferred_element_type=F32).astype(BF16)


def chunks_kernel(own_ref, other_ref, w_ref, out_ref, base_ref):
    steps, _, tokens, features = out_ref.shape
    for a in range(steps, 0, -1):
        for j, ref in enumerate((own_ref, other_ref)):
            out_ref[a - 1, j] = jnp.dot(ref[:tokens], w_ref[a], preferred_element_type=F32).astype(BF16)
    base_ref[...] = jnp.dot(own_ref[:tokens], w_ref[0], preferred_element_type=F32).astype(BF16)


def join_kernel(place, chunk_ref, gated_ref, *refs):
    got_refs, out_ref = refs[:-1], refs[-1]
    tokens = gated_ref.shape[0] - PAD
    squares = get_squares(gated_ref)
    total = chunk_ref[place].astype(F32)
    for ref in got_refs:
        squares = squares + get_squares(ref)
        total = total + ref[:tokens].astype(F32)
    out_ref[:tokens] = total.astype(BF16)
    put_squares(out_ref, squares)


def sum_kernel(base_ref, own_ref, got_ref, total_ref, square_ref):
    tokens = base_ref.shape[0]
    square_ref[...] = get_squares(own_ref) + get_squares(got_ref)
    total_ref[...] = base_ref[...].astype(F32) + got_ref[:tokens].astype(F32)


def end_kernel(inner, total_ref, square_ref, got_ref, out_ref):
    tokens, features = out_ref.shape
    squares = square_ref[...] + get_squares(got_ref)
    factor = lax.rsqrt(squares * (1.0 / inner) + 1e-05)
    factor = jnp.broadcast_to(factor, (128, tokens)).T
    for i in range(features // 128):
        span = slice(i * 128, (i + 1) * 128)
        total = total_ref[:, span] + got_ref[:tokens, span].astype(F32)
        out_ref[:, span] = (total * factor).astype(BF16)


def call(kernel, ins, outs, args, scratch=(), flops=0, moved=0, limit=24):
    return pl.pallas_call(
        kernel,
        in_specs=ins,
        out_specs=[VMEM] * len(outs),
        out_shape=[jax.ShapeDtypeStruct(*o) for o in outs],
        scratch_shapes=[pltpu.VMEM(a.shape, a.dtype) for a in scratch] + [pltpu.SemaphoreType.DMA((8,))] * (HBM in ins),
        cost_estimate=pl.CostEstimate(flops=flops, bytes_accessed=moved, transcendentals=0),
        compiler_params=pltpu.CompilerParams(vmem_limit_bytes=limit * 2**20),
    )(*args)


def body(
    input_x, input_z, input_b, input_c, step_raw, doc_starts, log_rate, step_bias, skip_gain, norm_gain, out_weight
):
    tokens, channels = input_x.shape
    heads = log_rate.shape[0]
    width = channels // heads
    state_width = input_b.shape[1]
    devices = lax.axis_size("seq")
    planes = devices // N_ROW
    in_plane = [[p * N_ROW + i for i in range(N_ROW)] for p in range(planes)]
    across = [[p * N_ROW + i for p in range(planes)] for i in range(N_ROW)]
    sent = (width + PAD, state_width)

    local = (
        log_rate.reshape(1, heads),
        step_bias.reshape(1, heads),
        step_raw.T,
        doc_starts.reshape(1, tokens),
        input_b,
        input_x,
    )
    pieces, rows = call(
        state_kernel,
        [HBM] * 6,
        [((heads, *sent), BF16), ((4 * heads, tokens), F32)],
        local,
        scratch=local,
        limit=60,
        flops=2 * tokens * channels * state_width,
        moved=2 * tokens * channels,
    )
    got = lax.all_to_all(pieces, "seq", 0, 0, axis_index_groups=in_plane)
    skip = skip_gain.reshape(1, heads)
    gain = norm_gain.reshape(1, channels)
    (totals,) = call(plane_kernel, [VMEM], [((planes, *sent), BF16)], (got,), moved=2**19)
    near = (input_c, input_b, rows, skip, input_x, input_z, gain)
    (gates,) = call(
        intra_kernel,
        [ANY] + [HBM] * 7,
        [((2 * tokens + 8, channels), F32)],
        (totals, *near),
        scratch=(*near, jax.ShapeDtypeStruct((tokens, 128), F32)),
        limit=60,
        flops=2 * tokens * tokens * channels,
        moved=8 * 2**20,
    )
    got_planes = lax.all_to_all(totals, "seq", 0, 0, axis_index_groups=across)
    got_planes, gates = lax.optimization_barrier((got_planes, gates))
    plane = lax.div(lax.axis_index("seq"), N_ROW).reshape(1)
    (entries,) = call(
        entry_kernel, [SMEM, VMEM, VMEM], [((N_ROW, width, state_width), BF16)], (plane, got, got_planes), moved=2**19
    )
    me = lax.axis_index("head").reshape(1)
    way = (1 - 2 * lax.rem(lax.axis_index("seq"), 2)).reshape(1)
    features = out_weight.shape[1] // N_PART
    steps = N_PART // 2 - 2
    *needed, w_near = call(
        bring_kernel,
        [SMEM] * 2 + [ANY] + [HBM] * 3,
        [(a.shape, a.dtype) for a in (input_c, gates)] + [((steps + 1, channels, features), BF16)],
        (me, way, entries, input_c, gates, out_weight),
        moved=2**21,
        limit=48,
    )
    entries = lax.all_to_all(entries, "seq", 0, 0, axis_index_groups=in_plane)
    slab = ((tokens + PAD, features), BF16)

    def send(array, steps, swap):
        pairs = []
        for seq in range(devices):
            for head in range(N_PART):
                there = (head + steps * (1 - 2 * (seq % 2))) % N_PART
                pairs.append((seq * N_PART + head, (seq ^ swap) * N_PART + there))
        return lax.ppermute(array, ("seq", "head"), pairs)

    gated, far, w_next = call(
        gate_kernel,
        [SMEM] * 2 + [VMEM] * 3 + [HBM],
        [slab, slab, ((channels, features), BF16)],
        (me, way, entries, *needed, out_weight),
        scratch=[jax.ShapeDtypeStruct((channels, features), BF16)],
        flops=2 * tokens * channels * features,
        moved=2**21,
        limit=50,
    )
    other = send(gated, 0, 1)
    own_got = send(far, 1, 0)
    (begin,) = call(
        begin_kernel,
        [VMEM] * 3,
        [((2, tokens, features), BF16)],
        (gated, other, w_next),
        flops=4 * tokens * channels * features,
        moved=2**22,
    )

    def join(place, chunk, mine, *got):
        kernel = functools.partial(join_kernel, place)
        return call(kernel, [VMEM] * (2 + len(got)), [slab], (chunk, mine, *got), moved=2**19)[0]

    other_sent = join(1, begin, other)
    other_got = send(other_sent, 1, 0)
    own_sent = join(0, begin, gated, own_got)
    own_got = send(own_sent, 1, 0)
    gated_then, _ = lax.optimization_barrier((gated, own_sent))
    chunks, base = call(
        chunks_kernel,
        [VMEM] * 3,
        [((steps, 2, tokens, features), BF16), ((tokens, features), BF16)],
        (gated_then, other, w_near),
        flops=10 * tokens * channels * features,
        moved=2**21,
    )
    for away in range(steps, 0, -1):
        other_got = send(join((away - 1, 1), chunks, other, other_got), 1, int(away == 1))
        own_got = send(join((away - 1, 0), chunks, gated, own_got), 1, 0)
    total, squares = call(
        sum_kernel, [VMEM] * 3, [((tokens, features), F32), ((1, tokens), F32)], (base, gated, other_got), moved=2**20
    )
    (out,) = call(
        functools.partial(end_kernel, channels * N_PART),
        [VMEM] * 3,
        [((tokens, features), BF16)],
        (total, squares, own_got),
        moved=2**20,
    )
    return out


def solution(mesh):
    in_specs = (
        P("seq", "head"),
        P("seq", "head"),
        P("seq", None),
        P("seq", None),
        P("seq", "head"),
        P("seq"),
        P("head"),
        P("head"),
        P("head"),
        P("head"),
        P("head", None),
    )
    out_specs = P("seq", "head")
    return jax.shard_map(body, mesh=mesh, in_specs=in_specs, out_specs=out_specs, check_vma=False)
```
